256 devices in a mesh: patch: 128 (over y, z, x_hi, core), lat: 2 (over x_lo).
Axes of the slice: x: 4 (x_hi: 2, x_lo: 2; x = x_hi * 2 + x_lo), y: 4, z: 8, core: 2. Of those that a mesh axis runs over, the one named last changes fastest.
Arguments:
- node_latents: bfloat16 [24576, 512], P('patch', 'lat'), may hold values from -6 to 6
- edge_latents: bfloat16 [196608, 512], P('patch', 'lat'), may hold values from -6 to 6
- senders: int32 [1536, 128], P('patch'), may hold values from 0 to 24575, as said below
- receivers: int32 [1536, 128], P('patch'), may hold values from 0 to 24575, as said below
- long_count: int32 [128], P('patch'), may hold values from 1 to 384, 24576 in all
- edge_inner: bfloat16 [3, 512, 512], P(None, 'lat'), may hold values from -0.15625 to 0.15625
- edge_outer: bfloat16 [512, 512], P('lat'), may hold values from -0.25 to 0.25
- node_inner: bfloat16 [2, 512, 512], P(None, 'lat'), may hold values from -0.1875 to 0.1875
- node_outer: bfloat16 [512, 512], P('lat'), may hold values from -0.25 to 0.25
- node_cotangent: bfloat16 [24576, 512], P('patch', 'lat'), may hold values from -3 to 3
- edge_cotangent: bfloat16 [196608, 512], P('patch', 'lat'), may hold values from -3 to 3
Outputs:
- edge_output: bfloat16 [196608, 512], P('patch', 'lat')
- node_output: bfloat16 [24576, 512], P('patch', 'lat')
- edge_grads: bfloat16 [196608, 512], P('patch', 'lat')
- node_grads: bfloat16 [24576, 512], P('patch', 'lat')
- edgeinner_grad: float32 [3, 512, 512], P(None, 'lat')
- edgeouter_grad: float32 [512, 512], P('lat')
- nodeinner_grad: float32 [2, 512, 512], P(None, 'lat')
- nodeouter_grad: float32 [512, 512], P('lat')
The draws below stay inside these ranges and needn't reach their ends.
Inputs may be any that keep to these rules, and one draw needn't show every extreme that they name: `senders`: patch p holds nodes p*192 to (p+1)*192 - 1. The sender of each of a patch's first 1152 slots is 1 to 32 nodes away from its receiver, counted cyclically over all 24576 nodes; the sender of each long slot is a coarse node, a node whose index within its patch is below 8. Every slot's receiver is a node of the slot's own patch; long slots' receivers are coarse nodes of that patch. The first long_count[p] of patch p's 384 long slots are live.
All inputs are finite; a program needn't handle non-finite values. No bound on the sum of `long_count` on one device may be relied on, other than what follows from the above.
Results may differ from the reference program's by a relative error of at most 0.014.
Values may be sent and summed in bfloat16 or wider, within the bound.
No kernel may reach another device: no remote copies, remote signals or barrier semaphores. Data moves between devices by JAX's collectives and lax.ppermute only.
A program may use at most 128 MiB of HBM per device.

```python
import math
import jax
import jax.numpy as jnp
import numpy as np
from jax import lax

D = 512
NODE_DEV = 192
HALO = 32
COARSE_DEV = 8
FINE_DEV = 1152
LONG_DEV = 384
EDGE_DEV = 1536
PATCHES = 128
NODES = 24576
EDGES = 196608


def edge_ends(key):
    patch_count = NODES // NODE_DEV
    first_node = (jnp.arange(patch_count, dtype=jnp.int32) * NODE_DEV)[:, None]
    own_patch = jnp.arange(patch_count, dtype=jnp.int32)[:, None]
    keys = jax.random.split(key, 7)
    near_recv = first_node + jax.random.randint(keys[0], (patch_count, FINE_DEV), 0, NODE_DEV, dtype=jnp.int32)
    distance = jax.random.randint(keys[1], (patch_count, FINE_DEV), 1, HALO + 1, dtype=jnp.int32)
    direction = 2 * jax.random.randint(keys[2], (patch_count, FINE_DEV), 0, 2, dtype=jnp.int32) - 1
    near_send = (near_recv + direction * distance) % NODES
    far_recv = first_node + jax.random.randint(keys[3], (patch_count, LONG_DEV), 0, COARSE_DEV, dtype=jnp.int32)
    anywhere = jax.random.randint(keys[4], (patch_count, LONG_DEV), 0, patch_count, dtype=jnp.int32)
    opposite = (own_patch + patch_count // 2) % patch_count
    pick = jax.random.randint(keys[6], (patch_count, LONG_DEV), 0, 2, dtype=jnp.int32)
    source = pick * opposite + (1 - pick) * anywhere
    far_send = source * NODE_DEV + jax.random.randint(keys[5], (patch_count, LONG_DEV), 0, COARSE_DEV, dtype=jnp.int32)
    sender_ids = jnp.concatenate([near_send, far_send], 1).reshape(EDGES // 128, 128)
    receiver_ids = jnp.concatenate([near_recv, far_recv], 1).reshape(EDGES // 128, 128)
    return (sender_ids, receiver_ids)


def draw_senders(key, part):
    return edge_ends(key)[0]


def draw_receivers(key, part):
    return edge_ends(key)[1]


def block_levels(key, shape, cuts, least, high):
    level, own = 1.0, jax.random.fold_in(key, 6)
    for dim, parts in cuts:
        heights = jnp.exp(jax.random.uniform(jax.random.fold_in(own, dim), (parts,), jnp.float32, least / len(cuts), high / len(cuts)))
        level = level * jnp.repeat(heights, shape[dim] // parts).reshape([-1 if axis == dim else 1 for axis in range(len(shape))])
    return level


def profile(amount, total, most, lean):
    weights = [(1 << 20) // math.isqrt(grade ** lean) + 1 for grade in range(2, amount + 1)]
    spare, counts = total - most - (amount - 1), [1] * (amount - 1)
    while spare > 0:
        movable = [i for i in range(amount - 1) if counts[i] < most]
        mass, left = sum([weights[i] for i in movable]), spare
        for i in movable:
            extra = min(most - counts[i], max(1, left * weights[i] // mass), spare)
            counts[i] = counts[i] + extra
            spare = spare - extra
    return np.array([most] + counts)


def uneven_parts(rng, count, total, bound, skew):
    if count == 2:
        one = jax.random.randint(rng, (), max(1, total - bound), min(bound, total - 1) + 1)
        return jnp.stack([one, total - one])
    lengths = jnp.asarray(profile(count, total, bound, skew), jnp.int32)
    pairs = (count - 1) // 2
    donor, sink = lengths[1:1 + 2 * pairs:2], lengths[2:2 + 2 * pairs:2]
    slack = jnp.minimum(donor - 1, bound - sink)
    passed = jax.random.randint(jax.random.fold_in(rng, 1), (pairs,), 0, 1 << 20) % (slack + 1)
    lengths = lengths.at[1:1 + 2 * pairs:2].set(donor - passed).at[2:2 + 2 * pairs:2].set(sink + passed)
    return lengths[jax.random.permutation(jax.random.fold_in(rng, 2), count)]


def noise(key, dims, scale, limit, cuts=(), kind=jnp.bfloat16):
    loudness = block_levels(key, dims, cuts, -0.22, 0.18) if cuts else 1.0
    drawn = jax.random.normal(key, dims, jnp.float32) * scale * loudness
    return jnp.minimum(jnp.maximum(drawn, -limit), limit).astype(kind)


def setup_inputs(seed: int = 0) -> dict:
    seeds = jax.random.split(jax.random.key(seed), 12)
    return {
        "node_latents": noise(seeds[0], (NODES, D), 1.0, 6.0, ((0, 128), (1, 2))),
        "edge_latents": noise(seeds[1], (EDGES, D), 1.0, 6.0, ((0, 128), (1, 2))),
        "senders": draw_senders(jax.random.fold_in(seeds[11], 71), 0),
        "receivers": draw_receivers(jax.random.fold_in(seeds[11], 71), 0),
        "long_count": uneven_parts(seeds[4], PATCHES, PATCHES * LONG_DEV // 2, LONG_DEV, 2).astype(jnp.int32),
        "edge_inner": noise(seeds[5], (3, D, D), (3 * D) ** -0.5, 0.15625, ((1, 2),)),
        "edge_outer": noise(seeds[6], (D, D), D ** -0.5, 0.25, ((0, 2),)),
        "node_inner": noise(seeds[7], (2, D, D), (2 * D) ** -0.5, 0.1875, ((1, 2),)),
        "node_outer": noise(seeds[8], (D, D), D ** -0.5, 0.25, ((0, 2),)),
        "node_cotangent": noise(seeds[9], (NODES, D), 0.5, 3.0, ((0, 128), (1, 2))),
        "edge_cotangent": noise(seeds[10], (EDGES, D), 0.5, 3.0, ((0, 128), (1, 2))),
    }


EPSILON = 1e-05

def swish_slope(values):
    sigmoid = jax.nn.sigmoid(values)
    return sigmoid * (1.0 + values * (1.0 - sigmoid))

def layer_norm(values):
    centered = values - lax.optimization_barrier(jnp.mean(values, axis=1, keepdims=True))
    inverse = lax.rsqrt(lax.optimization_barrier(jnp.mean(centered * centered, axis=1, keepdims=True)) + EPSILON)
    return (centered * inverse, inverse)

def norm_backward(cotangent, normed, inverse):
    return (cotangent - lax.optimization_barrier(jnp.mean(cotangent, axis=1, keepdims=True)) - normed * lax.optimization_barrier(jnp.mean(cotangent * normed, axis=1, keepdims=True))) * inverse

def product(left, right):
    return jnp.dot(left, right, preferred_element_type=jnp.float32)

def reference(node_latents, edge_latents, senders, receivers, long_count, edge_inner, edge_outer, node_inner, node_outer, node_cotangent, edge_cotangent):
    sender_ids = senders.reshape(EDGES)
    receiver_ids = receivers.reshape(EDGES)
    slot_index = jnp.arange(EDGE_DEV, dtype=jnp.int32)[None, :]
    live_mask = jnp.logical_or(slot_index < FINE_DEV, slot_index - FINE_DEV < long_count[:, None]).astype(jnp.float32).reshape(EDGES, 1)
    sender_rows = node_latents[sender_ids]
    receiver_rows = node_latents[receiver_ids]
    operands = (edge_latents, sender_rows, receiver_rows)
    hidden_pre = product(edge_latents, edge_inner[0]) + product(sender_rows, edge_inner[1]) + product(receiver_rows, edge_inner[2])
    hidden_act = jax.nn.silu(hidden_pre).astype(jnp.bfloat16)
    normed, inverse = layer_norm(product(hidden_act, edge_outer))
    update = live_mask * normed
    edge_output = (edge_latents.astype(jnp.float32) + update).astype(jnp.bfloat16)
    aggregate = jax.ops.segment_sum(update.astype(jnp.bfloat16).astype(jnp.float32), receiver_ids, num_segments=NODES).astype(jnp.bfloat16)
    node_pre = product(node_latents, node_inner[0]) + product(aggregate, node_inner[1])
    node_act = jax.nn.silu(node_pre).astype(jnp.bfloat16)
    node_normed, node_inverse = layer_norm(product(node_act, node_outer))
    node_output = (node_latents.astype(jnp.float32) + node_normed).astype(jnp.bfloat16)
    node_dy = norm_backward(node_cotangent.astype(jnp.float32), node_normed, node_inverse).astype(jnp.bfloat16)
    nodeouter_grad = product(node_act.T, node_dy) / PATCHES
    node_dpre = (product(node_dy, node_outer.T) * swish_slope(node_pre)).astype(jnp.bfloat16)
    nodeinner_grad = jnp.stack([product(node_latents.T, node_dpre), product(aggregate.T, node_dpre)]) / PATCHES
    aggregate_grad = product(node_dpre, node_inner[1].T).astype(jnp.bfloat16)
    node_self = node_cotangent.astype(jnp.float32) + product(node_dpre, node_inner[0].T)
    update_grad = edge_cotangent.astype(jnp.float32) + aggregate_grad[receiver_ids].astype(jnp.float32)
    edge_dy = norm_backward(live_mask * update_grad, normed, inverse).astype(jnp.bfloat16)
    edgeouter_grad = product(hidden_act.T, edge_dy) / PATCHES
    edge_dpre = (product(edge_dy, edge_outer.T) * swish_slope(hidden_pre)).astype(jnp.bfloat16)
    edgeinner_grad = jnp.stack([product(operand.T, edge_dpre) for operand in operands]) / PATCHES
    edge_grads = (edge_cotangent.astype(jnp.float32) + product(edge_dpre, edge_inner[0].T)).astype(jnp.bfloat16)
    sender_grads = product(edge_dpre, edge_inner[1].T).astype(jnp.bfloat16)
    receiver_grads = product(edge_dpre, edge_inner[2].T).astype(jnp.bfloat16)
    node_grads = node_self + jax.ops.segment_sum(sender_grads.astype(jnp.float32), sender_ids, num_segments=NODES)
    node_grads = (node_grads + jax.ops.segment_sum(receiver_grads.astype(jnp.float32), receiver_ids, num_segments=NODES)).astype(jnp.bfloat16)
    return (edge_output, node_output, edge_grads, node_grads, edgeinner_grad, edgeouter_grad, nodeinner_grad, nodeouter_grad)
```

```python
import jax
import jax.numpy as jnp
from jax import lax
from jax.sharding import PartitionSpec as P

HALO = 32
COARSE = 8
FINE = 1152
EPSILON = 1e-05
F32 = jnp.float32
BF16 = jnp.bfloat16


def dot(left, right):
    return jnp.dot(left, right, preferred_element_type=F32)


def contract_rows(left, right):
    return lax.dot_general(left, right, (((0,), (0,)), ((), ())), preferred_element_type=F32)


def contract_cols(left, right):
    return lax.dot_general(left, right, (((1,), (1,)), ((), ())), preferred_element_type=F32)


def swish_slope(values):
    sigmoid = jax.nn.sigmoid(values)
    return sigmoid * (1.0 + values * (1.0 - sigmoid))


def layer_norm(values):
    middle = jnp.mean(values, axis=1, keepdims=True)
    centered = values - middle
    inverse = lax.rsqrt(jnp.mean(centered * centered, axis=1, keepdims=True) + EPSILON)
    return centered * inverse, inverse


def norm_backward(cotangent, normed, inverse):
    mean = jnp.mean(cotangent, axis=1, keepdims=True)
    crossed = jnp.mean(cotangent * normed, axis=1, keepdims=True)
    return (cotangent - mean - normed * crossed) * inverse


def swap_lat(value):
    return lax.ppermute(value, "lat", [(0, 1), (1, 0)])


def swap_core(value):
    count = lax.axis_size("patch")
    return lax.ppermute(value, "patch", [(i, i ^ 1) for i in range(count)])


def shifted(value, steps):
    count = lax.axis_size("patch")
    return lax.ppermute(value, "patch", [(i, (i + steps) % count) for i in range(count)])


def other_neighbour(value):
    count = lax.axis_size("patch")
    pairs = []
    for patch in range(count):
        for lat in range(2):
            across = patch ^ 2
            pairs.append((patch * 2 + lat, across * 2 + (1 - lat)))
    return lax.ppermute(value, ("patch", "lat"), pairs)


def same_core_groups():
    count = lax.axis_size("patch")
    return [list(range(core, count, 2)) for core in range(2)]


def chips_all_to_all(value):
    return lax.all_to_all(value, "patch", 0, 0, tiled=True, axis_index_groups=same_core_groups())


def take(value, start, size, axis):
    return lax.dynamic_slice_in_dim(value, start, size, axis)


def one_hot(index, width):
    return (index[:, None] == jnp.arange(width, dtype=jnp.int32)[None, :]).astype(BF16)


def body(
    node_latents,
    edge_latents,
    senders,
    receivers,
    long_count,
    edge_inner,
    edge_outer,
    node_inner,
    node_outer,
    node_cotangent,
    edge_cotangent,
):
    nodes, half = node_latents.shape
    edges = edge_latents.shape[0]
    fine, longs = FINE // 2, (edges - FINE) // 2
    patches = lax.axis_size("patch")
    chips = patches // 2
    lat = lax.axis_index("lat")
    patch = lax.axis_index("patch")
    core = patch % 2
    first_node = patch * nodes

    def rows_of(value, side):
        return jnp.concatenate(
            [take(value, side * fine, fine, 0), take(value, FINE + side * longs, longs, 0)], 0
        )

    def ordered(mine, other, axis):
        return jnp.where(
            lat == 0,
            jnp.concatenate([mine, other], axis),
            jnp.concatenate([other, mine], axis),
        )

    def own_cols(value):
        return take(value, lat * half, half, 1)

    def other_cols(value):
        return take(value, (1 - lat) * half, half, 1)

    def whole_rows(value):
        return ordered(rows_of(value, lat), swap_lat(rows_of(value, 1 - lat)), 1)

    def back_to_columns(value):
        mine, got = own_cols(value), swap_lat(other_cols(value))
        fine_rows = ordered(mine[:fine], got[:fine], 0)
        long_rows = ordered(mine[fine:], got[fine:], 0)
        return jnp.concatenate([fine_rows, long_rows], 0)

    pair = swap_lat(jnp.concatenate([node_latents, node_cotangent], 0))
    node_x = ordered(node_latents, pair[:nodes], 1)
    node_g = ordered(node_cotangent, pair[nodes:], 1)
    low = shifted(node_x[nodes - HALO :], 1)
    high = shifted(node_x[:HALO], -1)
    extended = jnp.concatenate([low, node_x, high], 0)
    coarse_mine = chips_all_to_all(
        jnp.broadcast_to(node_x[None, :COARSE], (chips, COARSE, 2 * half))
    )
    coarse_other = swap_core(coarse_mine)
    coarse = jnp.where(
        core == 0,
        jnp.stack([coarse_mine, coarse_other], 1),
        jnp.stack([coarse_other, coarse_mine], 1),
    ).reshape(patches * COARSE, 2 * half)

    def whole_weight(weight):
        rows = weight.shape[-2] // 2
        axis = weight.ndim - 2
        got = other_neighbour(take(weight, core * rows, rows, axis))
        again = swap_core(got)
        missing = jnp.where(
            core == 0,
            jnp.concatenate([got, again], axis),
            jnp.concatenate([again, got], axis),
        )
        return ordered(weight, missing, axis)

    edge_in, edge_out = whole_weight(edge_inner), whole_weight(edge_outer)
    node_in, node_out = whole_weight(node_inner), whole_weight(node_outer)

    edge_x = whole_rows(edge_latents)
    edge_g = whole_rows(edge_cotangent)
    sender_ids = rows_of(senders.reshape(edges), lat)
    receiver_ids = rows_of(receivers.reshape(edges), lat) - first_node
    near_index = (sender_ids[:fine] - first_node + HALO) % (nodes * patches)
    far_ids = sender_ids[fine:]
    far_index = far_ids // nodes * COARSE + far_ids % nodes
    near_table = one_hot(near_index, extended.shape[0])
    far_table = one_hot(far_index, coarse.shape[0])
    recv_table = one_hot(receiver_ids, nodes)
    slot_index = jnp.arange(longs, dtype=jnp.int32) + lat * longs
    live_mask = jnp.concatenate(
        [jnp.ones((fine,), F32), (slot_index < long_count[0]).astype(F32)]
    )[:, None]

    sender_rows = jnp.concatenate(
        [dot(near_table, extended), dot(far_table, coarse)], 0
    ).astype(BF16)
    receiver_rows = dot(recv_table, node_x).astype(BF16)
    hidden_pre = (
        dot(edge_x, edge_in[0]) + dot(sender_rows, edge_in[1]) + dot(receiver_rows, edge_in[2])
    )
    hidden_act = jax.nn.silu(hidden_pre).astype(BF16)
    normed, inverse = layer_norm(dot(hidden_act, edge_out))
    update = live_mask * normed
    edge_output = back_to_columns((edge_x.astype(F32) + update).astype(BF16))
    partial = contract_rows(recv_table, update.astype(BF16))
    aggregate = (partial + swap_lat(partial.astype(BF16)).astype(F32)).astype(BF16)

    node_pre = dot(node_x, node_in[0]) + dot(aggregate, node_in[1])
    node_act = jax.nn.silu(node_pre).astype(BF16)
    node_normed, node_inverse = layer_norm(dot(node_act, node_out))
    node_output = (node_latents.astype(F32) + own_cols(node_normed)).astype(BF16)
    node_dy = norm_backward(node_g.astype(F32), node_normed, node_inverse).astype(BF16)
    node_dpre = (contract_cols(node_dy, node_out) * swish_slope(node_pre)).astype(BF16)
    node_grad_parts = jnp.concatenate(
        [
            contract_rows(node_latents, node_dpre),
            contract_rows(own_cols(aggregate), node_dpre),
            contract_rows(own_cols(node_act), node_dy),
        ],
        0,
    ).astype(BF16)
    aggregate_grad = contract_cols(node_dpre, node_in[1]).astype(BF16)
    node_self = node_cotangent.astype(F32) + contract_cols(
        node_dpre, node_inner[0]
    )

    update_grad = edge_g.astype(F32) + dot(recv_table, aggregate_grad)
    edge_dy = norm_backward(live_mask * update_grad, normed, inverse).astype(BF16)
    edge_dpre = (contract_cols(edge_dy, edge_out) * swish_slope(hidden_pre)).astype(BF16)
    edge_grad_parts = jnp.stack(
        [
            contract_rows(edge_x, edge_dpre),
            contract_rows(sender_rows, edge_dpre),
            contract_rows(receiver_rows, edge_dpre),
            contract_rows(hidden_act, edge_dy),
        ]
    ).astype(BF16)
    edge_grads = back_to_columns(
        (edge_g.astype(F32) + contract_cols(edge_dpre, edge_in[0])).astype(BF16)
    )
    sender_grads = contract_cols(edge_dpre, edge_in[1]).astype(BF16)
    receiver_grads = contract_cols(edge_dpre, edge_in[2]).astype(BF16)
    near_grads = contract_rows(near_table, sender_grads[:fine])
    far_grads = contract_rows(far_table, sender_grads[fine:]).astype(BF16)
    recv_grads = contract_rows(recv_table, receiver_grads)
    near_grads = near_grads + jnp.pad(recv_grads, ((HALO, HALO), (0, 0)))

    summed = own_cols(near_grads) + swap_lat(other_cols(near_grads).astype(BF16)).astype(F32)
    to_low = shifted(summed[:HALO].astype(BF16), -1).astype(F32)
    to_high = shifted(summed[HALO + nodes :].astype(BF16), 1).astype(F32)

    lanes = 128
    blocks = 2 * half // 2 // lanes

    def core_cols(value, which):
        return take(value, which * half, half, value.ndim - 1)

    def over_cores_cols(value):
        got = swap_core(core_cols(value, 1 - core))
        return core_cols(value, core).astype(F32) + got.astype(F32)

    edge_parts = over_cores_cols(edge_grad_parts).astype(BF16)
    edge_parts = take(edge_parts, lat * half, half, 1).astype(F32) + swap_lat(
        take(edge_parts, (1 - lat) * half, half, 1)
    ).astype(F32)
    node_parts = over_cores_cols(node_grad_parts)
    weight_parts = jnp.concatenate(
        [edge_parts.reshape(4 * half, half), node_parts], 0
    ).astype(BF16)
    total_rows = weight_parts.shape[0] * blocks
    share = total_rows // chips
    weight_parts = jnp.concatenate(
        [weight_parts[:, i * lanes : (i + 1) * lanes] for i in range(blocks)], 0
    ).reshape(chips, share, lanes)

    far_parts = far_grads.reshape(chips, 2, COARSE, 2 * half)
    far_own = jnp.where(core == 0, far_parts[:, 0], far_parts[:, 1])
    far_sent = jnp.where(core == 0, far_parts[:, 1], far_parts[:, 0])
    far_own = far_own.astype(F32) + swap_core(far_sent).astype(F32)
    far_own = take(far_own, lat * half, half, 2) + swap_lat(
        take(far_own, (1 - lat) * half, half, 2).astype(BF16)
    ).astype(F32)
    far_own = far_own.astype(BF16)
    far_own = jnp.concatenate(
        [far_own[:, :, i * lanes : (i + 1) * lanes] for i in range(blocks)], 1
    )
    arrived = chips_all_to_all(jnp.concatenate([weight_parts, far_own], 1))
    total = jnp.sum(arrived.astype(F32), 0)
    coarse_share = jnp.concatenate(
        [total[share + i * COARSE : share + (i + 1) * COARSE] for i in range(blocks)], 1
    )
    weight_share = (total[:share] / patches).astype(BF16)
    mine = chips_all_to_all(jnp.broadcast_to(weight_share[None], (chips, share, lanes)))
    mine = mine.reshape(blocks, total_rows // blocks, lanes)
    mine = jnp.concatenate([mine[i] for i in range(blocks)], 1)
    other = swap_core(mine)
    weights = jnp.where(
        core == 0, jnp.concatenate([mine, other], 1), jnp.concatenate([other, mine], 1)
    ).astype(F32)

    own_grads = node_self + summed[HALO : HALO + nodes]
    own_grads = own_grads.at[nodes - HALO :].add(to_low)
    own_grads = own_grads.at[:HALO].add(to_high)
    own_grads = own_grads.at[:COARSE].add(coarse_share)
    node_grads = own_grads.astype(BF16)
    return (
        edge_output,
        node_output,
        edge_grads,
        node_grads,
        weights[: 3 * half].reshape(3, half, 2 * half),
        weights[3 * half : 4 * half],
        weights[4 * half : 6 * half].reshape(2, half, 2 * half),
        weights[6 * half :],
    )


def solution(mesh):
    placed = (
        P("patch", "lat"),
        P("patch", "lat"),
        P("patch", None),
        P("patch", None),
        P("patch"),
        P(None, "lat", None),
        P("lat", None),
        P(None, "lat", None),
        P("lat", None),
        P("patch", "lat"),
        P("patch", "lat"),
    )
    return jax.shard_map(
        body,
        mesh=mesh,
        in_specs=placed,
        out_specs=(
            P("patch", "lat"),
            P("patch", "lat"),
            P("patch", "lat"),
            P("patch", "lat"),
            P(None, "lat", None),
            P("lat", None),
            P(None, "lat", None),
            P("lat", None),
        ),
        check_vma=False,
    )
```

```python
import jax
import jax.numpy as jnp
from jax import lax
from jax.experimental import pallas as pl
from jax.experimental.pallas import tpu as pltpu
from jax.sharding import PartitionSpec as P

HALO = 32
COARSE = 8
FINE = 1152
EPSILON = 1e-05
F32 = jnp.float32
BF16 = jnp.bfloat16
I32 = jnp.int32
LANES = 128
VMEM_LIMIT = 48 * 1024 * 1024


def dot(left, right):
    return jnp.dot(left, right, preferred_element_type=F32)


def contract_rows(left, right):
    return lax.dot_general(left, right, (((0,), (0,)), ((), ())), preferred_element_type=F32)


def contract_cols(left, right):
    return lax.dot_general(left, right, (((1,), (1,)), ((), ())), preferred_element_type=F32)


def layer_norm(values):
    centered = values - jnp.mean(values, axis=1, keepdims=True)
    inverse = lax.rsqrt(jnp.mean(centered * centered, axis=1, keepdims=True) + EPSILON)
    return centered * inverse, inverse


def norm_backward(cotangent, normed, inverse):
    mean = jnp.mean(cotangent, axis=1, keepdims=True)
    crossed = jnp.mean(cotangent * normed, axis=1, keepdims=True)
    return (cotangent - mean - normed * crossed) * inverse


def swish_parts(values):
    sigmoid = jax.nn.sigmoid(values)
    return values * sigmoid, sigmoid * (1.0 + values * (1.0 - sigmoid))


def one_hot(index, width):
    return (index == lax.broadcasted_iota(I32, (index.shape[0], width), 1)).astype(F32).astype(BF16)


def one_hot_t(index, width):
    return (index == lax.broadcasted_iota(I32, (width, index.shape[1]), 0)).astype(F32).astype(BF16)


def swap_lat(value):
    return lax.ppermute(value, "lat", [(0, 1), (1, 0)])


def swap_core(value):
    count = lax.axis_size("patch")
    return lax.ppermute(value, "patch", [(i, i ^ 1) for i in range(count)])


def shifted(value, steps):
    count = lax.axis_size("patch")
    return lax.ppermute(value, "patch", [(i, (i + steps) % count) for i in range(count)])


def other_neighbour(value):
    count = lax.axis_size("patch")
    pairs = []
    for patch in range(count):
        for lat in range(2):
            pairs.append((patch * 2 + lat, (patch ^ 2) * 2 + (1 - lat)))
    return lax.ppermute(value, ("patch", "lat"), pairs)


def chips_all_to_all(value):
    count = lax.axis_size("patch")
    groups = [list(range(core, count, 2)) for core in range(2)]
    return lax.all_to_all(value, "patch", 0, 0, tiled=True, axis_index_groups=groups)


def pairs_all_to_all(value):
    count = lax.axis_size("patch")
    groups = [
        [patch * 2 + lat for patch in range(core, count, 2) for lat in range(2)]
        for core in range(2)
    ]
    return lax.all_to_all(value, ("patch", "lat"), 0, 0, tiled=True, axis_index_groups=groups)


def whole(shape):
    return pl.BlockSpec(shape, lambda i, s: (0,) * len(shape), pipeline_mode=pl.Buffered(1))


def block(shape, index):
    return pl.BlockSpec(shape, index, pipeline_mode=pl.Buffered(1))


def call(kernel, info, operands, in_specs, outs, scratch=(), flops=0, moved=0, name=None):
    return pl.pallas_call(
        kernel,
        grid_spec=pltpu.PrefetchScalarGridSpec(
            num_scalar_prefetch=1,
            grid=(1,),
            in_specs=in_specs,
            out_specs=[whole(shape) for shape, _ in outs],
            scratch_shapes=list(scratch),
        ),
        out_shape=[jax.ShapeDtypeStruct(shape, dtype) for shape, dtype in outs],
        compiler_params=pltpu.CompilerParams(vmem_limit_bytes=VMEM_LIMIT),
        cost_estimate=pl.CostEstimate(flops=flops, bytes_accessed=moved, transcendentals=0),
        name=name,
    )(info, *operands)


def pack_kernel(info, xf, xl, gf, gl, n, ng, wi, wo, ni, no, xs, gs, ns, wes, wns, coarse):
    fine, nodes = xf.shape[0], n.shape[0]
    ns[:nodes] = n[...]
    ns[nodes:] = ng[...]
    xs[:fine] = xf[...]
    xs[fine:] = xl[...]
    gs[:fine] = gf[...]
    gs[fine:] = gl[...]
    wes[:3] = wi[...]
    wes[3] = wo[...]
    wns[:2] = ni[...]
    wns[2] = no[...]
    coarse[...] = jnp.broadcast_to(n[:COARSE][None], coarse.shape)


def results_kernel(info, mine, other, inner, outer, node_inner, node_outer, staged, sems):
    first = info[1] == 0
    blocks, half = mine.shape[0], staged.shape[1]
    targets = [inner.at[0], inner.at[1], inner.at[2], outer, node_inner.at[0], node_inner.at[1], node_outer]
    copies = []
    for k, target in enumerate(targets):
        rows = slice(k * half, (k + 1) * half)
        for i in range(blocks):
            a, b = mine[i, rows].astype(F32), other[i, rows].astype(F32)
            staged[k, :, i * LANES : (i + 1) * LANES] = jnp.where(first, a, b)
            staged[k, :, half + i * LANES : half + (i + 1) * LANES] = jnp.where(first, b, a)
        copies.append(pltpu.make_async_copy(staged.at[k], target, sems.at[k]))
        copies[-1].start()
    for copy in copies:
        copy.wait()


def weights_kernel(info, wi, wo, got, again, full_in, full_out):
    lat, core = info[0], info[1]
    half = wo.shape[0]
    quarter = half // 2
    inner = wi.shape[0]
    first = core == 0
    for k in range(inner):
        full_in[k, :half] = wi[k]
        full_in[k, half : half + quarter] = jnp.where(first, got[k], again[k])
        full_in[k, half + quarter :] = jnp.where(first, again[k], got[k])
    own = wo[...]
    top = jnp.where(first, got[inner], again[inner])
    bottom = jnp.where(first, again[inner], got[inner])
    missing = jnp.concatenate([top, bottom], 0)
    low = lat == 0
    for rows, value in ((slice(0, half), jnp.where(low, own, missing)), (slice(half, 2 * half), jnp.where(low, missing, own))):
        full_out[rows, :half] = jnp.where(low, value[:, :half], value[:, half:])
        full_out[rows, half:] = jnp.where(low, value[:, half:], value[:, :half])


def edge_rows(x, sender, receiver, mask, w_in, w_out, rows, half, slope, act, normed, inverse, out_own, out_sent, update):
    pre = dot(x, w_in[0]) + dot(sender, w_in[1]) + dot(receiver, w_in[2])
    value, derivative = swish_parts(pre)
    value = value.astype(BF16)
    slope[rows] = derivative
    act[rows] = value
    scaled, scale = layer_norm(dot(value, w_out[...]))
    normed[rows] = scaled
    inverse[rows] = scale
    change = scaled if mask is None else scaled * mask
    out = (x.astype(F32) + change).astype(BF16)
    out_own[rows] = out[:, :half]
    out_sent[rows] = out[:, half:]
    update[rows] = change.astype(BF16)


def fine_kernel(info, x_own, x_got, n_own, n_got, low, high, near, recv, recv_t, w_in, w_out,
                slope, act, normed, inverse, out_own, out_sent, partial, ext, update):
    half = x_own.shape[1]
    nodes = n_own.shape[0]
    ext[:HALO] = low[...]
    ext[HALO : HALO + nodes, :half] = n_own[...]
    ext[HALO : HALO + nodes, half:] = n_got[...]
    ext[HALO + nodes :] = high[...]
    node_x = ext[HALO : HALO + nodes]
    chunk = 192
    for start in range(0, x_own.shape[0], chunk):
        rows = pl.ds(start, chunk)
        x = jnp.concatenate([x_own[rows], x_got[rows]], 1)
        sender = dot(one_hot(near[rows], ext.shape[0]), ext[...]).astype(BF16)
        receiver = dot(one_hot(recv[rows], nodes), node_x).astype(BF16)
        edge_rows(x, sender, receiver, None, w_in, w_out, rows, half, slope, act, normed, inverse, out_own, out_sent, update)
    partial[...] = dot(one_hot_t(recv_t[...], nodes), update[...])


def long_kernel(info, x_own, x_got, n_own, n_got, same, other, far_same, far_other, recv, recv_t, mask, w_in, w_out, before,
                slope, act, normed, inverse, out_own, out_sent, partial, sent, sender_rows, update):
    lat = info[0]
    half = x_own.shape[1]
    nodes = n_own.shape[0]
    rows = pl.ds(0, x_own.shape[0])
    count = same.shape[0]
    for side, columns in ((lat, slice(0, half)), (1 - lat, slice(half, 2 * half))):
        value = dot(one_hot(far_same[...] + side * COARSE, count), same[...])
        value = value + dot(one_hot(far_other[...] + side * COARSE, count), other[...])
        sender_rows[:, columns] = value.astype(BF16)
    x = jnp.concatenate([x_own[...], x_got[...]], 1)
    node_x = jnp.concatenate([n_own[...], n_got[...]], 1)
    receiver = dot(one_hot(recv[...], nodes), node_x).astype(BF16)
    edge_rows(x, sender_rows[...], receiver, mask[...], w_in, w_out, rows, half, slope, act, normed, inverse, out_own, out_sent, update)
    total = before[...] + dot(one_hot_t(recv_t[...], nodes), update[...])
    partial[...] = total
    sent[...] = total.astype(BF16)


def back_kernel(info, partial, got, n_own, n_got, ng_own, ng_got, low, high, nin, nout,
                xf_own, xl_own, xf_got, xl_got, gf_own, gl_own, gf_got, gl_got,
                slope_f, slope_l, act_f, act_l, normed_f, normed_l, inverse_f, inverse_l, mask, srow_l,
                recv, recv_t, near_t, far_t, w_in, w_out,
                node_out, node_self, node_keep, node_send, edge_keep, edge_send, far_keep, far_send, dpre, near_sum, recv_sum,
                ndpre, ndy, nact, agg_grad, dy, ext):
    lat, core = info[0], info[1]
    half = n_own.shape[1]
    nodes = n_own.shape[0]
    fine, longs = xf_own.shape[0], xl_own.shape[0]
    mine = pl.ds(pl.multiple_of(core * half, half), half)
    theirs = pl.ds(pl.multiple_of((1 - core) * half, half), half)
    turn = (core + lat) % 2
    mine_own = pl.ds(pl.multiple_of(turn * half, half), half)
    theirs_own = pl.ds(pl.multiple_of((1 - turn) * half, half), half)
    hidden_mine = pl.ds(pl.multiple_of(lat * half, half), half)
    hidden_theirs = pl.ds(pl.multiple_of((1 - lat) * half, half), half)

    ext[:HALO] = low[...]
    ext[HALO : HALO + nodes, :half] = n_own[...]
    ext[HALO : HALO + nodes, half:] = n_got[...]
    ext[HALO + nodes :] = high[...]
    node_x = ext[HALO : HALO + nodes]
    received = got[...].astype(F32)
    agg = (partial[...] + jnp.concatenate([received[:, half:], received[:, :half]], 1)).astype(BF16)
    node_value, node_slope = swish_parts(dot(node_x, nin[0]) + dot(agg, nin[1]))
    nact[...] = node_value.astype(BF16)
    node_normed, node_inverse = layer_norm(dot(nact[...], nout[...]))
    node_out[...] = (n_own[...].astype(F32) + node_normed[:, :half]).astype(BF16)
    node_g = jnp.concatenate([ng_own[...], ng_got[...]], 1).astype(F32)
    ndy[...] = norm_backward(node_g, node_normed, node_inverse).astype(BF16)
    ndpre[...] = (contract_cols(ndy[...], nout[...]) * node_slope).astype(BF16)
    agg_grad[...] = contract_cols(ndpre[...], nin[1]).astype(BF16)
    node_self[...] = ng_own[...].astype(F32) + contract_cols(ndpre[...], nin[0, :half])

    chunk = 192
    for start in range(0, fine + longs, chunk):
        rows = pl.ds(start, chunk)
        if start < fine:
            part = pl.ds(start, chunk)
            g_own, g_got, normed, inverse, slope = gf_own, gf_got, normed_f, inverse_f, slope_f
        else:
            part = pl.ds(start - fine, chunk)
            g_own, g_got, normed, inverse, slope = gl_own, gl_got, normed_l, inverse_l, slope_l
        cotangent = jnp.concatenate([g_own[part], g_got[part]], 1).astype(F32)
        cotangent = cotangent + dot(one_hot(recv[rows], nodes), agg_grad[...])
        if start >= fine:
            cotangent = cotangent * mask[part]
        dy[rows] = norm_backward(cotangent, normed[part], inverse[part]).astype(BF16)
        dpre[rows] = (contract_cols(dy[rows], w_out[...]) * slope[part]).astype(BF16)

    tail = pl.ds(fine, longs)
    head = pl.ds(0, fine)
    srow_grads = contract_cols(dpre[tail], w_in[1]).astype(BF16)
    far = dot(one_hot_t(far_t[...], 2 * far_keep.shape[0]), srow_grads).astype(BF16)
    far_keep[...] = far[: far_keep.shape[0]]
    far_send[...] = far[far_keep.shape[0] :]
    near_sum[...] = dot(one_hot_t(near_t[...], ext.shape[0]), dpre[head]).astype(BF16)
    recv_sum[...] = dot(one_hot_t(recv_t[...], nodes), dpre[...]).astype(BF16)
    for keep, node_keep_ref, columns, columns_own in (
        (edge_send, node_send, theirs, theirs_own),
        (edge_keep, node_keep, mine, mine_own),
    ):
        for side, xf, xl, hidden, cols in (
            (1, xf_got, xl_got, hidden_theirs, slice(half, 2 * half)),
            (0, xf_own, xl_own, hidden_mine, slice(0, half)),
        ):
            grad = contract_rows(xf[...], dpre[head, columns]) + contract_rows(xl[...], dpre[tail, columns])
            keep[side, 0] = grad.astype(BF16)
            grad = contract_rows(ext[:, cols], near_sum[:, columns]) + contract_rows(srow_l[:, cols], dpre[tail, columns])
            keep[side, 1] = grad.astype(BF16)
            keep[side, 2] = contract_rows(ext[HALO : HALO + nodes, cols], recv_sum[:, columns]).astype(BF16)
            grad = contract_rows(act_f[:, hidden], dy[head, columns_own]) + contract_rows(act_l[:, hidden], dy[tail, columns_own])
            keep[side, 3] = grad.astype(BF16)
        node_keep_ref[0] = contract_rows(n_own[...], ndpre[:, columns]).astype(BF16)
        node_keep_ref[1] = contract_rows(agg[:, :half], ndpre[:, columns]).astype(BF16)
        node_keep_ref[2] = contract_rows(nact[:, hidden_mine], ndy[:, columns_own]).astype(BF16)


def inputs_kernel(info, dpre, gf_own, gl_own, g_got, near_sum, recv_sum, w_in,
                  grads_own, grads_sent, rim_own, rim_sent):
    half = g_got.shape[1]
    fine, longs = gf_own.shape[0], gl_own.shape[0]
    nodes = recv_sum.shape[0]
    for start, rows, own in ((0, fine, gf_own), (fine, longs, gl_own)):
        part = pl.ds(start, rows)
        change = contract_cols(dpre[part], w_in[0])
        grads_own[part] = (own[...].astype(F32) + change[:, :half]).astype(BF16)
        grads_sent[part] = (g_got[part].astype(F32) + change[:, half:]).astype(BF16)
    near = contract_cols(near_sum[...], w_in[1])
    received = contract_cols(recv_sum[...], w_in[2])
    for rows, value in (
        (slice(0, HALO), near[:HALO]),
        (slice(HALO, HALO + nodes), near[HALO : HALO + nodes] + received),
        (slice(HALO + nodes, 2 * HALO + nodes), near[HALO + nodes :]),
    ):
        rim_own[rows] = value[:, :half]
        rim_sent[rows] = value[:, half:].astype(BF16)


def body(
    node_latents,
    edge_latents,
    senders,
    receivers,
    long_count,
    edge_inner,
    edge_outer,
    node_inner,
    node_outer,
    node_cotangent,
    edge_cotangent,
):
    nodes, half = node_latents.shape
    full = 2 * half
    edges = edge_latents.shape[0]
    rows = edges // 2
    fine, longs = FINE // 2, (edges - FINE) // 2
    quarter = half // 2
    patches = lax.axis_size("patch")
    chips = patches // 2
    extent = nodes + 2 * HALO
    lat = lax.axis_index("lat")
    patch = lax.axis_index("patch")
    core = patch % 2
    first_node = patch * nodes
    info = jnp.stack([lat, core]).astype(I32)

    fine_other = block((fine, half), lambda i, s: (1 - s[0], 0))
    long_other = block((longs, half), lambda i, s: (FINE // longs + 1 - s[0], 0))
    quarter_rows = block((quarter, full), lambda i, s: (s[1], 0))
    sent_x, sent_g, sent_n, sent_we, sent_wn, sent_coarse = call(
        pack_kernel,
        info,
        (edge_latents, edge_latents, edge_cotangent, edge_cotangent, node_latents, node_cotangent,
         edge_inner, edge_outer, node_inner, node_outer),
        [
            fine_other, long_other, fine_other, long_other, whole((nodes, half)), whole((nodes, half)),
            block((3, quarter, full), lambda i, s: (0, s[1], 0)), quarter_rows,
            block((2, quarter, full), lambda i, s: (0, s[1], 0)), quarter_rows,
        ],
        [
            ((rows, half), BF16),
            ((rows, half), BF16),
            ((2 * nodes, half), BF16),
            ((4, quarter, full), BF16),
            ((3, quarter, full), BF16),
            ((patches, COARSE, half), BF16),
        ],
        moved=5_000_000,
        name="pack",
    )
    node_got = swap_lat(sent_n)
    we_got = other_neighbour(sent_we)
    x_got = swap_lat(sent_x)
    same = pairs_all_to_all(sent_coarse)
    other = swap_core(same)
    same, other = same.reshape(patches * COARSE, half), other.reshape(patches * COARSE, half)
    low = shifted(
        jnp.concatenate([node_latents[nodes - HALO :], node_got[nodes - HALO : nodes]], 1), 1
    )
    high = shifted(jnp.concatenate([node_latents[:HALO], node_got[:HALO]], 1), -1)
    we_again = swap_core(we_got)
    wn_got = other_neighbour(sent_wn)
    wn_again = swap_core(wn_got)
    g_got = swap_lat(sent_g)

    def rows_of(value):
        return jnp.concatenate(
            [
                lax.dynamic_slice_in_dim(value, lat * fine, fine, 0),
                lax.dynamic_slice_in_dim(value, FINE + lat * longs, longs, 0),
            ]
        )

    sender_ids = rows_of(senders.reshape(edges))
    recv = rows_of(receivers.reshape(edges)) - first_node
    near = (sender_ids[:fine] - first_node + HALO) % (nodes * patches)
    far_ids = sender_ids[fine:]
    far_patch, far_row = far_ids // nodes, far_ids % nodes
    is_same = far_patch % 2 == core
    far_base = far_patch // 2 * (2 * COARSE) + far_row
    far_same = jnp.where(is_same, far_base, -4 * patches * COARSE)
    far_other = jnp.where(is_same, -4 * patches * COARSE, far_base)
    far_slot = jnp.where(is_same, 0, chips * COARSE) + far_patch // 2 * COARSE + far_row
    mask = (jnp.arange(longs, dtype=I32) + lat * longs < long_count[0]).astype(F32)[:, None]
    recv_c, recv_r = recv[:, None], recv[None, :]
    recv_fc, recv_fr = recv[:fine, None], recv[None, :fine]
    recv_lc, recv_lr = recv[fine:, None], recv[None, fine:]

    def weights_of(wi, wo, got, again, name):
        count = wi.shape[0]
        return call(
            weights_kernel,
            info,
            (wi, wo, got, again),
            [
                whole((count, half, full)),
                whole((half, full)),
                whole((count + 1, quarter, full)),
                whole((count + 1, quarter, full)),
            ],
            [((count, full, full), BF16), ((full, full), BF16)],
            moved=4 * (count + 1) * full * full,
            name=name,
        )

    w_in, w_out = weights_of(edge_inner, edge_outer, we_got, we_again, "edge_weights")
    nin, nout = weights_of(node_inner, node_outer, wn_got, wn_again, "node_weights")

    def fine_own():
        return block((fine, half), lambda i, s: (s[0], 0))

    def long_own():
        return block((longs, half), lambda i, s: (FINE // longs + s[0], 0))

    def fine_got():
        return whole((fine, half))

    def long_got():
        return block((longs, half), lambda i, s: (fine // longs, 0))

    node_spec = whole((nodes, half))
    second_nodes = block((nodes, half), lambda i, s: (1, 0))
    rim = whole((HALO, full))
    win_spec, wout_spec = whole((3, full, full)), whole((full, full))

    def forward_outs(count):
        return [
            ((count, full), F32),
            ((count, full), BF16),
            ((count, full), F32),
            ((count, 1), F32),
            ((count, half), BF16),
            ((count, half), BF16),
            ((nodes, full), F32),
        ]

    slope_f, act_f, normed_f, inverse_f, fine_out, fine_sent, partial_f = call(
        fine_kernel,
        info,
        (edge_latents, x_got, node_latents, node_got, low, high, near[:, None], recv_fc, recv_fr, w_in, w_out),
        [
            fine_own(), fine_got(), node_spec, whole((nodes, half)), rim, rim,
            whole((fine, 1)), whole((fine, 1)), whole((1, fine)), win_spec, wout_spec,
        ],
        forward_outs(fine),
        [pltpu.VMEM((extent, full), BF16), pltpu.VMEM((fine, full), BF16)],
        flops=2 * fine * full * (4 * full + extent + 2 * nodes),
        moved=8_000_000,
        name="edges_forward_fine",
    )
    slope_l, act_l, normed_l, inverse_l, long_out, long_sent, partial, partial_sent, srow_l = call(
        long_kernel,
        info,
        (edge_latents, x_got, node_latents, node_got, same, other, far_same[:, None], far_other[:, None],
         recv_lc, recv_lr, mask, w_in, w_out, partial_f),
        [
            long_own(), long_got(), node_spec, whole((nodes, half)),
            whole((patches * COARSE, half)), whole((patches * COARSE, half)),
            whole((longs, 1)), whole((longs, 1)), whole((longs, 1)), whole((1, longs)), whole((longs, 1)),
            win_spec, wout_spec, whole((nodes, full)),
        ],
        forward_outs(longs) + [((nodes, full), BF16), ((longs, full), BF16)],
        [pltpu.VMEM((longs, full), BF16)],
        flops=2 * longs * full * (4 * full + 4 * patches * COARSE + 2 * nodes),
        moved=6_000_000,
        name="edges_forward_long",
    )
    partial_got = swap_lat(partial_sent)

    (node_output, node_self, node_keep, node_send, edge_keep, edge_send, far_keep, far_send,
     dpre, near_sum, recv_sum) = call(
        back_kernel,
        info,
        (partial, partial_got, node_latents, node_got, node_cotangent, node_got, low, high, nin, nout,
         edge_latents, edge_latents, x_got, x_got, edge_cotangent, edge_cotangent, g_got, g_got,
         slope_f, slope_l, act_f, act_l, normed_f, normed_l, inverse_f, inverse_l, mask, srow_l,
         recv_c, recv_r, near[None, :], far_slot[None, :], w_in, w_out),
        [
            whole((nodes, full)), whole((nodes, full)), node_spec, whole((nodes, half)), node_spec, second_nodes,
            rim, rim, whole((2, full, full)), wout_spec,
            fine_own(), long_own(), fine_got(), long_got(), fine_own(), long_own(), fine_got(), long_got(),
            whole((fine, full)), whole((longs, full)), whole((fine, full)), whole((longs, full)),
            whole((fine, full)), whole((longs, full)), whole((fine, 1)), whole((longs, 1)), whole((longs, 1)),
            whole((longs, full)),
            whole((rows, 1)), whole((1, rows)), whole((1, fine)), whole((1, longs)), win_spec, wout_spec,
        ],
        [
            ((nodes, half), BF16),
            ((nodes, half), F32),
            ((3, half, half), BF16),
            ((3, half, half), BF16),
            ((2, 4, half, half), BF16),
            ((2, 4, half, half), BF16),
            ((chips * COARSE, full), BF16),
            ((chips * COARSE, full), BF16),
            ((rows, full), BF16),
            ((extent, full), BF16),
            ((nodes, full), BF16),
        ],
        [
            pltpu.VMEM((nodes, full), BF16),
            pltpu.VMEM((nodes, full), BF16),
            pltpu.VMEM((nodes, full), BF16),
            pltpu.VMEM((nodes, full), BF16),
            pltpu.VMEM((rows, full), BF16),
            pltpu.VMEM((extent, full), BF16),
        ],
        flops=8 * rows * full * full,
        moved=14_000_000,
        name="nodes_and_edges_backward",
    )

    core_edge, core_far, core_node = swap_core(edge_send), swap_core(far_send), swap_core(node_send)
    edge_parts = edge_keep.astype(F32) + core_edge.astype(F32)
    far_parts = far_keep.astype(F32) + core_far.astype(F32)
    node_parts = node_keep.astype(F32) + core_node.astype(F32)
    edge_sent, far_sent = edge_parts[1].astype(BF16), far_parts[:, half:].astype(BF16)
    middle = chips * COARSE // 2
    lat_edge = jnp.concatenate([swap_lat(edge_sent[:2]), other_neighbour(edge_sent[2:])], 0)
    lat_far = jnp.concatenate([swap_lat(far_sent[:middle]), other_neighbour(far_sent[middle:])], 0)
    weight_parts = jnp.concatenate(
        [(edge_parts[0] + lat_edge.astype(F32)).reshape(4 * half, half), node_parts.reshape(3 * half, half)], 0
    ).astype(BF16)
    far_own = (far_parts[:, :half] + lat_far.astype(F32)).astype(BF16).reshape(chips, COARSE, half)
    blocks = half // LANES
    total_rows = weight_parts.shape[0] * blocks
    share = total_rows // chips
    weight_parts = jnp.concatenate(
        [weight_parts[:, i * LANES : (i + 1) * LANES] for i in range(blocks)], 0
    ).reshape(chips, share, LANES)
    far_own = jnp.concatenate(
        [far_own[:, :, i * LANES : (i + 1) * LANES] for i in range(blocks)], 1
    )
    arrived = chips_all_to_all(jnp.concatenate([weight_parts, far_own], 1))

    grads_own, grads_sent, rim_own, rim_sent = call(
        inputs_kernel,
        info,
        (dpre, edge_cotangent, edge_cotangent, g_got, near_sum, recv_sum, w_in),
        [
            whole((rows, full)), fine_own(), long_own(), whole((rows, half)),
            whole((extent, full)), whole((nodes, full)), win_spec,
        ],
        [((rows, half), BF16), ((rows, half), BF16), ((extent, half), F32), ((extent, half), BF16)],
        flops=4 * rows * full * full,
        moved=5_000_000,
        name="input_gradients",
    )

    def ordered(mine, other):
        return jnp.where(lat == 0, jnp.concatenate([mine, other], 0), jnp.concatenate([other, mine], 0))

    def back_to_columns(fine_mine, long_mine, got):
        return jnp.concatenate([ordered(fine_mine, got[:fine]), ordered(long_mine, got[fine:])], 0)

    edge_output = back_to_columns(fine_out, long_out, swap_lat(jnp.concatenate([fine_sent, long_sent], 0)))
    edge_grads = back_to_columns(grads_own[:fine], grads_own[fine:], swap_lat(grads_sent))
    summed = rim_own + swap_lat(rim_sent).astype(F32)
    to_low = shifted(summed[:HALO].astype(BF16), -1).astype(F32)
    to_high = shifted(summed[HALO + nodes :].astype(BF16), 1).astype(F32)

    total = jnp.sum(arrived.astype(F32), 0)
    coarse_share = jnp.concatenate(
        [total[share + i * COARSE : share + (i + 1) * COARSE] for i in range(blocks)], 1
    )
    weight_share = (total[:share] / patches).astype(BF16)
    own_grads = node_self + summed[HALO : HALO + nodes]
    own_grads = own_grads.at[nodes - HALO :].add(to_low)
    own_grads = own_grads.at[:HALO].add(to_high)
    own_grads = own_grads.at[:COARSE].add(coarse_share)
    node_grads = own_grads.astype(BF16)
    mine = chips_all_to_all(jnp.broadcast_to(weight_share[None], (chips, share, LANES)))
    mine = mine.reshape(blocks, total_rows // blocks, LANES)
    other = swap_core(mine)
    square = (half, full)
    weights = pl.pallas_call(
        results_kernel,
        grid_spec=pltpu.PrefetchScalarGridSpec(
            num_scalar_prefetch=1,
            grid=(1,),
            in_specs=[whole(mine.shape)] * 2,
            out_specs=[pl.BlockSpec(memory_space=pl.ANY)] * 4,
            scratch_shapes=[pltpu.VMEM((7,) + square, F32), pltpu.SemaphoreType.DMA((7,))],
        ),
        out_shape=[jax.ShapeDtypeStruct(shape, F32) for shape in ((3,) + square, square, (2,) + square, square)],
        compiler_params=pltpu.CompilerParams(vmem_limit_bytes=VMEM_LIMIT),
        cost_estimate=pl.CostEstimate(flops=0, bytes_accessed=6_000_000, transcendentals=0),
        name="results",
    )(info, mine, other)
    return (edge_output, node_output, edge_grads, node_grads, *weights)


def solution(mesh):
    placed = (
        P("patch", "lat"),
        P("patch", "lat"),
        P("patch", None),
        P("patch", None),
        P("patch"),
        P(None, "lat", None),
        P("lat", None),
        P(None, "lat", None),
        P("lat", None),
        P("patch", "lat"),
        P("patch", "lat"),
    )
    return jax.shard_map(
        body,
        mesh=mesh,
        in_specs=placed,
        out_specs=(
            P("patch", "lat"),
            P("patch", "lat"),
            P("patch", "lat"),
            P("patch", "lat"),
            P(None, "lat", None),
            P("lat", None),
            P(None, "lat", None),
            P("lat", None),
        ),
        check_vma=False,
    )
```

```python
import functools

import jax
import jax.numpy as jnp
from jax import lax
from jax.experimental import pallas as pl
from jax.experimental.pallas import tpu as pltpu
from jax.sharding import PartitionSpec as P

HALO = 32
COARSE = 8
FINE = 1152
EPSILON = 1e-05
F32 = jnp.float32
BF16 = jnp.bfloat16
I32 = jnp.int32
LANES = 128
VMEM_LIMIT = 28 * 1024 * 1024


def dot(left, right):
    return jnp.dot(left, right, preferred_element_type=F32)


def contract_rows(left, right):
    return lax.dot_general(left, right, (((0,), (0,)), ((), ())), preferred_element_type=F32)


def contract_cols(left, right):
    return lax.dot_general(left, right, (((1,), (1,)), ((), ())), preferred_element_type=F32)


def layer_norm(values):
    centered = values - jnp.mean(values, axis=1, keepdims=True)
    inverse = lax.rsqrt(jnp.mean(centered * centered, axis=1, keepdims=True) + EPSILON)
    return centered * inverse, inverse


def norm_backward(cotangent, normed, inverse):
    mean = jnp.mean(cotangent, axis=1, keepdims=True)
    crossed = jnp.mean(cotangent * normed, axis=1, keepdims=True)
    return (cotangent - mean - normed * crossed) * inverse


def swish_parts(values):
    sigmoid = jax.nn.sigmoid(values)
    return values * sigmoid, sigmoid * (1.0 + values * (1.0 - sigmoid))


def one_hot(index, width):
    return (index == lax.broadcasted_iota(I32, (index.shape[0], width), 1)).astype(F32).astype(BF16)


def one_hot_t(index, width):
    return (index == lax.broadcasted_iota(I32, (width, index.shape[1]), 0)).astype(F32).astype(BF16)


def swap_lat(value):
    return lax.ppermute(value, "lat", [(0, 1), (1, 0)])


def swap_core(value):
    count = lax.axis_size("patch")
    return lax.ppermute(value, "patch", [(i, i ^ 1) for i in range(count)])


def shifted(value, steps):
    count = lax.axis_size("patch")
    return lax.ppermute(value, "patch", [(i, (i + steps) % count) for i in range(count)])


def other_neighbour(value):
    count = lax.axis_size("patch")
    pairs = []
    for patch in range(count):
        for lat in range(2):
            pairs.append((patch * 2 + lat, (patch ^ 2) * 2 + (1 - lat)))
    return lax.ppermute(value, ("patch", "lat"), pairs)


def chips_all_to_all(value):
    count = lax.axis_size("patch")
    groups = [list(range(core, count, 2)) for core in range(2)]
    return lax.all_to_all(value, "patch", 0, 0, tiled=True, axis_index_groups=groups)


def whole(shape):
    return pl.BlockSpec(shape, lambda i, s: (0,) * len(shape), pipeline_mode=pl.Buffered(1))


def block(shape, index):
    return pl.BlockSpec(shape, index, pipeline_mode=pl.Buffered(1))


def call(kernel, info, operands, in_specs, outs, scratch=(), flops=0, moved=0, name=None):
    return pl.pallas_call(
        kernel,
        grid_spec=pltpu.PrefetchScalarGridSpec(
            num_scalar_prefetch=1,
            grid=(1,),
            in_specs=in_specs,
            out_specs=[whole(shape) for shape, _ in outs],
            scratch_shapes=list(scratch),
        ),
        out_shape=[jax.ShapeDtypeStruct(shape, dtype) for shape, dtype in outs],
        compiler_params=pltpu.CompilerParams(vmem_limit_bytes=VMEM_LIMIT),
        cost_estimate=pl.CostEstimate(flops=flops, bytes_accessed=moved, transcendentals=0),
        name=name,
    )(info, *operands)


def pinned(value):
    return pltpu.with_memory_space_constraint(value, pltpu.HBM)


def pack_kernel(info, xf, xl, n, ng, wi, wo, xs, ns, wes):
    fine, nodes = xf.shape[0], n.shape[0]
    ns[:nodes] = n[...]
    ns[nodes:] = ng[...]
    wes[:3] = wi[...]
    wes[3] = wo[...]
    xs[:fine] = xf[...]
    xs[fine:] = xl[...]


def coarse_kernel(info, n_own, n_got, idx_f, idx_l, out):
    rows = jnp.concatenate([n_own[:COARSE], n_got[:COARSE]], 1)
    out[...] = jnp.broadcast_to(rows[None], out.shape)


def lat_stage_kernel(info, keep, got, first, second):
    rows = first.shape[0]
    first[...] = (keep[:rows].astype(F32) + got[:rows].astype(F32)).astype(BF16)
    second[...] = (keep[rows:].astype(F32) + got[rows:].astype(F32)).astype(BF16)


def combine_kernel(info, keep, got, first, second, out):
    chips = out.shape[0]
    rows = first.shape[0]
    edge_rows_count, far_rows = 2 * rows - chips * COARSE, chips * COARSE
    half_chips = chips // 2
    total = keep[...].astype(F32) + got[...].astype(F32)
    pair = jnp.concatenate([first[...], second[...]], 0).astype(F32)
    weights = jnp.concatenate(
        [total[:edge_rows_count] + pair[:edge_rows_count], total[edge_rows_count:-far_rows]], 0
    )
    far = total[-far_rows:] + pair[edge_rows_count:]
    share = weights.shape[0] // half_chips
    parts = [weights[:, i * LANES : (i + 1) * LANES].reshape(half_chips, share, LANES) for i in range(2)]
    coarse = [far[:, i * LANES : (i + 1) * LANES].reshape(chips, COARSE, LANES) for i in range(2)]
    out[...] = jnp.concatenate([jnp.concatenate(parts, 0)] + coarse, 1).astype(BF16)


def share_kernel(info, arrived, output, grads, low, high, weights, coarse, *, scale):
    share = weights.shape[1]
    total = jnp.sum(arrived[...].astype(F32), 0)
    weights[...] = jnp.broadcast_to((total[:share] * scale).astype(BF16)[None], weights.shape)
    coarse[...] = total[share:]


def rows_kernel(info, own_f, own_l, got, out):
    lat = info[0]
    fine, longs = own_f.shape[0], own_l.shape[0]
    for side, f, l in ((lat, own_f[...], own_l[...]), (1 - lat, got[:fine], got[fine:])):
        out[pl.ds(pl.multiple_of(side * fine, 64), fine)] = f
        out[pl.ds(pl.multiple_of(FINE + side * longs, 64), longs)] = l


def results_kernel(info, mine, other, inner, outer, node_inner, node_outer, staged, sems):
    first = info[1] == 0
    blocks, half = mine.shape[0], staged.shape[1]
    targets = [inner.at[0], inner.at[1], inner.at[2], outer, node_inner.at[0], node_inner.at[1], node_outer]
    copies = []
    for k, target in enumerate(targets):
        rows = slice(k * half, (k + 1) * half)
        for i in range(blocks):
            a, b = mine[i, rows].astype(F32), other[i, rows].astype(F32)
            staged[k, :, i * LANES : (i + 1) * LANES] = jnp.where(first, a, b)
            staged[k, :, half + i * LANES : half + (i + 1) * LANES] = jnp.where(first, b, a)
        copies.append(pltpu.make_async_copy(staged.at[k], target, sems.at[k]))
        copies[-1].start()
    for copy in copies:
        copy.wait()


def edge_weights_kernel(info, wi, wo, got, again, gf, gl, ni, no, after, full_in, full_out, gs, wns):
    fine = gf.shape[0]
    wns[:2] = ni[...]
    wns[2] = no[...]
    gs[:fine] = gf[...]
    gs[fine:] = gl[...]
    weights_kernel(info, wi, wo, got, again, full_in, full_out)


def weights_kernel(info, wi, wo, got, again, full_in, full_out):
    lat, core = info[0], info[1]
    half = wo.shape[0]
    quarter = half // 2
    inner = wi.shape[0]
    first = core == 0
    for k in range(inner):
        full_in[k, :half] = wi[k]
        full_in[k, half : half + quarter] = jnp.where(first, got[k], again[k])
        full_in[k, half + quarter :] = jnp.where(first, again[k], got[k])
    own = wo[...]
    top = jnp.where(first, got[inner], again[inner])
    bottom = jnp.where(first, again[inner], got[inner])
    missing = jnp.concatenate([top, bottom], 0)
    low = lat == 0
    for rows, value in ((slice(0, half), jnp.where(low, own, missing)), (slice(half, 2 * half), jnp.where(low, missing, own))):
        full_out[rows, :half] = jnp.where(low, value[:, :half], value[:, half:])
        full_out[rows, half:] = jnp.where(low, value[:, half:], value[:, :half])


def edge_rows(x, sender, receiver, mask, w_in, w_out, rows, half, slope, act, normed, inverse, out_own, out_sent, update):
    pre = dot(x, w_in[0]) + dot(sender, w_in[1]) + dot(receiver, w_in[2])
    value, derivative = swish_parts(pre)
    value = value.astype(BF16)
    slope[rows] = derivative
    act[rows] = value
    scaled, scale = layer_norm(dot(value, w_out[...]))
    normed[rows] = scaled
    inverse[rows] = scale
    change = scaled if mask is None else scaled * mask
    out = (x.astype(F32) + change).astype(BF16)
    out_own[rows] = out[:, :half]
    out_sent[rows] = out[:, half:]
    update[rows] = change.astype(BF16)


def fine_kernel(info, x_own, x_got, n_own, n_got, low, high, idx_c, idx_r, w_in, w_out,
                slope, act, normed, inverse, out_own, out_sent, partial, sent, ext, update):
    half = x_own.shape[1]
    nodes = n_own.shape[0]
    ext[:HALO] = low[...]
    ext[HALO : HALO + nodes, :half] = n_own[...]
    ext[HALO : HALO + nodes, half:] = n_got[...]
    ext[HALO + nodes :] = high[...]
    node_x = ext[HALO : HALO + nodes]
    chunk = 192
    for start in range(0, x_own.shape[0], chunk):
        rows = pl.ds(start, chunk)
        x = jnp.concatenate([x_own[rows], x_got[rows]], 1)
        sender = dot(one_hot(idx_c[rows, 0:1], ext.shape[0]), ext[...]).astype(BF16)
        receiver = dot(one_hot(idx_c[rows, 1:2], nodes), node_x).astype(BF16)
        edge_rows(x, sender, receiver, None, w_in, w_out, rows, half, slope, act, normed, inverse, out_own, out_sent, update)
    total = dot(one_hot_t(idx_r[1:2], nodes), update[...])
    partial[...] = total
    sent[...] = total.astype(BF16)


def long_kernel(info, x_own, x_got, n_own, n_got, same, other, idx_c, idx_r, w_in, w_out,
                slope, act, normed, inverse, out_own, out_sent, partial, sent, sender_rows, update):
    half = x_own.shape[1]
    rows = pl.ds(0, x_own.shape[0])
    count = same.shape[0]
    value = dot(one_hot(idx_c[:, 0:1], count), same[...])
    value = value + dot(one_hot(idx_c[:, 0:1] - count, count), other[...])
    sender_rows[...] = value.astype(BF16)
    x = jnp.concatenate([x_own[...], x_got[...]], 1)
    near = n_own.shape[0]
    node_x = jnp.concatenate([n_own[...], n_got[...]], 1)
    receiver = dot(one_hot(idx_c[:, 1:2], near), node_x).astype(BF16)
    edge_rows(x, sender_rows[...], receiver, idx_c[:, 2:3].astype(F32), w_in, w_out, rows, half, slope, act, normed, inverse, out_own, out_sent, update)
    total = dot(one_hot_t(idx_r[1:2], near), update[...])
    partial[...] = total
    sent[...] = total.astype(BF16)


def back_kernel(info, partial, got, partial_l, got_l, n_own, n_got, ng_own, ng_got, low, high, nin, nout,
                xf_own, xl_own, xf_got, xl_got, gf_own, gl_own, gf_got, gl_got,
                slope_f, slope_l, act_f, act_l, normed_f, normed_l, inverse_f, inverse_l, srow_l,
                idx_cf, idx_cl, idx_rf, idx_rl, w_in, w_out,
                node_out, node_self, keep_own, send_own, keep_pair, send_pair, dpre, near_sum, recv_sum,
                ndpre, ndy, nact, agg_grad, dy, ext):
    lat, core = info[0], info[1]
    half = n_own.shape[1]
    nodes = n_own.shape[0]
    fine, longs = xf_own.shape[0], xl_own.shape[0]
    mine = pl.ds(pl.multiple_of(core * half, half), half)
    theirs = pl.ds(pl.multiple_of((1 - core) * half, half), half)
    turn = (core + lat) % 2
    mine_own = pl.ds(pl.multiple_of(turn * half, half), half)
    theirs_own = pl.ds(pl.multiple_of((1 - turn) * half, half), half)
    hidden_mine = pl.ds(pl.multiple_of(lat * half, half), half)
    hidden_theirs = pl.ds(pl.multiple_of((1 - lat) * half, half), half)

    ext[:HALO] = low[...]
    ext[HALO : HALO + nodes, :half] = n_own[...]
    ext[HALO : HALO + nodes, half:] = n_got[...]
    ext[HALO + nodes :] = high[...]
    node_x = ext[HALO : HALO + nodes]
    received, received_l = got[...].astype(F32), got_l[...].astype(F32)
    total = partial[...] + jnp.concatenate([received[:, half:], received[:, :half]], 1)
    coarse = partial_l[...] + jnp.concatenate([received_l[:, half:], received_l[:, :half]], 1)
    near = coarse.shape[0]
    agg = jnp.concatenate([total[:near] + coarse, total[near:]], 0).astype(BF16)
    node_value, node_slope = swish_parts(dot(node_x, nin[0]) + dot(agg, nin[1]))
    nact[...] = node_value.astype(BF16)
    node_normed, node_inverse = layer_norm(dot(nact[...], nout[...]))
    node_out[...] = (n_own[...].astype(F32) + node_normed[:, :half]).astype(BF16)
    node_g = jnp.concatenate([ng_own[...], ng_got[...]], 1).astype(F32)
    ndy[...] = norm_backward(node_g, node_normed, node_inverse).astype(BF16)
    ndpre[...] = (contract_cols(ndy[...], nout[...]) * node_slope).astype(BF16)
    agg_grad[...] = contract_cols(ndpre[...], nin[1]).astype(BF16)
    node_self[...] = ng_own[...].astype(F32) + contract_cols(ndpre[...], nin[0, :half])

    chunk = 192
    for start in range(0, fine + longs, chunk):
        rows = pl.ds(start, chunk)
        if start < fine:
            part = pl.ds(start, chunk)
            idx_c = idx_cf
            g_own, g_got, normed, inverse, slope = gf_own, gf_got, normed_f, inverse_f, slope_f
        else:
            part = pl.ds(start - fine, chunk)
            idx_c = idx_cl
            g_own, g_got, normed, inverse, slope = gl_own, gl_got, normed_l, inverse_l, slope_l
        cotangent = jnp.concatenate([g_own[part], g_got[part]], 1).astype(F32)
        cotangent = cotangent + dot(one_hot(idx_c[part, 1:2], nodes), agg_grad[...])
        if start >= fine:
            cotangent = cotangent * idx_cl[part, 2:3].astype(F32)
        dy[rows] = norm_backward(cotangent, normed[part], inverse[part]).astype(BF16)
        dpre[rows] = (contract_cols(dy[rows], w_out[...]) * slope[part]).astype(BF16)

    tail = pl.ds(fine, longs)
    head = pl.ds(0, fine)
    srow_grads = contract_cols(dpre[tail], w_in[1]).astype(BF16)
    rows_pair, rows_own = keep_pair.shape[0], keep_own.shape[0]
    edge_count, far_count = 4 * half, keep_pair.shape[0] - 4 * half
    far = dot(one_hot_t(idx_rl[0:1], 2 * far_count), srow_grads).astype(BF16)
    for value, own, pair in (
        (far[:far_count], keep_own, keep_pair),
        (far[far_count:], send_own, send_pair),
    ):
        own[rows_own - far_count :] = value[:, :half]
        pair[rows_pair - far_count :] = value[:, half:]
    near_sum[...] = dot(one_hot_t(idx_rf[0:1], ext.shape[0]), dpre[head]).astype(BF16)
    recv_sum[...] = (
        dot(one_hot_t(idx_rf[1:2], nodes), dpre[head]) + dot(one_hot_t(idx_rl[1:2], nodes), dpre[tail])
    ).astype(BF16)
    for own, pair, columns, columns_own in (
        (send_own, send_pair, theirs, theirs_own),
        (keep_own, keep_pair, mine, mine_own),
    ):
        for out, xf, xl, hidden, cols in (
            (pair, xf_got, xl_got, hidden_theirs, slice(half, 2 * half)),
            (own, xf_own, xl_own, hidden_mine, slice(0, half)),
        ):
            grad = contract_rows(xf[...], dpre[head, columns]) + contract_rows(xl[...], dpre[tail, columns])
            out[:half] = grad.astype(BF16)
            grad = contract_rows(ext[:, cols], near_sum[:, columns]) + contract_rows(srow_l[:, cols], dpre[tail, columns])
            out[half : 2 * half] = grad.astype(BF16)
            grad = contract_rows(ext[HALO : HALO + nodes, cols], recv_sum[:, columns])
            out[2 * half : 3 * half] = grad.astype(BF16)
            grad = contract_rows(act_f[:, hidden], dy[head, columns_own]) + contract_rows(act_l[:, hidden], dy[tail, columns_own])
            out[3 * half : 4 * half] = grad.astype(BF16)
        own[4 * half : 5 * half] = contract_rows(n_own[...], ndpre[:, columns]).astype(BF16)
        own[5 * half : 6 * half] = contract_rows(agg[:, :half], ndpre[:, columns]).astype(BF16)
        own[6 * half : 7 * half] = contract_rows(nact[:, hidden_mine], ndy[:, columns_own]).astype(BF16)


def inputs_kernel(info, dpre, gf_own, gl_own, g_got, near_sum, recv_sum, w_in,
                  grads_own, grads_sent, rim_own, rim_sent):
    half = g_got.shape[1]
    fine, longs = gf_own.shape[0], gl_own.shape[0]
    nodes = recv_sum.shape[0]
    for start, rows, own in ((0, fine, gf_own), (fine, longs, gl_own)):
        part = pl.ds(start, rows)
        change = contract_cols(dpre[part], w_in[0])
        grads_own[part] = (own[...].astype(F32) + change[:, :half]).astype(BF16)
        grads_sent[part] = (g_got[part].astype(F32) + change[:, half:]).astype(BF16)
    near = contract_cols(near_sum[...], w_in[1])
    received = contract_cols(recv_sum[...], w_in[2])
    for rows, value in (
        (slice(0, HALO), near[:HALO]),
        (slice(HALO, HALO + nodes), near[HALO : HALO + nodes] + received),
        (slice(HALO + nodes, 2 * HALO + nodes), near[HALO + nodes :]),
    ):
        rim_own[rows] = value[:, :half]
        rim_sent[rows] = value[:, half:].astype(BF16)


def body(
    node_latents,
    edge_latents,
    senders,
    receivers,
    long_count,
    edge_inner,
    edge_outer,
    node_inner,
    node_outer,
    node_cotangent,
    edge_cotangent,
):
    nodes, half = node_latents.shape
    full = 2 * half
    edges = edge_latents.shape[0]
    rows = edges // 2
    fine, longs = FINE // 2, (edges - FINE) // 2
    quarter = half // 2
    patches = lax.axis_size("patch")
    chips = patches // 2
    extent = nodes + 2 * HALO
    lat = lax.axis_index("lat")
    patch = lax.axis_index("patch")
    core = patch % 2
    first_node = patch * nodes
    info = jnp.stack([lat, core]).astype(I32)

    x_hbm, g_hbm = pinned(edge_latents), pinned(edge_cotangent)
    n_hbm, ng_hbm = pinned(node_latents), pinned(node_cotangent)
    wi_hbm, wo_hbm = pinned(edge_inner), pinned(edge_outer)
    ni_hbm, no_hbm = pinned(node_inner), pinned(node_outer)

    def rows_of(value):
        return (
            lax.dynamic_slice_in_dim(value, lat * fine, fine, 0),
            lax.dynamic_slice_in_dim(value, FINE + lat * longs, longs, 0),
        )

    near_ids, far_ids = rows_of(senders.reshape(edges))
    recv_f, recv_l = rows_of(receivers.reshape(edges))
    near = (near_ids - first_node + HALO) % (nodes * patches)
    far_patch, far_row = far_ids // nodes, far_ids % nodes
    is_same = far_patch % 2 == core
    far_slot = jnp.where(is_same, 0, chips * COARSE) + far_patch // 2 * COARSE + far_row
    live = (jnp.arange(longs, dtype=I32) + lat * longs < long_count[0]).astype(I32)
    idx_rf = jnp.stack([near, recv_f - first_node])
    idx_rl = jnp.stack([far_slot, recv_l - first_node, live])
    idx_cf, idx_cl = idx_rf.T, idx_rl.T

    fine_other = block((fine, half), lambda i, s: (1 - s[0], 0))
    long_other = block((longs, half), lambda i, s: (FINE // longs + 1 - s[0], 0))
    quarter_rows = block((quarter, full), lambda i, s: (s[1], 0))
    sent_x, sent_n, sent_we = call(
        pack_kernel,
        info,
        (x_hbm, x_hbm, n_hbm, ng_hbm, wi_hbm, wo_hbm),
        [
            fine_other, long_other, whole((nodes, half)), whole((nodes, half)),
            block((3, quarter, full), lambda i, s: (0, s[1], 0)), quarter_rows,
        ],
        [((rows, half), BF16), ((2 * nodes, half), BF16), ((4, quarter, full), BF16)],
        moved=3_000_000,
        name="pack",
    )
    node_got = swap_lat(sent_n)
    we_got = other_neighbour(sent_we)
    x_got = swap_lat(sent_x)
    (sent_coarse,) = call(
        coarse_kernel,
        info,
        (n_hbm, node_got, idx_cf, idx_cl),
        [whole((16, half)), whole((16, half)), whole((fine, 2)), whole((longs, 3))],
        [((chips, COARSE, full), BF16)],
        moved=600_000,
        name="coarse_rows",
    )
    far_rows = chips * COARSE
    same = chips_all_to_all(sent_coarse)
    other = swap_core(same).reshape(far_rows, full)
    same = same.reshape(far_rows, full)
    low = shifted(
        jnp.concatenate([node_latents[nodes - HALO :], node_got[nodes - HALO : nodes]], 1), 1
    )
    high = shifted(jnp.concatenate([node_latents[:HALO], node_got[:HALO]], 1), -1)
    we_again = swap_core(we_got)

    got_spec = [whole((4, quarter, full))] * 2
    w_in, w_out, sent_g, sent_wn = call(
        edge_weights_kernel,
        info,
        (wi_hbm, wo_hbm, we_got, we_again, g_hbm, g_hbm, ni_hbm, no_hbm, x_got),
        [whole((3, half, full)), whole((half, full))] + got_spec + [
            fine_other, long_other, block((2, quarter, full), lambda i, s: (0, s[1], 0)), quarter_rows,
            pl.BlockSpec(memory_space=pl.ANY),
        ],
        [((3, full, full), BF16), ((full, full), BF16), ((rows, half), BF16), ((3, quarter, full), BF16)],
        moved=7_000_000,
        name="edge_weights",
    )
    wn_got = other_neighbour(sent_wn)
    wn_again = swap_core(wn_got)
    g_got = swap_lat(sent_g)
    nin, nout = call(
        weights_kernel,
        info,
        (ni_hbm, no_hbm, wn_got, wn_again),
        [whole((2, half, full)), whole((half, full)), whole((3, quarter, full)), whole((3, quarter, full))],
        [((2, full, full), BF16), ((full, full), BF16)],
        moved=3_000_000,
        name="node_weights",
    )

    def fine_own():
        return block((fine, half), lambda i, s: (s[0], 0))

    def long_own():
        return block((longs, half), lambda i, s: (FINE // longs + s[0], 0))

    def fine_got():
        return whole((fine, half))

    def long_got():
        return block((longs, half), lambda i, s: (fine // longs, 0))

    node_spec = whole((nodes, half))
    second_nodes = block((nodes, half), lambda i, s: (1, 0))
    rim = whole((HALO, full))
    win_spec, wout_spec = whole((3, full, full)), whole((full, full))

    def forward_outs(count, reach):
        return [
            ((count, full), F32),
            ((count, full), BF16),
            ((count, full), F32),
            ((count, 1), F32),
            ((count, half), BF16),
            ((count, half), BF16),
            ((reach, full), F32),
            ((reach, full), BF16),
        ]

    slope_f, act_f, normed_f, inverse_f, fine_out, fine_sent, partial_f, partial_f_sent = call(
        fine_kernel,
        info,
        (x_hbm, x_got, n_hbm, node_got, low, high, idx_cf, idx_rf, w_in, w_out),
        [
            fine_own(), fine_got(), node_spec, whole((nodes, half)), rim, rim,
            whole((fine, 2)), whole((2, fine)), win_spec, wout_spec,
        ],
        forward_outs(fine, nodes),
        [pltpu.VMEM((extent, full), BF16), pltpu.VMEM((fine, full), BF16)],
        flops=2 * fine * full * (4 * full + extent + 2 * nodes),
        moved=8_000_000,
        name="edges_forward_fine",
    )
    slope_l, act_l, normed_l, inverse_l, long_out, long_sent, partial_l, partial_l_sent, srow_l = call(
        long_kernel,
        info,
        (x_hbm, x_got, n_hbm, node_got, pinned(same), pinned(other), idx_cl, idx_rl, w_in, w_out),
        [
            long_own(), long_got(), whole((16, half)), whole((16, half)),
            whole((far_rows, full)), whole((far_rows, full)),
            whole((longs, 3)), whole((3, longs)), win_spec, wout_spec,
        ],
        forward_outs(longs, 16) + [((longs, full), BF16)],
        [pltpu.VMEM((longs, full), BF16)],
        flops=2 * longs * full * (4 * full + 4 * patches * COARSE + 2 * nodes),
        moved=6_000_000,
        name="edges_forward_long",
    )
    partial_f_got = swap_lat(partial_f_sent)
    partial_l_got = swap_lat(partial_l_sent)

    edge_out_got = swap_lat(jnp.concatenate([fine_sent, long_sent], 0))
    rows_pair, rows_own = 4 * half + far_rows, 7 * half + far_rows

    (node_output, node_self, keep_own, send_own, keep_pair, send_pair, dpre, near_sum, recv_sum) = call(
        back_kernel,
        info,
        (partial_f, partial_f_got, partial_l, partial_l_got, n_hbm, node_got, ng_hbm, node_got, low, high, nin, nout,
         x_hbm, x_hbm, x_got, x_got, g_hbm, g_hbm, g_got, g_got,
         slope_f, slope_l, act_f, act_l, normed_f, normed_l, inverse_f, inverse_l, srow_l,
         idx_cf, idx_cl, idx_rf, idx_rl, w_in, w_out),
        [
            whole((nodes, full)), whole((nodes, full)), whole((16, full)), whole((16, full)),
            node_spec, whole((nodes, half)), node_spec, second_nodes,
            rim, rim, whole((2, full, full)), wout_spec,
            fine_own(), long_own(), fine_got(), long_got(), fine_own(), long_own(), fine_got(), long_got(),
            whole((fine, full)), whole((longs, full)), whole((fine, full)), whole((longs, full)),
            whole((fine, full)), whole((longs, full)), whole((fine, 1)), whole((longs, 1)),
            whole((longs, full)),
            whole((fine, 2)), whole((longs, 3)), whole((2, fine)), whole((3, longs)), win_spec, wout_spec,
        ],
        [
            ((nodes, half), BF16),
            ((nodes, half), F32),
            ((rows_own, half), BF16),
            ((rows_own, half), BF16),
            ((rows_pair, half), BF16),
            ((rows_pair, half), BF16),
            ((rows, full), BF16),
            ((extent, full), BF16),
            ((nodes, full), BF16),
        ],
        [
            pltpu.VMEM((nodes, full), BF16),
            pltpu.VMEM((nodes, full), BF16),
            pltpu.VMEM((nodes, full), BF16),
            pltpu.VMEM((nodes, full), BF16),
            pltpu.VMEM((rows, full), BF16),
            pltpu.VMEM((extent, full), BF16),
        ],
        flops=8 * rows * full * full,
        moved=14_000_000,
        name="nodes_and_edges_backward",
    )

    core_pair, core_own = swap_core(send_pair), swap_core(send_own)
    by_lat, by_other = call(
        lat_stage_kernel,
        info,
        (keep_pair, core_pair),
        [whole((rows_pair, half)), whole((rows_pair, half))],
        [((rows_pair // 2, half), BF16), ((rows_pair // 2, half), BF16)],
        moved=2_400_000,
        name="lat_stage",
    )
    blocks = half // LANES
    total_rows = 7 * half * blocks
    share = total_rows // chips
    slot = share + blocks * COARSE
    (gathered,) = call(
        combine_kernel,
        info,
        (keep_own, core_own, swap_lat(by_lat), other_neighbour(by_other)),
        [whole((rows_own, half)), whole((rows_own, half)), whole((rows_pair // 2, half)), whole((rows_pair // 2, half))],
        [((chips, slot, LANES), BF16)],
        moved=4_300_000,
        name="combine",
    )
    arrived = chips_all_to_all(gathered)

    grads_own, grads_sent, rim_own, rim_sent = call(
        inputs_kernel,
        info,
        (dpre, g_hbm, g_hbm, g_got, near_sum, recv_sum, w_in),
        [
            whole((rows, full)), fine_own(), long_own(), whole((rows, half)),
            whole((extent, full)), whole((nodes, full)), win_spec,
        ],
        [((rows, half), BF16), ((rows, half), BF16), ((extent, half), F32), ((extent, half), BF16)],
        flops=4 * rows * full * full,
        moved=5_000_000,
        name="input_gradients",
    )

    (edge_output,) = call(
        rows_kernel,
        info,
        (fine_out, long_out, edge_out_got),
        [whole((fine, half)), whole((longs, half)), whole((rows, half))],
        [((edges, half), BF16)],
        moved=1_600_000,
        name="edge_output_rows",
    )
    (edge_grads,) = call(
        rows_kernel,
        info,
        (grads_own, grads_own, swap_lat(grads_sent)),
        [whole((fine, half)), block((longs, half), lambda i, s: (fine // longs, 0)), whole((rows, half))],
        [((edges, half), BF16)],
        moved=1_600_000,
        name="edge_gradient_rows",
    )
    summed = rim_own + swap_lat(rim_sent).astype(F32)
    to_low = shifted(summed[:HALO].astype(BF16), -1).astype(F32)
    to_high = shifted(summed[HALO + nodes :].astype(BF16), 1).astype(F32)

    weight_share, coarse_total = call(
        functools.partial(share_kernel, scale=1.0 / patches),
        info,
        (arrived, edge_output, edge_grads, to_low, to_high),
        [whole((chips, slot, LANES))] + [pl.BlockSpec(memory_space=pl.ANY)] * 4,
        [((chips, share, LANES), BF16), ((blocks * COARSE, LANES), F32)],
        moved=2_200_000,
        name="share",
    )
    coarse_share = jnp.concatenate(
        [coarse_total[i * COARSE : (i + 1) * COARSE] for i in range(blocks)], 1
    )
    own_grads = node_self + summed[HALO : HALO + nodes]
    own_grads = own_grads.at[nodes - HALO :].add(to_low)
    own_grads = own_grads.at[:HALO].add(to_high)
    own_grads = own_grads.at[:COARSE].add(coarse_share)
    node_grads = own_grads.astype(BF16)
    mine = chips_all_to_all(weight_share)
    mine = mine.reshape(blocks, total_rows // blocks, LANES)
    other = swap_core(mine)
    square = (half, full)
    weights = pl.pallas_call(
        results_kernel,
        grid_spec=pltpu.PrefetchScalarGridSpec(
            num_scalar_prefetch=1,
            grid=(1,),
            in_specs=[whole(mine.shape)] * 2,
            out_specs=[pl.BlockSpec(memory_space=pl.ANY)] * 4,
            scratch_shapes=[pltpu.VMEM((7,) + square, F32), pltpu.SemaphoreType.DMA((7,))],
        ),
        out_shape=[jax.ShapeDtypeStruct(shape, F32) for shape in ((3,) + square, square, (2,) + square, square)],
        compiler_params=pltpu.CompilerParams(vmem_limit_bytes=VMEM_LIMIT),
        cost_estimate=pl.CostEstimate(flops=0, bytes_accessed=6_000_000, transcendentals=0),
        name="results",
    )(info, mine, other)
    return (edge_output, node_output, edge_grads, node_grads, *weights)


def solution(mesh):
    placed = (
        P("patch", "lat"),
        P("patch", "lat"),
        P("patch", None),
        P("patch", None),
        P("patch"),
        P(None, "lat", None),
        P("lat", None),
        P(None, "lat", None),
        P("lat", None),
        P("patch", "lat"),
        P("patch", "lat"),
    )
    return jax.shard_map(
        body,
        mesh=mesh,
        in_specs=placed,
        out_specs=(
            P("patch", "lat"),
            P("patch", "lat"),
            P("patch", "lat"),
            P("patch", "lat"),
            P(None, "lat", None),
            P("lat", None),
            P(None, "lat", None),
            P("lat", None),
        ),
        check_vma=False,
    )
```

```python
import functools

import jax
import jax.numpy as jnp
from jax import lax
from jax.experimental import pallas as pl
from jax.experimental.pallas import tpu as pltpu
from jax.sharding import PartitionSpec as P

HALO = 32
COARSE = 8
FINE = 1152
EPSILON = 1e-05
F32 = jnp.float32
BF16 = jnp.bfloat16
I32 = jnp.int32
LANES = 128
MIB = 1024 * 1024


def dot(left, right):
    return jnp.dot(left, right, preferred_element_type=F32)


def contract_rows(left, right):
    return lax.dot_general(left, right, (((0,), (0,)), ((), ())), preferred_element_type=F32)


def contract_cols(left, right):
    return lax.dot_general(left, right, (((1,), (1,)), ((), ())), preferred_element_type=F32)


def layer_norm(values):
    centered = values - jnp.mean(values, axis=1, keepdims=True)
    inverse = lax.rsqrt(jnp.mean(centered * centered, axis=1, keepdims=True) + EPSILON)
    return centered * inverse, inverse


def norm_backward(cotangent, normed, inverse):
    mean = jnp.mean(cotangent, axis=1, keepdims=True)
    crossed = jnp.mean(cotangent * normed, axis=1, keepdims=True)
    return (cotangent - mean - normed * crossed) * inverse


def swish_parts(values):
    sigmoid = jax.nn.sigmoid(values)
    return values * sigmoid, sigmoid * (1.0 + values * (1.0 - sigmoid))


def one_hot(index, width):
    return (index == lax.broadcasted_iota(I32, (index.shape[0], width), 1)).astype(F32).astype(BF16)


def one_hot_t(index, width):
    return (index == lax.broadcasted_iota(I32, (width, index.shape[1]), 0)).astype(F32).astype(BF16)


def swap_lat(value):
    return lax.ppermute(value, "lat", [(0, 1), (1, 0)])


def swap_core(value):
    count = lax.axis_size("patch")
    return lax.ppermute(value, "patch", [(i, i ^ 1) for i in range(count)])


def shifted(value, steps):
    count = lax.axis_size("patch")
    return lax.ppermute(value, "patch", [(i, (i + steps) % count) for i in range(count)])


def other_neighbour(value):
    count = lax.axis_size("patch")
    pairs = []
    for patch in range(count):
        for lat in range(2):
            pairs.append((patch * 2 + lat, (patch ^ 2) * 2 + (1 - lat)))
    return lax.ppermute(value, ("patch", "lat"), pairs)


def chips_all_to_all(value):
    count = lax.axis_size("patch")
    groups = [list(range(core, count, 2)) for core in range(2)]
    return lax.all_to_all(value, "patch", 0, 0, tiled=True, axis_index_groups=groups)


def whole(shape):
    return pl.BlockSpec(shape, lambda i, s: (0,) * len(shape), pipeline_mode=pl.Buffered(1))


def block(shape, index):
    return pl.BlockSpec(shape, index, pipeline_mode=pl.Buffered(1))


def call(kernel, info, operands, in_specs, outs, scratch=(), flops=0, moved=0, name=None, in_hbm=(), limit=14):
    return pl.pallas_call(
        kernel,
        grid_spec=pltpu.PrefetchScalarGridSpec(
            num_scalar_prefetch=1,
            grid=(1,),
            in_specs=in_specs,
            out_specs=[
                pl.BlockSpec(memory_space=pltpu.HBM) if i in in_hbm else whole(shape)
                for i, (shape, _) in enumerate(outs)
            ],
            scratch_shapes=list(scratch),
        ),
        out_shape=[jax.ShapeDtypeStruct(shape, dtype) for shape, dtype in outs],
        compiler_params=pltpu.CompilerParams(vmem_limit_bytes=limit * MIB),
        cost_estimate=pl.CostEstimate(flops=flops, bytes_accessed=moved, transcendentals=0),
        name=name,
    )(info, *operands)


def pinned(value):
    return pltpu.with_memory_space_constraint(value, pltpu.HBM)


def pack_kernel(info, xf, xl, n, wi, wo, xs, wes, low, high):
    fine = xf.shape[0]
    low[...] = n[:HALO]
    high[...] = n[n.shape[0] - HALO :]
    wes[:3] = wi[...]
    wes[3] = wo[...]
    xs[:fine] = xf[...]
    xs[fine : fine + xl.shape[0]] = xl[...]
    xs[fine + xl.shape[0] :] = n[...]


def coarse_kernel(info, n_own, n_got, after, out, staged, sem):
    half = n_own.shape[1]
    for columns, n in ((slice(0, half), n_own), (slice(half, 2 * half), n_got)):
        staged[:, :, columns] = jnp.broadcast_to(n[:COARSE][None], (staged.shape[0], COARSE, half))
    copy = pltpu.make_async_copy(staged, out, sem)
    copy.start()
    copy.wait()


def gate_kernel(info, value, *rest):
    pass


def gated(info, value, after, space=pl.ANY):
    anywhere = pl.BlockSpec(memory_space=pl.ANY)
    return pl.pallas_call(
        gate_kernel,
        in_specs=[pl.BlockSpec(memory_space=pltpu.SMEM)] + [anywhere] + [pl.BlockSpec(memory_space=space)] * len(after),
        out_specs=anywhere,
        out_shape=jax.ShapeDtypeStruct(value.shape, value.dtype),
        input_output_aliases={1: 0},
        compiler_params=pltpu.CompilerParams(vmem_limit_bytes=MIB),
        name="gate",
    )(info, value, *after)


def lat_stage_kernel(info, keep, got, first, second):
    rows = first.shape[0]
    first[...] = (keep[:rows].astype(F32) + got[:rows].astype(F32)).astype(BF16)
    second[...] = (keep[rows:].astype(F32) + got[rows:].astype(F32)).astype(BF16)


def combine_kernel(info, keep, got, first, second, out, staged, sem):
    chips = out.shape[0]
    rows = first.shape[0]
    edge_rows_count, far_rows = 2 * rows - chips * COARSE, chips * COARSE
    half_chips = chips // 2
    total = keep[...].astype(F32) + got[...].astype(F32)
    pair = jnp.concatenate([first[...], second[...]], 0).astype(F32)
    weights = jnp.concatenate(
        [total[:edge_rows_count] + pair[:edge_rows_count], total[edge_rows_count:-far_rows]], 0
    )
    far = total[-far_rows:] + pair[edge_rows_count:]
    share = weights.shape[0] // half_chips
    parts = [weights[:, i * LANES : (i + 1) * LANES].reshape(half_chips, share, LANES) for i in range(2)]
    coarse = [far[:, i * LANES : (i + 1) * LANES].reshape(chips, COARSE, LANES) for i in range(2)]
    staged[...] = jnp.concatenate([jnp.concatenate(parts, 0)] + coarse, 1).astype(BF16)
    copy = pltpu.make_async_copy(staged, out, sem)
    copy.start()
    copy.wait()


def share_kernel(info, arrived, output, low, high, weights, coarse, taken, staged, sem, *, scale):
    share = staged.shape[1]
    copy = pltpu.make_async_copy(arrived, taken, sem)
    copy.start()
    copy.wait()
    total = jnp.sum(taken[...].astype(F32), 0)
    staged[...] = jnp.broadcast_to((total[:share] * scale).astype(BF16)[None], staged.shape)
    copy = pltpu.make_async_copy(staged, weights, sem)
    copy.start()
    coarse[...] = total[share:]
    copy.wait()


def rows_kernel(info, own_f, own_l, got, out, sems):
    lat = info[0]
    fine, longs = own_f.shape[0], own_l.shape[0]
    copies = []
    for side, f, l in (
        (lat, own_f, own_l),
        (1 - lat, got.at[pl.ds(0, fine)], got.at[pl.ds(fine, longs)]),
    ):
        copies.append((f, out.at[pl.ds(pl.multiple_of(side * fine, 64), fine)]))
        copies.append((l, out.at[pl.ds(pl.multiple_of(FINE + side * longs, 64), longs)]))
    made = [pltpu.make_async_copy(a, b, sems.at[k]) for k, (a, b) in enumerate(copies)]
    for copy in made:
        copy.start()
    for copy in made:
        copy.wait()


def results_kernel(info, mine, other, inner, outer, node_inner, node_outer, staged, sems):
    first = info[1] == 0
    blocks, half = mine.shape[0], staged.shape[1]
    targets = [inner.at[0], inner.at[1], inner.at[2], outer, node_inner.at[0], node_inner.at[1], node_outer]
    copies = []
    for k, target in enumerate(targets):
        rows = slice(k * half, (k + 1) * half)
        for i in range(blocks):
            a, b = mine[i, rows].astype(F32), other[i, rows].astype(F32)
            staged[k, :, i * LANES : (i + 1) * LANES] = jnp.where(first, a, b)
            staged[k, :, half + i * LANES : half + (i + 1) * LANES] = jnp.where(first, b, a)
        copies.append(pltpu.make_async_copy(staged.at[k], target, sems.at[k]))
        copies[-1].start()
    for copy in copies:
        copy.wait()


def edge_weights_kernel(info, wi, wo, got, again, gf, gl, ng, ni, no, after, idx_f, idx_l, full_in, full_out, gs, wns):
    fine = gf.shape[0]
    wns[:2] = ni[...]
    wns[2] = no[...]
    gs[:fine] = gf[...]
    gs[fine : fine + gl.shape[0]] = gl[...]
    gs[fine + gl.shape[0] :] = ng[...]
    weights_kernel(info, wi, wo, got, again, full_in, full_out)


def weights_kernel(info, wi, wo, got, again, full_in, full_out):
    lat, core = info[0], info[1]
    half = wo.shape[0]
    quarter = half // 2
    inner = wi.shape[0]
    first = core == 0
    for k in range(inner):
        full_in[k, :half] = wi[k]
        full_in[k, half : half + quarter] = jnp.where(first, got[k], again[k])
        full_in[k, half + quarter :] = jnp.where(first, again[k], got[k])
    own = wo[...]
    top = jnp.where(first, got[inner], again[inner])
    bottom = jnp.where(first, again[inner], got[inner])
    missing = jnp.concatenate([top, bottom], 0)
    low = lat == 0
    for rows, value in ((slice(0, half), jnp.where(low, own, missing)), (slice(half, 2 * half), jnp.where(low, missing, own))):
        full_out[rows, :half] = jnp.where(low, value[:, :half], value[:, half:])
        full_out[rows, half:] = jnp.where(low, value[:, half:], value[:, :half])


def edge_rows(x, sender, receiver, mask, w_in, w_out, rows, half, slope, act, normed, inverse, out_own, out_sent, update):
    pre = dot(x, w_in[0]) + dot(sender, w_in[1]) + dot(receiver, w_in[2])
    value, derivative = swish_parts(pre)
    value = value.astype(BF16)
    slope[rows] = derivative
    act[rows] = value
    scaled, scale = layer_norm(dot(value, w_out[...]))
    normed[rows] = scaled
    inverse[rows] = scale
    change = scaled if mask is None else scaled * mask
    out = (x.astype(F32) + change).astype(BF16)
    out_own[rows] = out[:, :half]
    out_sent[rows] = out[:, half:]
    update[rows] = change.astype(BF16)


def fine_kernel(info, x_own, x_got, n_own, n_got, low, high, rims_got, idx_c, idx_r, w_in, w_out,
                slope, act, normed, inverse, out_own, out_sent, partial, sent, ext, update):
    half = x_own.shape[1]
    nodes = n_own.shape[0]
    ext[:HALO, :half] = low[...]
    ext[:HALO, half:] = rims_got[:HALO]
    ext[HALO : HALO + nodes, :half] = n_own[...]
    ext[HALO : HALO + nodes, half:] = n_got[...]
    ext[HALO + nodes :, :half] = high[...]
    ext[HALO + nodes :, half:] = rims_got[HALO:]
    node_x = ext[HALO : HALO + nodes]
    chunk = 192
    for start in range(0, x_own.shape[0], chunk):
        rows = pl.ds(start, chunk)
        x = jnp.concatenate([x_own[rows], x_got[rows]], 1)
        sender = dot(one_hot(idx_c[rows, 0:1], ext.shape[0]), ext[...]).astype(BF16)
        receiver = dot(one_hot(idx_c[rows, 1:2], nodes), node_x).astype(BF16)
        edge_rows(x, sender, receiver, None, w_in, w_out, rows, half, slope, act, normed, inverse, out_own, out_sent, update)
    total = dot(one_hot_t(idx_r[1:2], nodes), update[...])
    partial[...] = total
    sent[...] = total.astype(BF16)


def long_kernel(info, x_own, x_got, n_own, n_got, same, other, idx_c, idx_r, w_in, w_out,
                slope, act, normed, inverse, out_own, out_sent, partial, sent, sender_rows, update):
    half = x_own.shape[1]
    rows = pl.ds(0, x_own.shape[0])
    count = same.shape[0]
    value = dot(one_hot(idx_c[:, 0:1], count), same[...])
    value = value + dot(one_hot(idx_c[:, 0:1] - count, count), other[...])
    sender_rows[...] = value.astype(BF16)
    x = jnp.concatenate([x_own[...], x_got[...]], 1)
    near = n_own.shape[0]
    node_x = jnp.concatenate([n_own[...], n_got[...]], 1)
    receiver = dot(one_hot(idx_c[:, 1:2], near), node_x).astype(BF16)
    edge_rows(x, sender_rows[...], receiver, idx_c[:, 2:3].astype(F32), w_in, w_out, rows, half, slope, act, normed, inverse, out_own, out_sent, update)
    total = dot(one_hot_t(idx_r[1:2], near), update[...])
    partial[...] = total
    sent[...] = total.astype(BF16)


def column_halves(info, half):
    lat, core = info[0], info[1]
    turn = (core + lat) % 2

    def at(which):
        return pl.ds(pl.multiple_of(which * half, half), half)

    return at(core), at(1 - core), at(turn), at(1 - turn), at(lat), at(1 - lat)


def edge_weight_grads(outs, xf, xl, node_x, extended, srow, cols, act_f, act_l, hidden, dpre, dy, near_sum, recv_sum, fine):
    half = xf.shape[1]
    head, tail = pl.ds(0, fine), pl.ds(fine, dpre.shape[0] - fine)
    for out, columns, columns_own in outs:
        grad = contract_rows(xf[...], dpre[head, columns]) + contract_rows(xl[...], dpre[tail, columns])
        out[:half] = grad.astype(BF16)
        grad = contract_rows(extended, near_sum[:, columns]) + contract_rows(srow[:, cols], dpre[tail, columns])
        out[half : 2 * half] = grad.astype(BF16)
        out[2 * half : 3 * half] = contract_rows(node_x, recv_sum[:, columns]).astype(BF16)
        grad = contract_rows(act_f[:, hidden], dy[head, columns_own]) + contract_rows(act_l[:, hidden], dy[tail, columns_own])
        out[3 * half : 4 * half] = grad.astype(BF16)


def far_sums(idx_r, dpre_long, weights, keep, send, count):
    grads = contract_cols(dpre_long, weights).astype(BF16)
    far = dot(one_hot_t(idx_r[0:1], 2 * count), grads).astype(BF16)
    keep[keep.shape[0] - count :] = far[:count]
    send[send.shape[0] - count :] = far[count:]


def back_kernel(info, partial, got, partial_l, got_l, n_own, n_got, ng_own, ng_got, low, high, rims_got, nin, nout,
                xf_own, xl_own, xf_got, xl_got, gf_own, gl_own, gf_got, gl_got,
                slope_f, slope_l, act_f, act_l, normed_f, normed_l, inverse_f, inverse_l, srow_l,
                idx_cf, idx_cl, idx_rf, idx_rl, w_in, w_out,
                node_out, node_self, keep_pair, send_pair, keep_own, send_own, dpre, near_sum, recv_sum,
                dy, ndpre, ndy, nact, agg_own, agg_grad, ext, ext_own):
    mine, theirs, mine_own, theirs_own, hidden_mine, hidden_theirs = column_halves(info, n_own.shape[1])
    half = n_own.shape[1]
    nodes = n_own.shape[0]
    fine, longs = xf_got.shape[0], xl_got.shape[0]
    far_count = keep_pair.shape[0] - 4 * half

    ext[:HALO] = rims_got[:HALO]
    ext[HALO : HALO + nodes] = n_got[...]
    ext[HALO + nodes :] = rims_got[HALO:]
    node_x = jnp.concatenate([n_own[...], n_got[...]], 1)
    received, received_l = got[...].astype(F32), got_l[...].astype(F32)
    total = partial[...] + jnp.concatenate([received[:, half:], received[:, :half]], 1)
    coarse = partial_l[...] + jnp.concatenate([received_l[:, half:], received_l[:, :half]], 1)
    near = coarse.shape[0]
    agg = jnp.concatenate([total[:near] + coarse, total[near:]], 0).astype(BF16)
    agg_own[...] = agg[:, :half]
    node_value, node_slope = swish_parts(dot(node_x, nin[0]) + dot(agg, nin[1]))
    nact[...] = node_value.astype(BF16)
    node_normed, node_inverse = layer_norm(dot(nact[...], nout[...]))
    node_out[...] = (n_own[...].astype(F32) + node_normed[:, :half]).astype(BF16)
    node_g = jnp.concatenate([ng_own[...], ng_got[...]], 1).astype(F32)
    ndy[...] = norm_backward(node_g, node_normed, node_inverse).astype(BF16)
    ndpre[...] = (contract_cols(ndy[...], nout[...]) * node_slope).astype(BF16)
    agg_grad[...] = contract_cols(ndpre[...], nin[1]).astype(BF16)
    node_self[...] = ng_own[...].astype(F32) + contract_cols(ndpre[...], nin[0, :half])

    chunk = 192
    for start in range(0, fine + longs, chunk):
        rows = pl.ds(start, chunk)
        if start < fine:
            part = pl.ds(start, chunk)
            idx_c = idx_cf
            g_own, g_got, normed, inverse, slope = gf_own, gf_got, normed_f, inverse_f, slope_f
        else:
            part = pl.ds(start - fine, chunk)
            idx_c = idx_cl
            g_own, g_got, normed, inverse, slope = gl_own, gl_got, normed_l, inverse_l, slope_l
        cotangent = jnp.concatenate([g_own[part], g_got[part]], 1).astype(F32)
        cotangent = cotangent + dot(one_hot(idx_c[part, 1:2], nodes), agg_grad[...])
        if start >= fine:
            cotangent = cotangent * idx_cl[part, 2:3].astype(F32)
        dy[rows] = norm_backward(cotangent, normed[part], inverse[part]).astype(BF16)
        dpre[rows] = (contract_cols(dy[rows], w_out[...]) * slope[part]).astype(BF16)

    tail = pl.ds(fine, longs)
    head = pl.ds(0, fine)
    near_sum[...] = dot(one_hot_t(idx_rf[0:1], ext.shape[0]), dpre[head]).astype(BF16)
    recv_sum[...] = (
        dot(one_hot_t(idx_rf[1:2], nodes), dpre[head]) + dot(one_hot_t(idx_rl[1:2], nodes), dpre[tail])
    ).astype(BF16)
    far_sums(idx_rl, dpre[tail], w_in[1, half:], keep_pair, send_pair, far_count)
    edge_weight_grads(
        ((send_pair, theirs, theirs_own), (keep_pair, mine, mine_own)),
        xf_got, xl_got, n_got[...], ext[...], srow_l, slice(half, 2 * half), act_f, act_l, hidden_theirs,
        dpre, dy, near_sum, recv_sum, fine,
    )
    ext_own[:HALO] = low[...]
    ext_own[HALO : HALO + nodes] = n_own[...]
    ext_own[HALO + nodes :] = high[...]
    for own, columns, columns_own in ((send_own, theirs, theirs_own), (keep_own, mine, mine_own)):
        own[4 * half : 5 * half] = contract_rows(n_own[...], ndpre[:, columns]).astype(BF16)
        own[5 * half : 6 * half] = contract_rows(agg_own[...], ndpre[:, columns]).astype(BF16)
        own[6 * half : 7 * half] = contract_rows(nact[:, hidden_mine], ndy[:, columns_own]).astype(BF16)
    far_sums(idx_rl, dpre[tail], w_in[1, :half], keep_own, send_own, far_count)
    edge_weight_grads(
        ((send_own, theirs, theirs_own), (keep_own, mine, mine_own)),
        xf_own, xl_own, n_own[...], ext_own[...], srow_l, slice(0, half), act_f, act_l, hidden_mine,
        dpre, dy, near_sum, recv_sum, fine,
    )


def inputs_kernel(info, dpre, gf_own, gl_own, g_got, near_sum, recv_sum, w_in,
                  grads_own, grads_sent, rim_own, rim_sent):
    half = g_got.shape[1]
    fine, longs = gf_own.shape[0], gl_own.shape[0]
    nodes = recv_sum.shape[0]
    for start, rows, own in ((0, fine, gf_own), (fine, longs, gl_own)):
        part = pl.ds(start, rows)
        change = contract_cols(dpre[part], w_in[0])
        grads_own[part] = (own[...].astype(F32) + change[:, :half]).astype(BF16)
        grads_sent[part] = (g_got[part].astype(F32) + change[:, half:]).astype(BF16)
    near = contract_cols(near_sum[...], w_in[1])
    received = contract_cols(recv_sum[...], w_in[2])
    for rows, value in (
        (slice(0, HALO), near[:HALO]),
        (slice(HALO, HALO + nodes), near[HALO : HALO + nodes] + received),
        (slice(HALO + nodes, 2 * HALO + nodes), near[HALO + nodes :]),
    ):
        rim_own[rows] = value[:, :half]
        rim_sent[rows] = value[:, half:].astype(BF16)


def body(
    node_latents,
    edge_latents,
    senders,
    receivers,
    long_count,
    edge_inner,
    edge_outer,
    node_inner,
    node_outer,
    node_cotangent,
    edge_cotangent,
):
    nodes, half = node_latents.shape
    full = 2 * half
    edges = edge_latents.shape[0]
    rows = edges // 2
    fine, longs = FINE // 2, (edges - FINE) // 2
    quarter = half // 2
    patches = lax.axis_size("patch")
    chips = patches // 2
    extent = nodes + 2 * HALO
    lat = lax.axis_index("lat")
    patch = lax.axis_index("patch")
    core = patch % 2
    first_node = patch * nodes
    info = jnp.stack([lat, core]).astype(I32)

    x_hbm, g_hbm = pinned(edge_latents), pinned(edge_cotangent)
    n_hbm, ng_hbm = pinned(node_latents), pinned(node_cotangent)
    wi_hbm, wo_hbm = pinned(edge_inner), pinned(edge_outer)
    ni_hbm, no_hbm = pinned(node_inner), pinned(node_outer)

    def rows_of(value):
        return (
            lax.dynamic_slice_in_dim(value, lat * fine, fine, 0),
            lax.dynamic_slice_in_dim(value, FINE + lat * longs, longs, 0),
        )

    near_ids, far_ids = rows_of(senders.reshape(edges))
    recv_f, recv_l = rows_of(receivers.reshape(edges))
    near = (near_ids - first_node + HALO) % (nodes * patches)
    far_patch, far_row = far_ids // nodes, far_ids % nodes
    is_same = far_patch % 2 == core
    far_slot = jnp.where(is_same, 0, chips * COARSE) + far_patch // 2 * COARSE + far_row
    live = (jnp.arange(longs, dtype=I32) + lat * longs < long_count[0]).astype(I32)
    idx_rf = jnp.stack([near, recv_f - first_node])
    idx_rl = jnp.stack([far_slot, recv_l - first_node, live])
    idx_cf, idx_cl = idx_rf.T, idx_rl.T

    fine_other = block((fine, half), lambda i, s: (1 - s[0], 0))
    long_other = block((longs, half), lambda i, s: (FINE // longs + 1 - s[0], 0))
    quarter_rows = block((quarter, full), lambda i, s: (s[1], 0))
    sent_x, sent_we, rim_low, rim_high = call(
        pack_kernel,
        info,
        (x_hbm, x_hbm, n_hbm, wi_hbm, wo_hbm),
        [
            fine_other, long_other, whole((nodes, half)),
            block((3, quarter, full), lambda i, s: (0, s[1], 0)), quarter_rows,
        ],
        [((rows + nodes, half), BF16), ((4, quarter, full), BF16), ((HALO, half), BF16), ((HALO, half), BF16)],
        moved=3_000_000,
        name="pack",
    )
    we_got = other_neighbour(sent_we)
    x_got = pinned(swap_lat(sent_x))
    low, high = shifted(rim_high, 1), shifted(rim_low, -1)
    far_rows = chips * COARSE
    (sent_coarse,) = call(
        coarse_kernel,
        info,
        (n_hbm, swap_lat(node_latents[:16]), rim_low),
        [whole((16, half)), whole((16, half)), pl.BlockSpec(memory_space=pl.ANY)],
        [((chips, COARSE, full), BF16)],
        [pltpu.VMEM((chips, COARSE, full), BF16), pltpu.SemaphoreType.DMA],
        moved=600_000,
        name="coarse_rows",
        in_hbm=(0,),
    )
    same = chips_all_to_all(sent_coarse)
    we_again = swap_core(we_got)
    rims_got = swap_lat(jnp.concatenate([low, high], 0))

    got_spec = [whole((4, quarter, full))] * 2
    w_in, w_out, sent_g, sent_wn = call(
        edge_weights_kernel,
        info,
        (wi_hbm, wo_hbm, pinned(we_got), pinned(we_again), g_hbm, g_hbm, ng_hbm, ni_hbm, no_hbm, rims_got, idx_cf, idx_cl),
        [whole((3, half, full)), whole((half, full))] + got_spec + [
            fine_other, long_other, whole((nodes, half)),
            block((2, quarter, full), lambda i, s: (0, s[1], 0)), quarter_rows,
            pl.BlockSpec(memory_space=pl.ANY), whole((fine, 2)), whole((longs, 3)),
        ],
        [((3, full, full), BF16), ((full, full), BF16), ((rows + nodes, half), BF16), ((3, quarter, full), BF16)],
        moved=7_000_000,
        name="edge_weights",
    )
    wn_got = other_neighbour(sent_wn)
    g_got = swap_lat(sent_g)
    def fine_own():
        return block((fine, half), lambda i, s: (s[0], 0))

    def long_own():
        return block((longs, half), lambda i, s: (FINE // longs + s[0], 0))

    def fine_got():
        return whole((fine, half))

    def long_got():
        return block((longs, half), lambda i, s: (fine // longs, 0))

    node_spec = whole((nodes, half))
    got_nodes = block((nodes, half), lambda i, s: (rows // nodes, 0))
    rim = whole((HALO, half))
    win_spec, wout_spec = whole((3, full, full)), whole((full, full))

    def forward_outs(count, reach):
        return [
            ((count, full), F32),
            ((count, full), BF16),
            ((count, full), F32),
            ((count, 1), F32),
            ((count, half), BF16),
            ((count, half), BF16),
            ((reach, full), F32),
            ((reach, full), BF16),
        ]

    slope_f, act_f, normed_f, inverse_f, fine_out, fine_sent, partial_f, partial_f_sent = call(
        fine_kernel,
        info,
        (x_hbm, x_got, n_hbm, x_got, low, high, rims_got, idx_cf, idx_rf, w_in, w_out),
        [
            fine_own(), fine_got(), node_spec, got_nodes, rim, rim, whole((2 * HALO, half)),
            whole((fine, 2)), whole((2, fine)), win_spec, wout_spec,
        ],
        forward_outs(fine, nodes),
        [pltpu.VMEM((extent, full), BF16), pltpu.VMEM((fine, full), BF16)],
        flops=2 * fine * full * (4 * full + extent + 2 * nodes),
        moved=8_000_000,
        name="edges_forward_fine",
    )
    other = swap_core(same).reshape(far_rows, full)
    same = same.reshape(far_rows, full)
    slope_l, act_l, normed_l, inverse_l, long_out, long_sent, partial_l, partial_l_sent, srow_l = call(
        long_kernel,
        info,
        (x_hbm, x_got, n_hbm, x_got, same, other, idx_cl, idx_rl, w_in, w_out),
        [
            long_own(), long_got(), whole((16, half)), block((16, half), lambda i, s: (rows // 16, 0)),
            whole((far_rows, full)), whole((far_rows, full)),
            whole((longs, 3)), whole((3, longs)), win_spec, wout_spec,
        ],
        forward_outs(longs, 16) + [((longs, full), BF16)],
        [pltpu.VMEM((longs, full), BF16)],
        flops=2 * longs * full * (4 * full + 4 * patches * COARSE + 2 * nodes),
        moved=6_000_000,
        name="edges_forward_long",
    )
    wn_got = gated(info, wn_got, (partial_l_sent, partial_f_sent))
    wn_again = swap_core(wn_got)
    nin, nout = call(
        weights_kernel,
        info,
        (ni_hbm, no_hbm, wn_got, wn_again),
        [whole((2, half, full)), whole((half, full)), whole((3, quarter, full)), whole((3, quarter, full))],
        [((2, full, full), BF16), ((full, full), BF16)],
        moved=3_000_000,
        name="node_weights",
    )
    partial_f_got = swap_lat(partial_f_sent)
    partial_l_got = swap_lat(partial_l_sent)

    edge_out_got = swap_lat(jnp.concatenate([fine_sent, long_sent], 0))
    rows_pair, rows_own = 4 * half + far_rows, 7 * half + far_rows

    node_output, node_self, keep_pair, send_pair, keep_own, send_own, dpre, near_sum, recv_sum = call(
        back_kernel,
        info,
        (partial_f, partial_f_got, partial_l, partial_l_got, n_hbm, x_got, ng_hbm, g_got, low, high, rims_got, nin, nout,
         x_hbm, x_hbm, x_got, x_got, g_hbm, g_hbm, g_got, g_got,
         slope_f, slope_l, act_f, act_l, normed_f, normed_l, inverse_f, inverse_l, srow_l,
         idx_cf, idx_cl, idx_rf, idx_rl, w_in, w_out),
        [
            whole((nodes, full)), whole((nodes, full)), whole((16, full)), whole((16, full)),
            node_spec, got_nodes, node_spec, got_nodes,
            rim, rim, whole((2 * HALO, half)), whole((2, full, full)), wout_spec,
            fine_own(), long_own(), fine_got(), long_got(), fine_own(), long_own(), fine_got(), long_got(),
            whole((fine, full)), whole((longs, full)), whole((fine, full)), whole((longs, full)),
            whole((fine, full)), whole((longs, full)), whole((fine, 1)), whole((longs, 1)),
            whole((longs, full)),
            whole((fine, 2)), whole((longs, 3)), whole((2, fine)), whole((3, longs)), win_spec, wout_spec,
        ],
        [
            ((nodes, half), BF16),
            ((nodes, half), F32),
            ((rows_pair, half), BF16),
            ((rows_pair, half), BF16),
            ((rows_own, half), BF16),
            ((rows_own, half), BF16),
            ((rows, full), BF16),
            ((extent, full), BF16),
            ((nodes, full), BF16),
        ],
        [
            pltpu.VMEM((rows, full), BF16),
            pltpu.VMEM((nodes, full), BF16),
            pltpu.VMEM((nodes, full), BF16),
            pltpu.VMEM((nodes, full), BF16),
            pltpu.VMEM((nodes, half), BF16),
            pltpu.VMEM((nodes, full), BF16),
            pltpu.VMEM((extent, half), BF16),
            pltpu.VMEM((extent, half), BF16),
        ],
        flops=8 * rows * full * full,
        moved=14_000_000,
        name="nodes_and_edges_backward",
        limit=28,
    )
    core_pair, core_own = swap_core(send_pair), swap_core(send_own)
    by_lat, by_other = call(
        lat_stage_kernel,
        info,
        (keep_pair, core_pair),
        [whole((rows_pair, half)), whole((rows_pair, half))],
        [((rows_pair // 2, half), BF16), ((rows_pair // 2, half), BF16)],
        moved=2_400_000,
        name="lat_stage",
    )
    blocks = half // LANES
    total_rows = 7 * half * blocks
    share = total_rows // chips
    slot = share + blocks * COARSE
    (gathered,) = call(
        combine_kernel,
        info,
        (keep_own, core_own, swap_lat(by_lat), other_neighbour(by_other)),
        [whole((rows_own, half)), whole((rows_own, half)), whole((rows_pair // 2, half)), whole((rows_pair // 2, half))],
        [((chips, slot, LANES), BF16)],
        [pltpu.VMEM((chips, slot, LANES), BF16), pltpu.SemaphoreType.DMA],
        moved=4_300_000,
        name="combine",
        in_hbm=(0,),
    )
    arrived = chips_all_to_all(gathered)

    grads_own, grads_sent, rim_own, rim_sent = call(
        inputs_kernel,
        info,
        (pinned(dpre), g_hbm, g_hbm, g_got, pinned(near_sum), pinned(recv_sum), w_in),
        [
            whole((rows, full)), fine_own(), long_own(), whole((rows, half)),
            whole((extent, full)), whole((nodes, full)), win_spec,
        ],
        [((rows, half), BF16), ((rows, half), BF16), ((extent, half), F32), ((extent, half), BF16)],
        flops=4 * rows * full * full,
        moved=5_000_000,
        name="input_gradients",
    )

    (edge_output,) = call(
        rows_kernel,
        info,
        (fine_out, long_out, edge_out_got),
        [whole((fine, half)), whole((longs, half)), whole((rows, half))],
        [((edges, half), BF16)],
        [pltpu.SemaphoreType.DMA((4,))],
        moved=1_600_000,
        name="edge_output_rows",
        in_hbm=(0,),
    )
    (edge_grads,) = call(
        rows_kernel,
        info,
        (grads_own, grads_own, swap_lat(grads_sent)),
        [whole((fine, half)), block((longs, half), lambda i, s: (fine // longs, 0)), whole((rows, half))],
        [((edges, half), BF16)],
        [pltpu.SemaphoreType.DMA((4,))],
        moved=1_600_000,
        name="edge_gradient_rows",
        in_hbm=(0,),
    )
    summed = rim_own + swap_lat(rim_sent).astype(F32)
    to_low = shifted(summed[:HALO].astype(BF16), -1).astype(F32)
    to_high = shifted(summed[HALO + nodes :].astype(BF16), 1).astype(F32)

    weight_share, coarse_total = call(
        functools.partial(share_kernel, scale=1.0 / patches),
        info,
        (arrived, pinned(edge_output), to_low, to_high),
        [pl.BlockSpec(memory_space=pl.ANY), pl.BlockSpec(memory_space=pltpu.HBM)]
        + [pl.BlockSpec(memory_space=pl.ANY)] * 2,
        [((chips, share, LANES), BF16), ((blocks * COARSE, LANES), F32)],
        [
            pltpu.VMEM((chips, slot, LANES), BF16),
            pltpu.VMEM((chips, share, LANES), BF16),
            pltpu.SemaphoreType.DMA,
        ],
        in_hbm=(0,),
        moved=2_200_000,
        name="share",
    )
    coarse_share = jnp.concatenate(
        [coarse_total[i * COARSE : (i + 1) * COARSE] for i in range(blocks)], 1
    )
    own_grads = node_self + summed[HALO : HALO + nodes]
    own_grads = own_grads.at[nodes - HALO :].add(to_low)
    own_grads = own_grads.at[:HALO].add(to_high)
    own_grads = own_grads.at[:COARSE].add(coarse_share)
    node_grads = own_grads.astype(BF16)
    mine = gated(info, chips_all_to_all(weight_share), (pinned(edge_grads), pinned(node_grads)), pltpu.HBM)
    mine = mine.reshape(blocks, total_rows // blocks, LANES)
    other = swap_core(mine)
    square = (half, full)
    weights = pl.pallas_call(
        results_kernel,
        grid_spec=pltpu.PrefetchScalarGridSpec(
            num_scalar_prefetch=1,
            grid=(1,),
            in_specs=[whole(mine.shape)] * 2,
            out_specs=[pl.BlockSpec(memory_space=pl.ANY)] * 4,
            scratch_shapes=[pltpu.VMEM((7,) + square, F32), pltpu.SemaphoreType.DMA((7,))],
        ),
        out_shape=[jax.ShapeDtypeStruct(shape, F32) for shape in ((3,) + square, square, (2,) + square, square)],
        compiler_params=pltpu.CompilerParams(vmem_limit_bytes=14 * MIB),
        cost_estimate=pl.CostEstimate(flops=0, bytes_accessed=6_000_000, transcendentals=0),
        name="results",
    )(info, mine, other)
    return (edge_output, node_output, edge_grads, node_grads, *weights)


def solution(mesh):
    placed = (
        P("patch", "lat"),
        P("patch", "lat"),
        P("patch", None),
        P("patch", None),
        P("patch"),
        P(None, "lat", None),
        P("lat", None),
        P(None, "lat", None),
        P("lat", None),
        P("patch", "lat"),
        P("patch", "lat"),
    )
    return jax.shard_map(
        body,
        mesh=mesh,
        in_specs=placed,
        out_specs=(
            P("patch", "lat"),
            P("patch", "lat"),
            P("patch", "lat"),
            P("patch", "lat"),
            P(None, "lat", None),
            P("lat", None),
            P(None, "lat", None),
            P("lat", None),
        ),
        check_vma=False,
    )
```

```python
import functools

import jax
import jax.numpy as jnp
from jax import lax
from jax.experimental import pallas as pl
from jax.experimental.pallas import tpu as pltpu
from jax.sharding import PartitionSpec as P

HALO = 32
COARSE = 8
FINE = 1152
EPSILON = 1e-05
F32 = jnp.float32
BF16 = jnp.bfloat16
I32 = jnp.int32
LANES = 128
MIB = 1024 * 1024


def dot(left, right):
    return jnp.dot(left, right, preferred_element_type=F32)


def contract_rows(left, right):
    return lax.dot_general(left, right, (((0,), (0,)), ((), ())), preferred_element_type=F32)


def contract_cols(left, right):
    return lax.dot_general(left, right, (((1,), (1,)), ((), ())), preferred_element_type=F32)


def layer_norm(values):
    centered = values - jnp.mean(values, axis=1, keepdims=True)
    inverse = lax.rsqrt(jnp.mean(centered * centered, axis=1, keepdims=True) + EPSILON)
    return centered * inverse, inverse


def norm_backward(cotangent, normed, inverse):
    mean = jnp.mean(cotangent, axis=1, keepdims=True)
    crossed = jnp.mean(cotangent * normed, axis=1, keepdims=True)
    return (cotangent - mean - normed * crossed) * inverse


def swish_parts(values):
    sigmoid = jax.nn.sigmoid(values)
    return values * sigmoid, sigmoid * (1.0 + values * (1.0 - sigmoid))


def one_hot(index, width):
    return (index == lax.broadcasted_iota(I32, (index.shape[0], width), 1)).astype(F32).astype(BF16)


def one_hot_t(index, width):
    return (index == lax.broadcasted_iota(I32, (width, index.shape[1]), 0)).astype(F32).astype(BF16)


def swap_lat(value):
    return lax.ppermute(value, "lat", [(0, 1), (1, 0)])


def swap_core(value):
    count = lax.axis_size("patch")
    return lax.ppermute(value, "patch", [(i, i ^ 1) for i in range(count)])


def shifted(value, steps):
    count = lax.axis_size("patch")
    return lax.ppermute(value, "patch", [(i, (i + steps) % count) for i in range(count)])


def other_neighbour(value):
    count = lax.axis_size("patch")
    pairs = []
    for patch in range(count):
        for lat in range(2):
            pairs.append((patch * 2 + lat, (patch ^ 2) * 2 + (1 - lat)))
    return lax.ppermute(value, ("patch", "lat"), pairs)


def chips_all_to_all(value):
    count = lax.axis_size("patch")
    groups = [list(range(core, count, 2)) for core in range(2)]
    return lax.all_to_all(value, "patch", 0, 0, tiled=True, axis_index_groups=groups)


def whole(shape):
    return pl.BlockSpec(shape, lambda i, s: (0,) * len(shape), pipeline_mode=pl.Buffered(1))


def block(shape, index):
    return pl.BlockSpec(shape, index, pipeline_mode=pl.Buffered(1))


def call(kernel, info, operands, in_specs, outs, scratch=(), flops=0, moved=0, name=None, in_hbm=(), limit=14):
    return pl.pallas_call(
        kernel,
        grid_spec=pltpu.PrefetchScalarGridSpec(
            num_scalar_prefetch=1,
            grid=(1,),
            in_specs=in_specs,
            out_specs=[
                pl.BlockSpec(memory_space=pltpu.HBM) if i in in_hbm else whole(shape)
                for i, (shape, _) in enumerate(outs)
            ],
            scratch_shapes=list(scratch),
        ),
        out_shape=[jax.ShapeDtypeStruct(shape, dtype) for shape, dtype in outs],
        compiler_params=pltpu.CompilerParams(vmem_limit_bytes=limit * MIB),
        cost_estimate=pl.CostEstimate(flops=flops, bytes_accessed=moved, transcendentals=0),
        name=name,
    )(info, *operands)


def pinned(value):
    return pltpu.with_memory_space_constraint(value, pltpu.HBM)


def pack_kernel(info, xf, xl, n, wi, wo, xs, wes, low, high):
    fine = xf.shape[0]
    low[...] = n[:HALO]
    high[...] = n[n.shape[0] - HALO :]
    wes[:3] = wi[...]
    wes[3] = wo[...]
    xs[:fine] = xf[...]
    xs[fine : fine + xl.shape[0]] = xl[...]
    xs[fine + xl.shape[0] :] = n[...]


def coarse_kernel(info, n_own, n_got, after, out, staged, sem):
    half = n_own.shape[1]
    for columns, n in ((slice(0, half), n_own), (slice(half, 2 * half), n_got)):
        staged[:, :, columns] = jnp.broadcast_to(n[:COARSE][None], (staged.shape[0], COARSE, half))
    copy = pltpu.make_async_copy(staged, out, sem)
    copy.start()
    copy.wait()


def gate_kernel(info, value, *rest):
    pass


def gated(info, value, after, space=pl.ANY):
    anywhere = pl.BlockSpec(memory_space=pl.ANY)
    return pl.pallas_call(
        gate_kernel,
        in_specs=[pl.BlockSpec(memory_space=pltpu.SMEM)] + [anywhere] + [pl.BlockSpec(memory_space=space)] * len(after),
        out_specs=anywhere,
        out_shape=jax.ShapeDtypeStruct(value.shape, value.dtype),
        input_output_aliases={1: 0},
        compiler_params=pltpu.CompilerParams(vmem_limit_bytes=MIB),
        name="gate",
    )(info, value, *after)


def lat_stage_kernel(info, keep, got, first, second):
    rows = first.shape[0]
    first[...] = (keep[:rows].astype(F32) + got[:rows].astype(F32)).astype(BF16)
    second[...] = (keep[rows:].astype(F32) + got[rows:].astype(F32)).astype(BF16)


def combine_kernel(info, keep, got, first, second, out, staged, sem):
    chips = out.shape[0]
    rows = first.shape[0]
    edge_rows_count, far_rows = 2 * rows - chips * COARSE, chips * COARSE
    half_chips = chips // 2
    total = keep[...].astype(F32) + got[...].astype(F32)
    pair = jnp.concatenate([first[...], second[...]], 0).astype(F32)
    weights = jnp.concatenate(
        [total[:edge_rows_count] + pair[:edge_rows_count], total[edge_rows_count:-far_rows]], 0
    )
    far = total[-far_rows:] + pair[edge_rows_count:]
    share = weights.shape[0] // half_chips
    parts = [weights[:, i * LANES : (i + 1) * LANES].reshape(half_chips, share, LANES) for i in range(2)]
    coarse = [far[:, i * LANES : (i + 1) * LANES].reshape(chips, COARSE, LANES) for i in range(2)]
    staged[...] = jnp.concatenate([jnp.concatenate(parts, 0)] + coarse, 1).astype(BF16)
    copy = pltpu.make_async_copy(staged, out, sem)
    copy.start()
    copy.wait()


def share_kernel(info, arrived, output, low, high, weights, coarse, taken, staged, sem, *, scale):
    share = staged.shape[1]
    copy = pltpu.make_async_copy(arrived, taken, sem)
    copy.start()
    copy.wait()
    total = jnp.sum(taken[...].astype(F32), 0)
    staged[...] = jnp.broadcast_to((total[:share] * scale).astype(BF16)[None], staged.shape)
    copy = pltpu.make_async_copy(staged, weights, sem)
    copy.start()
    coarse[...] = total[share:]
    copy.wait()


def rows_kernel(info, own_f, own_l, got, out, sems):
    lat = info[0]
    fine, longs = own_f.shape[0], own_l.shape[0]
    copies = []
    for side, f, l in (
        (lat, own_f, own_l),
        (1 - lat, got.at[pl.ds(0, fine)], got.at[pl.ds(fine, longs)]),
    ):
        copies.append((f, out.at[pl.ds(pl.multiple_of(side * fine, 64), fine)]))
        copies.append((l, out.at[pl.ds(pl.multiple_of(FINE + side * longs, 64), longs)]))
    made = [pltpu.make_async_copy(a, b, sems.at[k]) for k, (a, b) in enumerate(copies)]
    for copy in made:
        copy.start()
    for copy in made:
        copy.wait()


def results_kernel(info, mine, other, inner, outer, node_inner, node_outer, staged, sems):
    first = info[1] == 0
    blocks, half = mine.shape[0], staged.shape[1]
    targets = [inner.at[0], inner.at[1], inner.at[2], outer, node_inner.at[0], node_inner.at[1], node_outer]
    copies = []
    for k, target in enumerate(targets):
        rows = slice(k * half, (k + 1) * half)
        for i in range(blocks):
            a, b = mine[i, rows].astype(F32), other[i, rows].astype(F32)
            staged[k, :, i * LANES : (i + 1) * LANES] = jnp.where(first, a, b)
            staged[k, :, half + i * LANES : half + (i + 1) * LANES] = jnp.where(first, b, a)
        copies.append(pltpu.make_async_copy(staged.at[k], target, sems.at[k]))
        copies[-1].start()
    for copy in copies:
        copy.wait()


def edge_weights_kernel(info, wi, wo, got, again, gf, gl, ng, ni, no, after, idx_f, idx_l, full_in, full_out, gs, wns):
    fine = gf.shape[0]
    wns[:2] = ni[...]
    wns[2] = no[...]
    gs[:fine] = gf[...]
    gs[fine : fine + gl.shape[0]] = gl[...]
    gs[fine + gl.shape[0] :] = ng[...]
    weights_kernel(info, wi, wo, got, again, full_in, full_out)


def weights_kernel(info, wi, wo, got, again, full_in, full_out):
    lat, core = info[0], info[1]
    half = wo.shape[0]
    quarter = half // 2
    inner = wi.shape[0]
    first = core == 0
    for k in range(inner):
        full_in[k, :half] = wi[k]
        full_in[k, half : half + quarter] = jnp.where(first, got[k], again[k])
        full_in[k, half + quarter :] = jnp.where(first, again[k], got[k])
    own = wo[...]
    top = jnp.where(first, got[inner], again[inner])
    bottom = jnp.where(first, again[inner], got[inner])
    missing = jnp.concatenate([top, bottom], 0)
    low = lat == 0
    for rows, value in ((slice(0, half), jnp.where(low, own, missing)), (slice(half, 2 * half), jnp.where(low, missing, own))):
        full_out[rows, :half] = jnp.where(low, value[:, :half], value[:, half:])
        full_out[rows, half:] = jnp.where(low, value[:, half:], value[:, :half])


def edge_rows(x, sender, receiver, mask, w_in, w_out, rows, half, slope, act, normed, inverse, out_own, out_sent, update):
    pre = dot(x, w_in[0]) + dot(sender, w_in[1]) + dot(receiver, w_in[2])
    value, derivative = swish_parts(pre)
    value = value.astype(BF16)
    slope[rows] = derivative
    act[rows] = value
    scaled, scale = layer_norm(dot(value, w_out[...]))
    normed[rows] = scaled
    inverse[rows] = scale
    change = scaled if mask is None else scaled * mask
    out = (x.astype(F32) + change).astype(BF16)
    out_own[rows] = out[:, :half]
    out_sent[rows] = out[:, half:]
    update[rows] = change.astype(BF16)


def fine_kernel(info, x_own, x_got, n_own, n_got, low, high, rims_got, idx_c, idx_r, w_in, w_out,
                slope, act, normed, inverse, out_own, out_sent, partial, sent, ext, update):
    half = x_own.shape[1]
    nodes = n_own.shape[0]
    ext[:HALO, :half] = low[...]
    ext[:HALO, half:] = rims_got[:HALO]
    ext[HALO : HALO + nodes, :half] = n_own[...]
    ext[HALO : HALO + nodes, half:] = n_got[...]
    ext[HALO + nodes :, :half] = high[...]
    ext[HALO + nodes :, half:] = rims_got[HALO:]
    node_x = ext[HALO : HALO + nodes]
    chunk = 192
    for start in range(0, x_own.shape[0], chunk):
        rows = pl.ds(start, chunk)
        x = jnp.concatenate([x_own[rows], x_got[rows]], 1)
        sender = dot(one_hot(idx_c[rows, 0:1], ext.shape[0]), ext[...]).astype(BF16)
        receiver = dot(one_hot(idx_c[rows, 1:2], nodes), node_x).astype(BF16)
        edge_rows(x, sender, receiver, None, w_in, w_out, rows, half, slope, act, normed, inverse, out_own, out_sent, update)
    total = dot(one_hot_t(idx_r[1:2], nodes), update[...])
    partial[...] = total
    sent[...] = total.astype(BF16)


def long_kernel(info, x_own, x_got, n_own, n_got, same, other, idx_c, idx_r, w_in, w_out, after,
                slope, act, normed, inverse, out_own, out_sent, partial, sent, sender_rows, update):
    half = x_own.shape[1]
    rows = pl.ds(0, x_own.shape[0])
    count = same.shape[0]
    value = dot(one_hot(idx_c[:, 0:1], count), same[...])
    value = value + dot(one_hot(idx_c[:, 0:1] - count, count), other[...])
    sender_rows[...] = value.astype(BF16)
    x = jnp.concatenate([x_own[...], x_got[...]], 1)
    near = n_own.shape[0]
    node_x = jnp.concatenate([n_own[...], n_got[...]], 1)
    receiver = dot(one_hot(idx_c[:, 1:2], near), node_x).astype(BF16)
    edge_rows(x, sender_rows[...], receiver, idx_c[:, 2:3].astype(F32), w_in, w_out, rows, half, slope, act, normed, inverse, out_own, out_sent, update)
    total = dot(one_hot_t(idx_r[1:2], near), update[...])
    partial[...] = total
    sent[...] = total.astype(BF16)


def column_halves(info, half):
    lat, core = info[0], info[1]
    turn = (core + lat) % 2

    def at(which):
        return pl.ds(pl.multiple_of(which * half, half), half)

    return at(core), at(1 - core), at(turn), at(1 - turn), at(lat), at(1 - lat)


def edge_weight_grads(outs, xf, xl, node_x, extended, srow, cols, act_f, act_l, hidden, dpre, dy, near_sum, recv_sum, fine):
    half = xf.shape[1]
    head, tail = pl.ds(0, fine), pl.ds(fine, dpre.shape[0] - fine)
    for out, columns, columns_own in outs:
        grad = contract_rows(xf[...], dpre[head, columns]) + contract_rows(xl[...], dpre[tail, columns])
        out[:half] = grad.astype(BF16)
        grad = contract_rows(extended, near_sum[:, columns]) + contract_rows(srow[:, cols], dpre[tail, columns])
        out[half : 2 * half] = grad.astype(BF16)
        out[2 * half : 3 * half] = contract_rows(node_x, recv_sum[:, columns]).astype(BF16)
        grad = contract_rows(act_f[:, hidden], dy[head, columns_own]) + contract_rows(act_l[:, hidden], dy[tail, columns_own])
        out[3 * half : 4 * half] = grad.astype(BF16)


def far_sums(idx_r, dpre_long, weights, keep, send, count):
    grads = contract_cols(dpre_long, weights).astype(BF16)
    far = dot(one_hot_t(idx_r[0:1], 2 * count), grads).astype(BF16)
    keep[keep.shape[0] - count :] = far[:count]
    send[send.shape[0] - count :] = far[count:]


def back_kernel(info, partial, got, partial_l, got_l, n_own, n_got, ng_own, ng_got, low, high, rims_got, nin, nout,
                xf_own, xl_own, xf_got, xl_got, gf_own, gl_own, gf_got, gl_got,
                slope_f, slope_l, act_f, act_l, normed_f, normed_l, inverse_f, inverse_l, srow_l,
                idx_cf, idx_cl, idx_rf, idx_rl, w_in, w_out,
                node_out, node_self, keep_pair, send_pair, keep_own, send_own, dpre, near_sum, recv_sum,
                dy, ndpre, ndy, nact, agg_own, agg_grad, ext, ext_own):
    mine, theirs, mine_own, theirs_own, hidden_mine, hidden_theirs = column_halves(info, n_own.shape[1])
    half = n_own.shape[1]
    nodes = n_own.shape[0]
    fine, longs = xf_got.shape[0], xl_got.shape[0]
    far_count = keep_pair.shape[0] - 4 * half

    ext[:HALO] = rims_got[:HALO]
    ext[HALO : HALO + nodes] = n_got[...]
    ext[HALO + nodes :] = rims_got[HALO:]
    node_x = jnp.concatenate([n_own[...], n_got[...]], 1)
    received, received_l = got[...].astype(F32), got_l[...].astype(F32)
    total = partial[...] + jnp.concatenate([received[:, half:], received[:, :half]], 1)
    coarse = partial_l[...] + jnp.concatenate([received_l[:, half:], received_l[:, :half]], 1)
    near = coarse.shape[0]
    agg = jnp.concatenate([total[:near] + coarse, total[near:]], 0).astype(BF16)
    agg_own[...] = agg[:, :half]
    node_value, node_slope = swish_parts(dot(node_x, nin[0]) + dot(agg, nin[1]))
    nact[...] = node_value.astype(BF16)
    node_normed, node_inverse = layer_norm(dot(nact[...], nout[...]))
    node_out[...] = (n_own[...].astype(F32) + node_normed[:, :half]).astype(BF16)
    node_g = jnp.concatenate([ng_own[...], ng_got[...]], 1).astype(F32)
    ndy[...] = norm_backward(node_g, node_normed, node_inverse).astype(BF16)
    ndpre[...] = (contract_cols(ndy[...], nout[...]) * node_slope).astype(BF16)
    agg_grad[...] = contract_cols(ndpre[...], nin[1]).astype(BF16)
    node_self[...] = ng_own[...].astype(F32) + contract_cols(ndpre[...], nin[0, :half])

    chunk = 192
    for start in range(0, fine + longs, chunk):
        rows = pl.ds(start, chunk)
        if start < fine:
            part = pl.ds(start, chunk)
            idx_c = idx_cf
            g_own, g_got, normed, inverse, slope = gf_own, gf_got, normed_f, inverse_f, slope_f
        else:
            part = pl.ds(start - fine, chunk)
            idx_c = idx_cl
            g_own, g_got, normed, inverse, slope = gl_own, gl_got, normed_l, inverse_l, slope_l
        cotangent = jnp.concatenate([g_own[part], g_got[part]], 1).astype(F32)
        cotangent = cotangent + dot(one_hot(idx_c[part, 1:2], nodes), agg_grad[...])
        if start >= fine:
            cotangent = cotangent * idx_cl[part, 2:3].astype(F32)
        dy[rows] = norm_backward(cotangent, normed[part], inverse[part]).astype(BF16)
        dpre[rows] = (contract_cols(dy[rows], w_out[...]) * slope[part]).astype(BF16)

    tail = pl.ds(fine, longs)
    head = pl.ds(0, fine)
    near_sum[...] = dot(one_hot_t(idx_rf[0:1], ext.shape[0]), dpre[head]).astype(BF16)
    recv_sum[...] = (
        dot(one_hot_t(idx_rf[1:2], nodes), dpre[head]) + dot(one_hot_t(idx_rl[1:2], nodes), dpre[tail])
    ).astype(BF16)
    far_sums(idx_rl, dpre[tail], w_in[1, half:], keep_pair, send_pair, far_count)
    edge_weight_grads(
        ((send_pair, theirs, theirs_own), (keep_pair, mine, mine_own)),
        xf_got, xl_got, n_got[...], ext[...], srow_l, slice(half, 2 * half), act_f, act_l, hidden_theirs,
        dpre, dy, near_sum, recv_sum, fine,
    )
    ext_own[:HALO] = low[...]
    ext_own[HALO : HALO + nodes] = n_own[...]
    ext_own[HALO + nodes :] = high[...]
    for own, columns, columns_own in ((send_own, theirs, theirs_own), (keep_own, mine, mine_own)):
        own[4 * half : 5 * half] = contract_rows(n_own[...], ndpre[:, columns]).astype(BF16)
        own[5 * half : 6 * half] = contract_rows(agg_own[...], ndpre[:, columns]).astype(BF16)
        own[6 * half : 7 * half] = contract_rows(nact[:, hidden_mine], ndy[:, columns_own]).astype(BF16)
    far_sums(idx_rl, dpre[tail], w_in[1, :half], keep_own, send_own, far_count)
    edge_weight_grads(
        ((send_own, theirs, theirs_own), (keep_own, mine, mine_own)),
        xf_own, xl_own, n_own[...], ext_own[...], srow_l, slice(0, half), act_f, act_l, hidden_mine,
        dpre, dy, near_sum, recv_sum, fine,
    )


def inputs_kernel(info, dpre, gf_own, gl_own, g_got, near_sum, recv_sum, w_in,
                  grads_own, grads_sent, rim_own, rim_sent):
    half = g_got.shape[1]
    fine, longs = gf_own.shape[0], gl_own.shape[0]
    nodes = recv_sum.shape[0]
    for start, rows, own in ((0, fine, gf_own), (fine, longs, gl_own)):
        part = pl.ds(start, rows)
        change = contract_cols(dpre[part], w_in[0])
        grads_own[part] = (own[...].astype(F32) + change[:, :half]).astype(BF16)
        grads_sent[part] = (g_got[part].astype(F32) + change[:, half:]).astype(BF16)
    near = contract_cols(near_sum[...], w_in[1])
    received = contract_cols(recv_sum[...], w_in[2])
    for rows, value in (
        (slice(0, HALO), near[:HALO]),
        (slice(HALO, HALO + nodes), near[HALO : HALO + nodes] + received),
        (slice(HALO + nodes, 2 * HALO + nodes), near[HALO + nodes :]),
    ):
        rim_own[rows] = value[:, :half]
        rim_sent[rows] = value[:, half:].astype(BF16)


def body(
    node_latents,
    edge_latents,
    senders,
    receivers,
    long_count,
    edge_inner,
    edge_outer,
    node_inner,
    node_outer,
    node_cotangent,
    edge_cotangent,
):
    nodes, half = node_latents.shape
    full = 2 * half
    edges = edge_latents.shape[0]
    rows = edges // 2
    fine, longs = FINE // 2, (edges - FINE) // 2
    quarter = half // 2
    patches = lax.axis_size("patch")
    chips = patches // 2
    extent = nodes + 2 * HALO
    lat = lax.axis_index("lat")
    patch = lax.axis_index("patch")
    core = patch % 2
    first_node = patch * nodes
    info = jnp.stack([lat, core]).astype(I32)

    x_hbm, g_hbm = pinned(edge_latents), pinned(edge_cotangent)
    n_hbm, ng_hbm = pinned(node_latents), pinned(node_cotangent)
    wi_hbm, wo_hbm = pinned(edge_inner), pinned(edge_outer)
    ni_hbm, no_hbm = pinned(node_inner), pinned(node_outer)

    def rows_of(value):
        return (
            lax.dynamic_slice_in_dim(value, lat * fine, fine, 0),
            lax.dynamic_slice_in_dim(value, FINE + lat * longs, longs, 0),
        )

    near_ids, far_ids = rows_of(senders.reshape(edges))
    recv_f, recv_l = rows_of(receivers.reshape(edges))
    near = (near_ids - first_node + HALO) % (nodes * patches)
    far_patch, far_row = far_ids // nodes, far_ids % nodes
    is_same = far_patch % 2 == core
    far_slot = jnp.where(is_same, 0, chips * COARSE) + far_patch // 2 * COARSE + far_row
    live = (jnp.arange(longs, dtype=I32) + lat * longs < long_count[0]).astype(I32)
    idx_rf = jnp.stack([near, recv_f - first_node])
    idx_rl = jnp.stack([far_slot, recv_l - first_node, live])
    idx_cf, idx_cl = idx_rf.T, idx_rl.T

    fine_other = block((fine, half), lambda i, s: (1 - s[0], 0))
    long_other = block((longs, half), lambda i, s: (FINE // longs + 1 - s[0], 0))
    quarter_rows = block((quarter, full), lambda i, s: (s[1], 0))
    sent_x, sent_we, rim_low, rim_high = call(
        pack_kernel,
        info,
        (x_hbm, x_hbm, n_hbm, wi_hbm, wo_hbm),
        [
            fine_other, long_other, whole((nodes, half)),
            block((3, quarter, full), lambda i, s: (0, s[1], 0)), quarter_rows,
        ],
        [((rows + nodes, half), BF16), ((4, quarter, full), BF16), ((HALO, half), BF16), ((HALO, half), BF16)],
        moved=3_000_000,
        name="pack",
    )
    we_got = other_neighbour(sent_we)
    x_got = pinned(swap_lat(sent_x))
    low, high = shifted(rim_high, 1), shifted(rim_low, -1)
    far_rows = chips * COARSE
    (sent_coarse,) = call(
        coarse_kernel,
        info,
        (n_hbm, swap_lat(node_latents[:16]), rim_low),
        [whole((16, half)), whole((16, half)), pl.BlockSpec(memory_space=pl.ANY)],
        [((chips, COARSE, full), BF16)],
        [pltpu.VMEM((chips, COARSE, full), BF16), pltpu.SemaphoreType.DMA],
        moved=600_000,
        name="coarse_rows",
        in_hbm=(0,),
    )
    same = chips_all_to_all(sent_coarse)
    rims_got = swap_lat(jnp.concatenate([low, high], 0))
    we_got = gated(info, we_got, (rims_got,))
    we_again = swap_core(we_got)

    got_spec = [whole((4, quarter, full))] * 2
    w_in, w_out, sent_g, sent_wn = call(
        edge_weights_kernel,
        info,
        (wi_hbm, wo_hbm, pinned(we_got), pinned(we_again), g_hbm, g_hbm, ng_hbm, ni_hbm, no_hbm, x_got, idx_cf, idx_cl),
        [whole((3, half, full)), whole((half, full))] + got_spec + [
            fine_other, long_other, whole((nodes, half)),
            block((2, quarter, full), lambda i, s: (0, s[1], 0)), quarter_rows,
            pl.BlockSpec(memory_space=pl.ANY), whole((fine, 2)), whole((longs, 3)),
        ],
        [((3, full, full), BF16), ((full, full), BF16), ((rows + nodes, half), BF16), ((3, quarter, full), BF16)],
        moved=7_000_000,
        name="edge_weights",
    )
    wn_got = other_neighbour(sent_wn)
    g_got = swap_lat(sent_g)
    def fine_own():
        return block((fine, half), lambda i, s: (s[0], 0))

    def long_own():
        return block((longs, half), lambda i, s: (FINE // longs + s[0], 0))

    def fine_got():
        return whole((fine, half))

    def long_got():
        return block((longs, half), lambda i, s: (fine // longs, 0))

    node_spec = whole((nodes, half))
    got_nodes = block((nodes, half), lambda i, s: (rows // nodes, 0))
    rim = whole((HALO, half))
    win_spec, wout_spec = whole((3, full, full)), whole((full, full))

    def forward_outs(count, reach):
        return [
            ((count, full), F32),
            ((count, full), BF16),
            ((count, full), F32),
            ((count, 1), F32),
            ((count, half), BF16),
            ((count, half), BF16),
            ((reach, full), F32),
            ((reach, full), BF16),
        ]

    slope_f, act_f, normed_f, inverse_f, fine_out, fine_sent, partial_f, partial_f_sent = call(
        fine_kernel,
        info,
        (x_hbm, x_got, n_hbm, x_got, low, high, rims_got, idx_cf, idx_rf, w_in, w_out),
        [
            fine_own(), fine_got(), node_spec, got_nodes, rim, rim, whole((2 * HALO, half)),
            whole((fine, 2)), whole((2, fine)), win_spec, wout_spec,
        ],
        forward_outs(fine, nodes),
        [pltpu.VMEM((extent, full), BF16), pltpu.VMEM((fine, full), BF16)],
        flops=2 * fine * full * (4 * full + extent + 2 * nodes),
        moved=8_000_000,
        name="edges_forward_fine",
    )
    other = swap_core(same).reshape(far_rows, full)
    same = same.reshape(far_rows, full)
    slope_l, act_l, normed_l, inverse_l, long_out, long_sent, partial_l, partial_l_sent, srow_l = call(
        long_kernel,
        info,
        (x_hbm, x_got, n_hbm, x_got, same, other, idx_cl, idx_rl, w_in, w_out, g_got),
        [
            long_own(), long_got(), whole((16, half)), block((16, half), lambda i, s: (rows // 16, 0)),
            whole((far_rows, full)), whole((far_rows, full)),
            whole((longs, 3)), whole((3, longs)), win_spec, wout_spec,
            pl.BlockSpec(memory_space=pl.ANY),
        ],
        forward_outs(longs, 16) + [((longs, full), BF16)],
        [pltpu.VMEM((longs, full), BF16)],
        flops=2 * longs * full * (4 * full + 4 * patches * COARSE + 2 * nodes),
        moved=6_000_000,
        name="edges_forward_long",
    )
    partial_f_got = swap_lat(partial_f_sent)
    wn_got = gated(info, wn_got, (partial_l_sent, partial_f_got))
    wn_again = swap_core(wn_got)
    nin, nout = call(
        weights_kernel,
        info,
        (ni_hbm, no_hbm, wn_got, wn_again),
        [whole((2, half, full)), whole((half, full)), whole((3, quarter, full)), whole((3, quarter, full))],
        [((2, full, full), BF16), ((full, full), BF16)],
        moved=3_000_000,
        name="node_weights",
    )
    partial_l_got = swap_lat(partial_l_sent)

    edge_out_got = swap_lat(jnp.concatenate([fine_sent, long_sent], 0))
    rows_pair, rows_own = 4 * half + far_rows, 7 * half + far_rows

    node_output, node_self, keep_pair, send_pair, keep_own, send_own, dpre, near_sum, recv_sum = call(
        back_kernel,
        info,
        (partial_f, partial_f_got, partial_l, partial_l_got, n_hbm, x_got, ng_hbm, g_got, low, high, rims_got, nin, nout,
         x_hbm, x_hbm, x_got, x_got, g_hbm, g_hbm, g_got, g_got,
         slope_f, slope_l, act_f, act_l, normed_f, normed_l, inverse_f, inverse_l, srow_l,
         idx_cf, idx_cl, idx_rf, idx_rl, w_in, w_out),
        [
            whole((nodes, full)), whole((nodes, full)), whole((16, full)), whole((16, full)),
            node_spec, got_nodes, node_spec, got_nodes,
            rim, rim, whole((2 * HALO, half)), whole((2, full, full)), wout_spec,
            fine_own(), long_own(), fine_got(), long_got(), fine_own(), long_own(), fine_got(), long_got(),
            whole((fine, full)), whole((longs, full)), whole((fine, full)), whole((longs, full)),
            whole((fine, full)), whole((longs, full)), whole((fine, 1)), whole((longs, 1)),
            whole((longs, full)),
            whole((fine, 2)), whole((longs, 3)), whole((2, fine)), whole((3, longs)), win_spec, wout_spec,
        ],
        [
            ((nodes, half), BF16),
            ((nodes, half), F32),
            ((rows_pair, half), BF16),
            ((rows_pair, half), BF16),
            ((rows_own, half), BF16),
            ((rows_own, half), BF16),
            ((rows, full), BF16),
            ((extent, full), BF16),
            ((nodes, full), BF16),
        ],
        [
            pltpu.VMEM((rows, full), BF16),
            pltpu.VMEM((nodes, full), BF16),
            pltpu.VMEM((nodes, full), BF16),
            pltpu.VMEM((nodes, full), BF16),
            pltpu.VMEM((nodes, half), BF16),
            pltpu.VMEM((nodes, full), BF16),
            pltpu.VMEM((extent, half), BF16),
            pltpu.VMEM((extent, half), BF16),
        ],
        flops=8 * rows * full * full,
        moved=14_000_000,
        name="nodes_and_edges_backward",
        limit=28,
    )
    core_pair, core_own = swap_core(send_pair), swap_core(send_own)
    by_lat, by_other = call(
        lat_stage_kernel,
        info,
        (keep_pair, core_pair),
        [whole((rows_pair, half)), whole((rows_pair, half))],
        [((rows_pair // 2, half), BF16), ((rows_pair // 2, half), BF16)],
        moved=2_400_000,
        name="lat_stage",
    )
    blocks = half // LANES
    total_rows = 7 * half * blocks
    share = total_rows // chips
    slot = share + blocks * COARSE
    (gathered,) = call(
        combine_kernel,
        info,
        (keep_own, core_own, swap_lat(by_lat), other_neighbour(by_other)),
        [whole((rows_own, half)), whole((rows_own, half)), whole((rows_pair // 2, half)), whole((rows_pair // 2, half))],
        [((chips, slot, LANES), BF16)],
        [pltpu.VMEM((chips, slot, LANES), BF16), pltpu.SemaphoreType.DMA],
        moved=4_300_000,
        name="combine",
        in_hbm=(0,),
    )
    arrived = chips_all_to_all(gathered)

    grads_own, grads_sent, rim_own, rim_sent = call(
        inputs_kernel,
        info,
        (pinned(dpre), g_hbm, g_hbm, g_got, pinned(near_sum), pinned(recv_sum), w_in),
        [
            whole((rows, full)), fine_own(), long_own(), whole((rows, half)),
            whole((extent, full)), whole((nodes, full)), win_spec,
        ],
        [((rows, half), BF16), ((rows, half), BF16), ((extent, half), F32), ((extent, half), BF16)],
        flops=4 * rows * full * full,
        moved=5_000_000,
        name="input_gradients",
    )

    (edge_output,) = call(
        rows_kernel,
        info,
        (fine_out, long_out, edge_out_got),
        [whole((fine, half)), whole((longs, half)), whole((rows, half))],
        [((edges, half), BF16)],
        [pltpu.SemaphoreType.DMA((4,))],
        moved=1_600_000,
        name="edge_output_rows",
        in_hbm=(0,),
    )
    (edge_grads,) = call(
        rows_kernel,
        info,
        (grads_own, grads_own, swap_lat(grads_sent)),
        [whole((fine, half)), block((longs, half), lambda i, s: (fine // longs, 0)), whole((rows, half))],
        [((edges, half), BF16)],
        [pltpu.SemaphoreType.DMA((4,))],
        moved=1_600_000,
        name="edge_gradient_rows",
        in_hbm=(0,),
    )
    summed = rim_own + swap_lat(rim_sent).astype(F32)
    to_low = shifted(summed[:HALO].astype(BF16), -1).astype(F32)
    to_high = shifted(summed[HALO + nodes :].astype(BF16), 1).astype(F32)

    weight_share, coarse_total = call(
        functools.partial(share_kernel, scale=1.0 / patches),
        info,
        (arrived, pinned(edge_output), to_low, to_high),
        [pl.BlockSpec(memory_space=pl.ANY), pl.BlockSpec(memory_space=pltpu.HBM)]
        + [pl.BlockSpec(memory_space=pl.ANY)] * 2,
        [((chips, share, LANES), BF16), ((blocks * COARSE, LANES), F32)],
        [
            pltpu.VMEM((chips, slot, LANES), BF16),
            pltpu.VMEM((chips, share, LANES), BF16),
            pltpu.SemaphoreType.DMA,
        ],
        in_hbm=(0,),
        moved=2_200_000,
        name="share",
    )
    coarse_share = jnp.concatenate(
        [coarse_total[i * COARSE : (i + 1) * COARSE] for i in range(blocks)], 1
    )
    own_grads = node_self + summed[HALO : HALO + nodes]
    own_grads = own_grads.at[nodes - HALO :].add(to_low)
    own_grads = own_grads.at[:HALO].add(to_high)
    own_grads = own_grads.at[:COARSE].add(coarse_share)
    node_grads = own_grads.astype(BF16)
    mine = gated(info, chips_all_to_all(weight_share), (pinned(edge_grads), pinned(node_grads)), pltpu.HBM)
    mine = mine.reshape(blocks, total_rows // blocks, LANES)
    other = swap_core(mine)
    square = (half, full)
    weights = pl.pallas_call(
        results_kernel,
        grid_spec=pltpu.PrefetchScalarGridSpec(
            num_scalar_prefetch=1,
            grid=(1,),
            in_specs=[whole(mine.shape)] * 2,
            out_specs=[pl.BlockSpec(memory_space=pl.ANY)] * 4,
            scratch_shapes=[pltpu.VMEM((7,) + square, F32), pltpu.SemaphoreType.DMA((7,))],
        ),
        out_shape=[jax.ShapeDtypeStruct(shape, F32) for shape in ((3,) + square, square, (2,) + square, square)],
        compiler_params=pltpu.CompilerParams(vmem_limit_bytes=14 * MIB),
        cost_estimate=pl.CostEstimate(flops=0, bytes_accessed=6_000_000, transcendentals=0),
        name="results",
    )(info, mine, other)
    return (edge_output, node_output, edge_grads, node_grads, *weights)


def solution(mesh):
    placed = (
        P("patch", "lat"),
        P("patch", "lat"),
        P("patch", None),
        P("patch", None),
        P("patch"),
        P(None, "lat", None),
        P("lat", None),
        P(None, "lat", None),
        P("lat", None),
        P("patch", "lat"),
        P("patch", "lat"),
    )
    return jax.shard_map(
        body,
        mesh=mesh,
        in_specs=placed,
        out_specs=(
            P("patch", "lat"),
            P("patch", "lat"),
            P("patch", "lat"),
            P("patch", "lat"),
            P(None, "lat", None),
            P("lat", None),
            P(None, "lat", None),
            P("lat", None),
        ),
        check_vma=False,
    )
```

```python
import functools

import jax
import jax.numpy as jnp
from jax import lax
from jax.experimental import pallas as pl
from jax.experimental.pallas import tpu as pltpu
from jax.sharding import PartitionSpec as P

HALO = 32
COARSE = 8
FINE = 1152
EPSILON = 1e-05
F32 = jnp.float32
BF16 = jnp.bfloat16
I32 = jnp.int32
LANES = 128
MIB = 1024 * 1024


def dot(left, right):
    return jnp.dot(left, right, preferred_element_type=F32)


def contract_rows(left, right):
    return lax.dot_general(left, right, (((0,), (0,)), ((), ())), preferred_element_type=F32)


def contract_cols(left, right):
    return lax.dot_general(left, right, (((1,), (1,)), ((), ())), preferred_element_type=F32)


def layer_norm(values):
    centered = values - jnp.mean(values, axis=1, keepdims=True)
    inverse = lax.rsqrt(jnp.mean(centered * centered, axis=1, keepdims=True) + EPSILON)
    return centered * inverse, inverse


def norm_backward(cotangent, normed, inverse):
    mean = jnp.mean(cotangent, axis=1, keepdims=True)
    crossed = jnp.mean(cotangent * normed, axis=1, keepdims=True)
    return (cotangent - mean - normed * crossed) * inverse


def swish_parts(values):
    sigmoid = jax.nn.sigmoid(values)
    return values * sigmoid, sigmoid * (1.0 + values * (1.0 - sigmoid))


def one_hot(index, width):
    return (index == lax.broadcasted_iota(I32, (index.shape[0], width), 1)).astype(F32).astype(BF16)


def one_hot_t(index, width):
    return (index == lax.broadcasted_iota(I32, (width, index.shape[1]), 0)).astype(F32).astype(BF16)


def swap_lat(value):
    return lax.ppermute(value, "lat", [(0, 1), (1, 0)])


def swap_core(value):
    count = lax.axis_size("patch")
    return lax.ppermute(value, "patch", [(i, i ^ 1) for i in range(count)])


def shifted(value, steps):
    count = lax.axis_size("patch")
    return lax.ppermute(value, "patch", [(i, (i + steps) % count) for i in range(count)])


def other_neighbour(value):
    count = lax.axis_size("patch")
    pairs = []
    for patch in range(count):
        for lat in range(2):
            pairs.append((patch * 2 + lat, (patch ^ 2) * 2 + (1 - lat)))
    return lax.ppermute(value, ("patch", "lat"), pairs)


def chips_all_to_all(value):
    count = lax.axis_size("patch")
    groups = [list(range(core, count, 2)) for core in range(2)]
    return lax.all_to_all(value, "patch", 0, 0, tiled=True, axis_index_groups=groups)


def whole(shape):
    return pl.BlockSpec(shape, lambda i, s: (0,) * len(shape), pipeline_mode=pl.Buffered(1))


def block(shape, index):
    return pl.BlockSpec(shape, index, pipeline_mode=pl.Buffered(1))


def call(kernel, info, operands, in_specs, outs, scratch=(), flops=0, moved=0, name=None, in_hbm=(), limit=14):
    return pl.pallas_call(
        kernel,
        grid_spec=pltpu.PrefetchScalarGridSpec(
            num_scalar_prefetch=1,
            grid=(1,),
            in_specs=in_specs,
            out_specs=[
                pl.BlockSpec(memory_space=pltpu.HBM) if i in in_hbm else whole(shape)
                for i, (shape, _) in enumerate(outs)
            ],
            scratch_shapes=list(scratch),
        ),
        out_shape=[jax.ShapeDtypeStruct(shape, dtype) for shape, dtype in outs],
        compiler_params=pltpu.CompilerParams(vmem_limit_bytes=limit * MIB),
        cost_estimate=pl.CostEstimate(flops=flops, bytes_accessed=moved, transcendentals=0),
        name=name,
    )(info, *operands)


def pinned(value):
    return pltpu.with_memory_space_constraint(value, pltpu.HBM)


def pack_kernel(info, xf, xl, gf, gl, n, ng, wi, wo, xs, gs, wes, low, high):
    fine = xf.shape[0]
    low[...] = n[:HALO]
    high[...] = n[n.shape[0] - HALO :]
    wes[:3] = wi[...]
    wes[3] = wo[...]
    xs[:fine] = xf[...]
    xs[fine : fine + xl.shape[0]] = xl[...]
    xs[fine + xl.shape[0] :] = n[...]
    gs[:fine] = gf[...]
    gs[fine : fine + gl.shape[0]] = gl[...]
    gs[fine + gl.shape[0] :] = ng[...]


def coarse_kernel(info, n_own, n_got, after, out, staged, sem):
    half = n_own.shape[1]
    for columns, n in ((slice(0, half), n_own), (slice(half, 2 * half), n_got)):
        staged[:, :, columns] = jnp.broadcast_to(n[:COARSE][None], (staged.shape[0], COARSE, half))
    copy = pltpu.make_async_copy(staged, out, sem)
    copy.start()
    copy.wait()


def gate_kernel(info, value, *rest):
    pass


def gated(info, value, after, space=pl.ANY):
    anywhere = pl.BlockSpec(memory_space=pl.ANY)
    return pl.pallas_call(
        gate_kernel,
        in_specs=[pl.BlockSpec(memory_space=pltpu.SMEM)] + [anywhere] + [pl.BlockSpec(memory_space=space)] * len(after),
        out_specs=anywhere,
        out_shape=jax.ShapeDtypeStruct(value.shape, value.dtype),
        input_output_aliases={1: 0},
        compiler_params=pltpu.CompilerParams(vmem_limit_bytes=MIB),
        name="gate",
    )(info, value, *after)


def lat_stage_kernel(info, keep, got, first, second):
    rows = first.shape[0]
    first[...] = (keep[:rows].astype(F32) + got[:rows].astype(F32)).astype(BF16)
    second[...] = (keep[rows:].astype(F32) + got[rows:].astype(F32)).astype(BF16)


def combine_kernel(info, keep, got, first, second, out, staged, sem):
    chips = out.shape[0]
    rows = first.shape[0]
    edge_rows_count, far_rows = 2 * rows - chips * COARSE, chips * COARSE
    half_chips = chips // 2
    total = keep[...].astype(F32) + got[...].astype(F32)
    pair = jnp.concatenate([first[...], second[...]], 0).astype(F32)
    weights = jnp.concatenate(
        [total[:edge_rows_count] + pair[:edge_rows_count], total[edge_rows_count:-far_rows]], 0
    )
    far = total[-far_rows:] + pair[edge_rows_count:]
    share = weights.shape[0] // half_chips
    parts = [weights[:, i * LANES : (i + 1) * LANES].reshape(half_chips, share, LANES) for i in range(2)]
    coarse = [far[:, i * LANES : (i + 1) * LANES].reshape(chips, COARSE, LANES) for i in range(2)]
    staged[...] = jnp.concatenate([jnp.concatenate(parts, 0)] + coarse, 1).astype(BF16)
    copy = pltpu.make_async_copy(staged, out, sem)
    copy.start()
    copy.wait()


def share_kernel(info, arrived, output, low, high, weights, coarse, taken, staged, sem, *, scale):
    share = staged.shape[1]
    copy = pltpu.make_async_copy(arrived, taken, sem)
    copy.start()
    copy.wait()
    total = jnp.sum(taken[...].astype(F32), 0)
    staged[...] = jnp.broadcast_to((total[:share] * scale).astype(BF16)[None], staged.shape)
    copy = pltpu.make_async_copy(staged, weights, sem)
    copy.start()
    coarse[...] = total[share:]
    copy.wait()


def rows_kernel(info, own_f, own_l, got, out, sems):
    lat = info[0]
    fine, longs = own_f.shape[0], own_l.shape[0]
    copies = []
    for side, f, l in (
        (lat, own_f, own_l),
        (1 - lat, got.at[pl.ds(0, fine)], got.at[pl.ds(fine, longs)]),
    ):
        copies.append((f, out.at[pl.ds(pl.multiple_of(side * fine, 64), fine)]))
        copies.append((l, out.at[pl.ds(pl.multiple_of(FINE + side * longs, 64), longs)]))
    made = [pltpu.make_async_copy(a, b, sems.at[k]) for k, (a, b) in enumerate(copies)]
    for copy in made:
        copy.start()
    for copy in made:
        copy.wait()


def results_kernel(info, mine, other, inner, outer, node_inner, node_outer, staged, sems):
    first = info[1] == 0
    blocks, half = mine.shape[0], staged.shape[1]
    targets = [inner.at[0], inner.at[1], inner.at[2], outer, node_inner.at[0], node_inner.at[1], node_outer]
    copies = []
    for k, target in enumerate(targets):
        rows = slice(k * half, (k + 1) * half)
        for i in range(blocks):
            a, b = mine[i, rows].astype(F32), other[i, rows].astype(F32)
            staged[k, :, i * LANES : (i + 1) * LANES] = jnp.where(first, a, b)
            staged[k, :, half + i * LANES : half + (i + 1) * LANES] = jnp.where(first, b, a)
        copies.append(pltpu.make_async_copy(staged.at[k], target, sems.at[k]))
        copies[-1].start()
    for copy in copies:
        copy.wait()


def edge_weights_kernel(info, wi, wo, got, again, ni, no, after, idx_f, idx_l, full_in, full_out, wns):
    wns[:2] = ni[...]
    wns[2] = no[...]
    weights_kernel(info, wi, wo, got, again, full_in, full_out)


def weights_kernel(info, wi, wo, got, again, full_in, full_out):
    lat, core = info[0], info[1]
    half = wo.shape[0]
    quarter = half // 2
    inner = wi.shape[0]
    first = core == 0
    for k in range(inner):
        full_in[k, :half] = wi[k]
        full_in[k, half : half + quarter] = jnp.where(first, got[k], again[k])
        full_in[k, half + quarter :] = jnp.where(first, again[k], got[k])
    own = wo[...]
    top = jnp.where(first, got[inner], again[inner])
    bottom = jnp.where(first, again[inner], got[inner])
    missing = jnp.concatenate([top, bottom], 0)
    low = lat == 0
    for rows, value in ((slice(0, half), jnp.where(low, own, missing)), (slice(half, 2 * half), jnp.where(low, missing, own))):
        full_out[rows, :half] = jnp.where(low, value[:, :half], value[:, half:])
        full_out[rows, half:] = jnp.where(low, value[:, half:], value[:, :half])


def edge_rows(x, sender, receiver, mask, w_in, w_out, rows, half, slope, act, normed, inverse, out_own, out_sent, update):
    pre = dot(x, w_in[0]) + dot(sender, w_in[1]) + dot(receiver, w_in[2])
    value, derivative = swish_parts(pre)
    value = value.astype(BF16)
    slope[rows] = derivative
    act[rows] = value
    scaled, scale = layer_norm(dot(value, w_out[...]))
    normed[rows] = scaled
    inverse[rows] = scale
    change = scaled if mask is None else scaled * mask
    out = (x.astype(F32) + change).astype(BF16)
    out_own[rows] = out[:, :half]
    out_sent[rows] = out[:, half:]
    update[rows] = change.astype(BF16)


def fine_kernel(info, x_own, x_got, n_own, n_got, low, high, rims_got, idx_c, idx_r, w_in, w_out,
                slope, act, normed, inverse, out_own, out_sent, partial, sent, ext, update):
    half = x_own.shape[1]
    nodes = n_own.shape[0]
    ext[:HALO, :half] = low[...]
    ext[:HALO, half:] = rims_got[:HALO]
    ext[HALO : HALO + nodes, :half] = n_own[...]
    ext[HALO : HALO + nodes, half:] = n_got[...]
    ext[HALO + nodes :, :half] = high[...]
    ext[HALO + nodes :, half:] = rims_got[HALO:]
    node_x = ext[HALO : HALO + nodes]
    chunk = 192
    for start in range(0, x_own.shape[0], chunk):
        rows = pl.ds(start, chunk)
        x = jnp.concatenate([x_own[rows], x_got[rows]], 1)
        sender = dot(one_hot(idx_c[rows, 0:1], ext.shape[0]), ext[...]).astype(BF16)
        receiver = dot(one_hot(idx_c[rows, 1:2], nodes), node_x).astype(BF16)
        edge_rows(x, sender, receiver, None, w_in, w_out, rows, half, slope, act, normed, inverse, out_own, out_sent, update)
    total = dot(one_hot_t(idx_r[1:2], nodes), update[...])
    partial[...] = total
    sent[...] = total.astype(BF16)


def long_kernel(info, x_own, x_got, n_own, n_got, same, other, idx_c, idx_r, w_in, w_out, after,
                slope, act, normed, inverse, out_own, out_sent, partial, sent, sender_rows, update):
    half = x_own.shape[1]
    rows = pl.ds(0, x_own.shape[0])
    count = same.shape[0]
    value = dot(one_hot(idx_c[:, 0:1], count), same[...])
    value = value + dot(one_hot(idx_c[:, 0:1] - count, count), other[...])
    sender_rows[...] = value.astype(BF16)
    x = jnp.concatenate([x_own[...], x_got[...]], 1)
    near = n_own.shape[0]
    node_x = jnp.concatenate([n_own[...], n_got[...]], 1)
    receiver = dot(one_hot(idx_c[:, 1:2], near), node_x).astype(BF16)
    edge_rows(x, sender_rows[...], receiver, idx_c[:, 2:3].astype(F32), w_in, w_out, rows, half, slope, act, normed, inverse, out_own, out_sent, update)
    total = dot(one_hot_t(idx_r[1:2], near), update[...])
    partial[...] = total
    sent[...] = total.astype(BF16)


def column_halves(info, half):
    lat, core = info[0], info[1]
    turn = (core + lat) % 2

    def at(which):
        return pl.ds(pl.multiple_of(which * half, half), half)

    return at(core), at(1 - core), at(turn), at(1 - turn), at(lat), at(1 - lat)


def edge_weight_grads(outs, xf, xl, node_x, extended, srow, cols, act_f, act_l, hidden, dpre, dy, near_sum, recv_sum, fine):
    half = xf.shape[1]
    head, tail = pl.ds(0, fine), pl.ds(fine, dpre.shape[0] - fine)
    for out, columns, columns_own in outs:
        grad = contract_rows(xf[...], dpre[head, columns]) + contract_rows(xl[...], dpre[tail, columns])
        out[:half] = grad.astype(BF16)
        grad = contract_rows(extended, near_sum[:, columns]) + contract_rows(srow[:, cols], dpre[tail, columns])
        out[half : 2 * half] = grad.astype(BF16)
        out[2 * half : 3 * half] = contract_rows(node_x, recv_sum[:, columns]).astype(BF16)
        grad = contract_rows(act_f[:, hidden], dy[head, columns_own]) + contract_rows(act_l[:, hidden], dy[tail, columns_own])
        out[3 * half : 4 * half] = grad.astype(BF16)


def far_sums(idx_r, dpre_long, weights, keep, send, count):
    grads = contract_cols(dpre_long, weights).astype(BF16)
    far = dot(one_hot_t(idx_r[0:1], 2 * count), grads).astype(BF16)
    keep[keep.shape[0] - count :] = far[:count]
    send[send.shape[0] - count :] = far[count:]


def back_kernel(info, partial, got, partial_l, got_l, n_own, n_got, ng_own, ng_got, low, high, rims_got, nin, nout,
                xf_own, xl_own, xf_got, xl_got, gf_own, gl_own, gf_got, gl_got,
                slope_f, slope_l, act_f, act_l, normed_f, normed_l, inverse_f, inverse_l, srow_l,
                idx_cf, idx_cl, idx_rf, idx_rl, w_in, w_out,
                node_out, node_self, keep_pair, send_pair, keep_own, send_own, dpre, near_sum, recv_sum,
                dy, ndpre, ndy, nact, agg_own, agg_grad, ext, ext_own):
    mine, theirs, mine_own, theirs_own, hidden_mine, hidden_theirs = column_halves(info, n_own.shape[1])
    half = n_own.shape[1]
    nodes = n_own.shape[0]
    fine, longs = xf_got.shape[0], xl_got.shape[0]
    far_count = keep_pair.shape[0] - 4 * half

    ext[:HALO] = rims_got[:HALO]
    ext[HALO : HALO + nodes] = n_got[...]
    ext[HALO + nodes :] = rims_got[HALO:]
    node_x = jnp.concatenate([n_own[...], n_got[...]], 1)
    received, received_l = got[...].astype(F32), got_l[...].astype(F32)
    total = partial[...] + jnp.concatenate([received[:, half:], received[:, :half]], 1)
    coarse = partial_l[...] + jnp.concatenate([received_l[:, half:], received_l[:, :half]], 1)
    near = coarse.shape[0]
    agg = jnp.concatenate([total[:near] + coarse, total[near:]], 0).astype(BF16)
    agg_own[...] = agg[:, :half]
    node_value, node_slope = swish_parts(dot(node_x, nin[0]) + dot(agg, nin[1]))
    nact[...] = node_value.astype(BF16)
    node_normed, node_inverse = layer_norm(dot(nact[...], nout[...]))
    node_out[...] = (n_own[...].astype(F32) + node_normed[:, :half]).astype(BF16)
    node_g = jnp.concatenate([ng_own[...], ng_got[...]], 1).astype(F32)
    ndy[...] = norm_backward(node_g, node_normed, node_inverse).astype(BF16)
    ndpre[...] = (contract_cols(ndy[...], nout[...]) * node_slope).astype(BF16)
    agg_grad[...] = contract_cols(ndpre[...], nin[1]).astype(BF16)
    node_self[...] = ng_own[...].astype(F32) + contract_cols(ndpre[...], nin[0, :half])

    chunk = 192
    for start in range(0, fine + longs, chunk):
        rows = pl.ds(start, chunk)
        if start < fine:
            part = pl.ds(start, chunk)
            idx_c = idx_cf
            g_own, g_got, normed, inverse, slope = gf_own, gf_got, normed_f, inverse_f, slope_f
        else:
            part = pl.ds(start - fine, chunk)
            idx_c = idx_cl
            g_own, g_got, normed, inverse, slope = gl_own, gl_got, normed_l, inverse_l, slope_l
        cotangent = jnp.concatenate([g_own[part], g_got[part]], 1).astype(F32)
        cotangent = cotangent + dot(one_hot(idx_c[part, 1:2], nodes), agg_grad[...])
        if start >= fine:
            cotangent = cotangent * idx_cl[part, 2:3].astype(F32)
        dy[rows] = norm_backward(cotangent, normed[part], inverse[part]).astype(BF16)
        dpre[rows] = (contract_cols(dy[rows], w_out[...]) * slope[part]).astype(BF16)

    tail = pl.ds(fine, longs)
    head = pl.ds(0, fine)
    near_sum[...] = dot(one_hot_t(idx_rf[0:1], ext.shape[0]), dpre[head]).astype(BF16)
    recv_sum[...] = (
        dot(one_hot_t(idx_rf[1:2], nodes), dpre[head]) + dot(one_hot_t(idx_rl[1:2], nodes), dpre[tail])
    ).astype(BF16)
    far_sums(idx_rl, dpre[tail], w_in[1, half:], keep_pair, send_pair, far_count)
    edge_weight_grads(
        ((send_pair, theirs, theirs_own), (keep_pair, mine, mine_own)),
        xf_got, xl_got, n_got[...], ext[...], srow_l, slice(half, 2 * half), act_f, act_l, hidden_theirs,
        dpre, dy, near_sum, recv_sum, fine,
    )
    ext_own[:HALO] = low[...]
    ext_own[HALO : HALO + nodes] = n_own[...]
    ext_own[HALO + nodes :] = high[...]
    for own, columns, columns_own in ((send_own, theirs, theirs_own), (keep_own, mine, mine_own)):
        own[4 * half : 5 * half] = contract_rows(n_own[...], ndpre[:, columns]).astype(BF16)
        own[5 * half : 6 * half] = contract_rows(agg_own[...], ndpre[:, columns]).astype(BF16)
        own[6 * half : 7 * half] = contract_rows(nact[:, hidden_mine], ndy[:, columns_own]).astype(BF16)
    far_sums(idx_rl, dpre[tail], w_in[1, :half], keep_own, send_own, far_count)
    edge_weight_grads(
        ((send_own, theirs, theirs_own), (keep_own, mine, mine_own)),
        xf_own, xl_own, n_own[...], ext_own[...], srow_l, slice(0, half), act_f, act_l, hidden_mine,
        dpre, dy, near_sum, recv_sum, fine,
    )


def inputs_kernel(info, dpre, gf_own, gl_own, g_got, near_sum, recv_sum, w_in,
                  grads_own, grads_sent, rim_own, rim_sent):
    half = g_got.shape[1]
    fine, longs = gf_own.shape[0], gl_own.shape[0]
    nodes = recv_sum.shape[0]
    for start, rows, own in ((0, fine, gf_own), (fine, longs, gl_own)):
        part = pl.ds(start, rows)
        change = contract_cols(dpre[part], w_in[0])
        grads_own[part] = (own[...].astype(F32) + change[:, :half]).astype(BF16)
        grads_sent[part] = (g_got[part].astype(F32) + change[:, half:]).astype(BF16)
    near = contract_cols(near_sum[...], w_in[1])
    received = contract_cols(recv_sum[...], w_in[2])
    for rows, value in (
        (slice(0, HALO), near[:HALO]),
        (slice(HALO, HALO + nodes), near[HALO : HALO + nodes] + received),
        (slice(HALO + nodes, 2 * HALO + nodes), near[HALO + nodes :]),
    ):
        rim_own[rows] = value[:, :half]
        rim_sent[rows] = value[:, half:].astype(BF16)


def body(
    node_latents,
    edge_latents,
    senders,
    receivers,
    long_count,
    edge_inner,
    edge_outer,
    node_inner,
    node_outer,
    node_cotangent,
    edge_cotangent,
):
    nodes, half = node_latents.shape
    full = 2 * half
    edges = edge_latents.shape[0]
    rows = edges // 2
    fine, longs = FINE // 2, (edges - FINE) // 2
    quarter = half // 2
    patches = lax.axis_size("patch")
    chips = patches // 2
    extent = nodes + 2 * HALO
    lat = lax.axis_index("lat")
    patch = lax.axis_index("patch")
    core = patch % 2
    first_node = patch * nodes
    info = jnp.stack([lat, core]).astype(I32)

    x_hbm, g_hbm = pinned(edge_latents), pinned(edge_cotangent)
    n_hbm, ng_hbm = pinned(node_latents), pinned(node_cotangent)
    wi_hbm, wo_hbm = pinned(edge_inner), pinned(edge_outer)
    ni_hbm, no_hbm = pinned(node_inner), pinned(node_outer)

    def rows_of(value):
        return (
            lax.dynamic_slice_in_dim(value, lat * fine, fine, 0),
            lax.dynamic_slice_in_dim(value, FINE + lat * longs, longs, 0),
        )

    near_ids, far_ids = rows_of(senders.reshape(edges))
    recv_f, recv_l = rows_of(receivers.reshape(edges))
    near = (near_ids - first_node + HALO) % (nodes * patches)
    far_patch, far_row = far_ids // nodes, far_ids % nodes
    is_same = far_patch % 2 == core
    far_slot = jnp.where(is_same, 0, chips * COARSE) + far_patch // 2 * COARSE + far_row
    live = (jnp.arange(longs, dtype=I32) + lat * longs < long_count[0]).astype(I32)
    idx_rf = jnp.stack([near, recv_f - first_node])
    idx_rl = jnp.stack([far_slot, recv_l - first_node, live])
    idx_cf, idx_cl = idx_rf.T, idx_rl.T

    fine_other = block((fine, half), lambda i, s: (1 - s[0], 0))
    long_other = block((longs, half), lambda i, s: (FINE // longs + 1 - s[0], 0))
    quarter_rows = block((quarter, full), lambda i, s: (s[1], 0))
    sent_x, sent_g, sent_we, rim_low, rim_high = call(
        pack_kernel,
        info,
        (x_hbm, x_hbm, g_hbm, g_hbm, n_hbm, ng_hbm, wi_hbm, wo_hbm),
        [
            fine_other, long_other, fine_other, long_other, whole((nodes, half)), whole((nodes, half)),
            block((3, quarter, full), lambda i, s: (0, s[1], 0)), quarter_rows,
        ],
        [((rows + nodes, half), BF16), ((rows + nodes, half), BF16), ((4, quarter, full), BF16), ((HALO, half), BF16), ((HALO, half), BF16)],
        moved=3_000_000,
        name="pack",
    )
    we_got = other_neighbour(sent_we)
    x_got = pinned(swap_lat(sent_x))
    low, high = shifted(rim_high, 1), shifted(rim_low, -1)
    far_rows = chips * COARSE
    (sent_coarse,) = call(
        coarse_kernel,
        info,
        (n_hbm, swap_lat(node_latents[:16]), rim_low),
        [whole((16, half)), whole((16, half)), pl.BlockSpec(memory_space=pl.ANY)],
        [((chips, COARSE, full), BF16)],
        [pltpu.VMEM((chips, COARSE, full), BF16), pltpu.SemaphoreType.DMA],
        moved=600_000,
        name="coarse_rows",
        in_hbm=(0,),
    )
    same = chips_all_to_all(sent_coarse)
    rims_got = swap_lat(jnp.concatenate([low, high], 0))
    we_got = gated(info, we_got, (rims_got,))
    we_again = swap_core(we_got)

    got_spec = [whole((4, quarter, full))] * 2
    w_in, w_out, sent_wn = call(
        edge_weights_kernel,
        info,
        (wi_hbm, wo_hbm, pinned(we_got), pinned(we_again), ni_hbm, no_hbm, x_got, idx_cf, idx_cl),
        [whole((3, half, full)), whole((half, full))] + got_spec + [
            block((2, quarter, full), lambda i, s: (0, s[1], 0)), quarter_rows,
            pl.BlockSpec(memory_space=pl.ANY), whole((fine, 2)), whole((longs, 3)),
        ],
        [((3, full, full), BF16), ((full, full), BF16), ((3, quarter, full), BF16)],
        moved=7_000_000,
        name="edge_weights",
    )
    wn_got = other_neighbour(sent_wn)
    g_got = swap_lat(sent_g)
    def fine_own():
        return block((fine, half), lambda i, s: (s[0], 0))

    def long_own():
        return block((longs, half), lambda i, s: (FINE // longs + s[0], 0))

    def fine_got():
        return whole((fine, half))

    def long_got():
        return block((longs, half), lambda i, s: (fine // longs, 0))

    node_spec = whole((nodes, half))
    got_nodes = block((nodes, half), lambda i, s: (rows // nodes, 0))
    rim = whole((HALO, half))
    win_spec, wout_spec = whole((3, full, full)), whole((full, full))

    def forward_outs(count, reach):
        return [
            ((count, full), F32),
            ((count, full), BF16),
            ((count, full), F32),
            ((count, 1), F32),
            ((count, half), BF16),
            ((count, half), BF16),
            ((reach, full), F32),
            ((reach, full), BF16),
        ]

    slope_f, act_f, normed_f, inverse_f, fine_out, fine_sent, partial_f, partial_f_sent = call(
        fine_kernel,
        info,
        (x_hbm, x_got, n_hbm, x_got, low, high, rims_got, idx_cf, idx_rf, w_in, w_out),
        [
            fine_own(), fine_got(), node_spec, got_nodes, rim, rim, whole((2 * HALO, half)),
            whole((fine, 2)), whole((2, fine)), win_spec, wout_spec,
        ],
        forward_outs(fine, nodes),
        [pltpu.VMEM((extent, full), BF16), pltpu.VMEM((fine, full), BF16)],
        flops=2 * fine * full * (4 * full + extent + 2 * nodes),
        moved=8_000_000,
        name="edges_forward_fine",
    )
    other = swap_core(same).reshape(far_rows, full)
    same = same.reshape(far_rows, full)
    slope_l, act_l, normed_l, inverse_l, long_out, long_sent, partial_l, partial_l_sent, srow_l = call(
        long_kernel,
        info,
        (x_hbm, x_got, n_hbm, x_got, same, other, idx_cl, idx_rl, w_in, w_out, g_got),
        [
            long_own(), long_got(), whole((16, half)), block((16, half), lambda i, s: (rows // 16, 0)),
            whole((far_rows, full)), whole((far_rows, full)),
            whole((longs, 3)), whole((3, longs)), win_spec, wout_spec,
            pl.BlockSpec(memory_space=pl.ANY),
        ],
        forward_outs(longs, 16) + [((longs, full), BF16)],
        [pltpu.VMEM((longs, full), BF16)],
        flops=2 * longs * full * (4 * full + 4 * patches * COARSE + 2 * nodes),
        moved=6_000_000,
        name="edges_forward_long",
    )
    partial_f_got = swap_lat(partial_f_sent)
    wn_got = gated(info, wn_got, (partial_l_sent, partial_f_got))
    wn_again = swap_core(wn_got)
    nin, nout = call(
        weights_kernel,
        info,
        (ni_hbm, no_hbm, wn_got, wn_again),
        [whole((2, half, full)), whole((half, full)), whole((3, quarter, full)), whole((3, quarter, full))],
        [((2, full, full), BF16), ((full, full), BF16)],
        moved=3_000_000,
        name="node_weights",
    )
    partial_l_got = swap_lat(partial_l_sent)

    edge_out_got = swap_lat(jnp.concatenate([fine_sent, long_sent], 0))
    rows_pair, rows_own = 4 * half + far_rows, 7 * half + far_rows

    node_output, node_self, keep_pair, send_pair, keep_own, send_own, dpre, near_sum, recv_sum = call(
        back_kernel,
        info,
        (partial_f, partial_f_got, partial_l, partial_l_got, n_hbm, x_got, ng_hbm, g_got, low, high, rims_got, nin, nout,
         x_hbm, x_hbm, x_got, x_got, g_hbm, g_hbm, g_got, g_got,
         slope_f, slope_l, act_f, act_l, normed_f, normed_l, inverse_f, inverse_l, srow_l,
         idx_cf, idx_cl, idx_rf, idx_rl, w_in, w_out),
        [
            whole((nodes, full)), whole((nodes, full)), whole((16, full)), whole((16, full)),
            node_spec, got_nodes, node_spec, got_nodes,
            rim, rim, whole((2 * HALO, half)), whole((2, full, full)), wout_spec,
            fine_own(), long_own(), fine_got(), long_got(), fine_own(), long_own(), fine_got(), long_got(),
            whole((fine, full)), whole((longs, full)), whole((fine, full)), whole((longs, full)),
            whole((fine, full)), whole((longs, full)), whole((fine, 1)), whole((longs, 1)),
            whole((longs, full)),
            whole((fine, 2)), whole((longs, 3)), whole((2, fine)), whole((3, longs)), win_spec, wout_spec,
        ],
        [
            ((nodes, half), BF16),
            ((nodes, half), F32),
            ((rows_pair, half), BF16),
            ((rows_pair, half), BF16),
            ((rows_own, half), BF16),
            ((rows_own, half), BF16),
            ((rows, full), BF16),
            ((extent, full), BF16),
            ((nodes, full), BF16),
        ],
        [
            pltpu.VMEM((rows, full), BF16),
            pltpu.VMEM((nodes, full), BF16),
            pltpu.VMEM((nodes, full), BF16),
            pltpu.VMEM((nodes, full), BF16),
            pltpu.VMEM((nodes, half), BF16),
            pltpu.VMEM((nodes, full), BF16),
            pltpu.VMEM((extent, half), BF16),
            pltpu.VMEM((extent, half), BF16),
        ],
        flops=8 * rows * full * full,
        moved=14_000_000,
        name="nodes_and_edges_backward",
        limit=28,
    )
    core_pair, core_own = swap_core(send_pair), swap_core(send_own)
    by_lat, by_other = call(
        lat_stage_kernel,
        info,
        (keep_pair, core_pair),
        [whole((rows_pair, half)), whole((rows_pair, half))],
        [((rows_pair // 2, half), BF16), ((rows_pair // 2, half), BF16)],
        moved=2_400_000,
        name="lat_stage",
    )
    blocks = half // LANES
    total_rows = 7 * half * blocks
    share = total_rows // chips
    slot = share + blocks * COARSE
    (gathered,) = call(
        combine_kernel,
        info,
        (keep_own, core_own, swap_lat(by_lat), other_neighbour(by_other)),
        [whole((rows_own, half)), whole((rows_own, half)), whole((rows_pair // 2, half)), whole((rows_pair // 2, half))],
        [((chips, slot, LANES), BF16)],
        [pltpu.VMEM((chips, slot, LANES), BF16), pltpu.SemaphoreType.DMA],
        moved=4_300_000,
        name="combine",
        in_hbm=(0,),
    )
    arrived = chips_all_to_all(gathered)

    grads_own, grads_sent, rim_own, rim_sent = call(
        inputs_kernel,
        info,
        (pinned(dpre), g_hbm, g_hbm, g_got, pinned(near_sum), pinned(recv_sum), w_in),
        [
            whole((rows, full)), fine_own(), long_own(), whole((rows, half)),
            whole((extent, full)), whole((nodes, full)), win_spec,
        ],
        [((rows, half), BF16), ((rows, half), BF16), ((extent, half), F32), ((extent, half), BF16)],
        flops=4 * rows * full * full,
        moved=5_000_000,
        name="input_gradients",
    )

    (edge_output,) = call(
        rows_kernel,
        info,
        (fine_out, long_out, edge_out_got),
        [whole((fine, half)), whole((longs, half)), whole((rows, half))],
        [((edges, half), BF16)],
        [pltpu.SemaphoreType.DMA((4,))],
        moved=1_600_000,
        name="edge_output_rows",
        in_hbm=(0,),
    )
    (edge_grads,) = call(
        rows_kernel,
        info,
        (grads_own, grads_own, swap_lat(grads_sent)),
        [whole((fine, half)), block((longs, half), lambda i, s: (fine // longs, 0)), whole((rows, half))],
        [((edges, half), BF16)],
        [pltpu.SemaphoreType.DMA((4,))],
        moved=1_600_000,
        name="edge_gradient_rows",
        in_hbm=(0,),
    )
    summed = rim_own + swap_lat(rim_sent).astype(F32)
    to_low = shifted(summed[:HALO].astype(BF16), -1).astype(F32)
    to_high = shifted(summed[HALO + nodes :].astype(BF16), 1).astype(F32)

    weight_share, coarse_total = call(
        functools.partial(share_kernel, scale=1.0 / patches),
        info,
        (arrived, pinned(edge_output), to_low, to_high),
        [pl.BlockSpec(memory_space=pl.ANY), pl.BlockSpec(memory_space=pltpu.HBM)]
        + [pl.BlockSpec(memory_space=pl.ANY)] * 2,
        [((chips, share, LANES), BF16), ((blocks * COARSE, LANES), F32)],
        [
            pltpu.VMEM((chips, slot, LANES), BF16),
            pltpu.VMEM((chips, share, LANES), BF16),
            pltpu.SemaphoreType.DMA,
        ],
        in_hbm=(0,),
        moved=2_200_000,
        name="share",
    )
    coarse_share = jnp.concatenate(
        [coarse_total[i * COARSE : (i + 1) * COARSE] for i in range(blocks)], 1
    )
    own_grads = node_self + summed[HALO : HALO + nodes]
    own_grads = own_grads.at[nodes - HALO :].add(to_low)
    own_grads = own_grads.at[:HALO].add(to_high)
    own_grads = own_grads.at[:COARSE].add(coarse_share)
    node_grads = own_grads.astype(BF16)
    mine = gated(info, chips_all_to_all(weight_share), (pinned(edge_grads), pinned(node_grads)), pltpu.HBM)
    mine = mine.reshape(blocks, total_rows // blocks, LANES)
    other = swap_core(mine)
    square = (half, full)
    weights = pl.pallas_call(
        results_kernel,
        grid_spec=pltpu.PrefetchScalarGridSpec(
            num_scalar_prefetch=1,
            grid=(1,),
            in_specs=[whole(mine.shape)] * 2,
            out_specs=[pl.BlockSpec(memory_space=pl.ANY)] * 4,
            scratch_shapes=[pltpu.VMEM((7,) + square, F32), pltpu.SemaphoreType.DMA((7,))],
        ),
        out_shape=[jax.ShapeDtypeStruct(shape, F32) for shape in ((3,) + square, square, (2,) + square, square)],
        compiler_params=pltpu.CompilerParams(vmem_limit_bytes=14 * MIB),
        cost_estimate=pl.CostEstimate(flops=0, bytes_accessed=6_000_000, transcendentals=0),
        name="results",
    )(info, mine, other)
    return (edge_output, node_output, edge_grads, node_grads, *weights)


def solution(mesh):
    placed = (
        P("patch", "lat"),
        P("patch", "lat"),
        P("patch", None),
        P("patch", None),
        P("patch"),
        P(None, "lat", None),
        P("lat", None),
        P(None, "lat", None),
        P("lat", None),
        P("patch", "lat"),
        P("patch", "lat"),
    )
    return jax.shard_map(
        body,
        mesh=mesh,
        in_specs=placed,
        out_specs=(
            P("patch", "lat"),
            P("patch", "lat"),
            P("patch", "lat"),
            P("patch", "lat"),
            P(None, "lat", None),
            P("lat", None),
            P(None, "lat", None),
            P("lat", None),
        ),
        check_vma=False,
    )
```

```python
import functools

import jax
import jax.numpy as jnp
from jax import lax
from jax.experimental import pallas as pl
from jax.experimental.pallas import tpu as pltpu
from jax.sharding import PartitionSpec as P

HALO = 32
COARSE = 8
FINE = 1152
EPSILON = 1e-05
F32 = jnp.float32
BF16 = jnp.bfloat16
I32 = jnp.int32
LANES = 128
MIB = 1024 * 1024


def dot(left, right):
    return jnp.dot(left, right, preferred_element_type=F32)


def contract_rows(left, right):
    return lax.dot_general(left, right, (((0,), (0,)), ((), ())), preferred_element_type=F32)


def contract_cols(left, right):
    return lax.dot_general(left, right, (((1,), (1,)), ((), ())), preferred_element_type=F32)


def layer_norm(values):
    centered = values - jnp.mean(values, axis=1, keepdims=True)
    inverse = lax.rsqrt(jnp.mean(centered * centered, axis=1, keepdims=True) + EPSILON)
    return centered * inverse, inverse


def norm_backward(cotangent, normed, inverse):
    mean = jnp.mean(cotangent, axis=1, keepdims=True)
    crossed = jnp.mean(cotangent * normed, axis=1, keepdims=True)
    return (cotangent - mean - normed * crossed) * inverse


def swish_parts(values):
    sigmoid = jax.nn.sigmoid(values)
    return values * sigmoid, sigmoid * (1.0 + values * (1.0 - sigmoid))


def one_hot(index, width):
    return (index == lax.broadcasted_iota(I32, (index.shape[0], width), 1)).astype(F32).astype(BF16)


def one_hot_t(index, width):
    return (index == lax.broadcasted_iota(I32, (width, index.shape[1]), 0)).astype(F32).astype(BF16)


def swap_lat(value):
    return lax.ppermute(value, "lat", [(0, 1), (1, 0)])


def swap_core(value):
    count = lax.axis_size("patch")
    return lax.ppermute(value, "patch", [(i, i ^ 1) for i in range(count)])


def shifted(value, steps):
    count = lax.axis_size("patch")
    return lax.ppermute(value, "patch", [(i, (i + steps) % count) for i in range(count)])


def other_neighbour(value):
    count = lax.axis_size("patch")
    pairs = []
    for patch in range(count):
        for lat in range(2):
            pairs.append((patch * 2 + lat, (patch ^ 2) * 2 + (1 - lat)))
    return lax.ppermute(value, ("patch", "lat"), pairs)


def chips_all_to_all(value):
    count = lax.axis_size("patch")
    groups = [list(range(core, count, 2)) for core in range(2)]
    return lax.all_to_all(value, "patch", 0, 0, tiled=True, axis_index_groups=groups)


def whole(shape):
    return pl.BlockSpec(shape, lambda i, s: (0,) * len(shape), pipeline_mode=pl.Buffered(1))


def block(shape, index):
    return pl.BlockSpec(shape, index, pipeline_mode=pl.Buffered(1))


def call(kernel, info, operands, in_specs, outs, scratch=(), flops=0, moved=0, name=None, in_hbm=(), limit=14):
    return pl.pallas_call(
        kernel,
        grid_spec=pltpu.PrefetchScalarGridSpec(
            num_scalar_prefetch=1,
            grid=(1,),
            in_specs=in_specs,
            out_specs=[
                pl.BlockSpec(memory_space=pltpu.HBM) if i in in_hbm else whole(shape)
                for i, (shape, _) in enumerate(outs)
            ],
            scratch_shapes=list(scratch),
        ),
        out_shape=[jax.ShapeDtypeStruct(shape, dtype) for shape, dtype in outs],
        compiler_params=pltpu.CompilerParams(vmem_limit_bytes=limit * MIB),
        cost_estimate=pl.CostEstimate(flops=flops, bytes_accessed=moved, transcendentals=0),
        name=name,
    )(info, *operands)


def pinned(value):
    return pltpu.with_memory_space_constraint(value, pltpu.HBM)


def pack_kernel(info, xf, xl, gf, gl, n, ng, wi, wo, xs, gs, wes, low, high):
    fine = xf.shape[0]
    low[...] = n[:HALO]
    high[...] = n[n.shape[0] - HALO :]
    wes[:3] = wi[...]
    wes[3] = wo[...]
    xs[:fine] = xf[...]
    xs[fine : fine + xl.shape[0]] = xl[...]
    xs[fine + xl.shape[0] :] = n[...]
    gs[:fine] = gf[...]
    gs[fine : fine + gl.shape[0]] = gl[...]
    gs[fine + gl.shape[0] :] = ng[...]


def coarse_kernel(info, n_own, n_got, after, out, staged, sem):
    half = n_own.shape[1]
    for columns, n in ((slice(0, half), n_own), (slice(half, 2 * half), n_got)):
        staged[:, :, columns] = jnp.broadcast_to(n[:COARSE][None], (staged.shape[0], COARSE, half))
    copy = pltpu.make_async_copy(staged, out, sem)
    copy.start()
    copy.wait()


def gate_kernel(info, value, *rest):
    pass


def gated(info, value, after, space=pl.ANY):
    anywhere = pl.BlockSpec(memory_space=pl.ANY)
    return pl.pallas_call(
        gate_kernel,
        in_specs=[pl.BlockSpec(memory_space=pltpu.SMEM)] + [anywhere] + [pl.BlockSpec(memory_space=space)] * len(after),
        out_specs=anywhere,
        out_shape=jax.ShapeDtypeStruct(value.shape, value.dtype),
        input_output_aliases={1: 0},
        compiler_params=pltpu.CompilerParams(vmem_limit_bytes=MIB),
        name="gate",
    )(info, value, *after)


def lat_stage_kernel(info, keep, got, first, second):
    rows = first.shape[0]
    first[...] = (keep[:rows].astype(F32) + got[:rows].astype(F32)).astype(BF16)
    second[...] = (keep[rows:].astype(F32) + got[rows:].astype(F32)).astype(BF16)


def combine_kernel(info, keep, got, first, second, out, staged, sem):
    chips = out.shape[0]
    rows = first.shape[0]
    edge_rows_count, far_rows = 2 * rows - chips * COARSE, chips * COARSE
    half_chips = chips // 2
    total = keep[...].astype(F32) + got[...].astype(F32)
    pair = jnp.concatenate([first[...], second[...]], 0).astype(F32)
    weights = jnp.concatenate(
        [total[:edge_rows_count] + pair[:edge_rows_count], total[edge_rows_count:-far_rows]], 0
    )
    far = total[-far_rows:] + pair[edge_rows_count:]
    share = weights.shape[0] // half_chips
    parts = [weights[:, i * LANES : (i + 1) * LANES].reshape(half_chips, share, LANES) for i in range(2)]
    coarse = [far[:, i * LANES : (i + 1) * LANES].reshape(chips, COARSE, LANES) for i in range(2)]
    staged[...] = jnp.concatenate([jnp.concatenate(parts, 0)] + coarse, 1).astype(BF16)
    copy = pltpu.make_async_copy(staged, out, sem)
    copy.start()
    copy.wait()


def share_kernel(info, arrived, output, low, high, weights, coarse, taken, staged, sem, *, scale):
    share = staged.shape[1]
    copy = pltpu.make_async_copy(arrived, taken, sem)
    copy.start()
    copy.wait()
    total = jnp.sum(taken[...].astype(F32), 0)
    staged[...] = jnp.broadcast_to((total[:share] * scale).astype(BF16)[None], staged.shape)
    copy = pltpu.make_async_copy(staged, weights, sem)
    copy.start()
    coarse[...] = total[share:]
    copy.wait()


def rows_kernel(info, own_f, own_l, got, out, sems):
    lat = info[0]
    fine, longs = own_f.shape[0], own_l.shape[0]
    copies = []
    for side, f, l in (
        (lat, own_f, own_l),
        (1 - lat, got.at[pl.ds(0, fine)], got.at[pl.ds(fine, longs)]),
    ):
        copies.append((f, out.at[pl.ds(pl.multiple_of(side * fine, 64), fine)]))
        copies.append((l, out.at[pl.ds(pl.multiple_of(FINE + side * longs, 64), longs)]))
    made = [pltpu.make_async_copy(a, b, sems.at[k]) for k, (a, b) in enumerate(copies)]
    for copy in made:
        copy.start()
    for copy in made:
        copy.wait()


def results_kernel(info, mine, other, inner, outer, node_inner, node_outer, staged, sems):
    first = info[1] == 0
    blocks, half = mine.shape[0], staged.shape[1]
    targets = [inner.at[0], inner.at[1], inner.at[2], outer, node_inner.at[0], node_inner.at[1], node_outer]
    copies = []
    for k, target in enumerate(targets):
        rows = slice(k * half, (k + 1) * half)
        for i in range(blocks):
            a, b = mine[i, rows].astype(F32), other[i, rows].astype(F32)
            staged[k, :, i * LANES : (i + 1) * LANES] = jnp.where(first, a, b)
            staged[k, :, half + i * LANES : half + (i + 1) * LANES] = jnp.where(first, b, a)
        copies.append(pltpu.make_async_copy(staged.at[k], target, sems.at[k]))
        copies[-1].start()
    for copy in copies:
        copy.wait()


def edge_weights_kernel(info, wi, wo, got, again, ni, no, after, idx_f, idx_l, full_in, full_out, wns):
    wns[:2] = ni[...]
    wns[2] = no[...]
    weights_kernel(info, wi, wo, got, again, full_in, full_out)


def weights_kernel(info, wi, wo, got, again, full_in, full_out):
    lat, core = info[0], info[1]
    half = wo.shape[0]
    quarter = half // 2
    inner = wi.shape[0]
    first = core == 0
    for k in range(inner):
        full_in[k, :half] = wi[k]
        full_in[k, half : half + quarter] = jnp.where(first, got[k], again[k])
        full_in[k, half + quarter :] = jnp.where(first, again[k], got[k])
    own = wo[...]
    top = jnp.where(first, got[inner], again[inner])
    bottom = jnp.where(first, again[inner], got[inner])
    missing = jnp.concatenate([top, bottom], 0)
    low = lat == 0
    for rows, value in ((slice(0, half), jnp.where(low, own, missing)), (slice(half, 2 * half), jnp.where(low, missing, own))):
        full_out[rows, :half] = jnp.where(low, value[:, :half], value[:, half:])
        full_out[rows, half:] = jnp.where(low, value[:, half:], value[:, :half])


def edge_rows(x, sender, receiver, mask, w_in, w_out, rows, half, slope, act, normed, inverse, out_own, out_sent, update):
    pre = dot(x, w_in[0]) + dot(sender, w_in[1]) + dot(receiver, w_in[2])
    value, derivative = swish_parts(pre)
    value = value.astype(BF16)
    slope[rows] = derivative
    act[rows] = value
    scaled, scale = layer_norm(dot(value, w_out[...]))
    normed[rows] = scaled
    inverse[rows] = scale
    change = scaled if mask is None else scaled * mask
    out = (x.astype(F32) + change).astype(BF16)
    out_own[rows] = out[:, :half]
    out_sent[rows] = out[:, half:]
    update[rows] = change.astype(BF16)


def fine_kernel(info, x_own, x_got, n_own, n_got, low, high, rims_got, idx_c, idx_r, w_in, w_out,
                slope, act, normed, inverse, out_own, out_sent, partial, sent, ext, update):
    half = x_own.shape[1]
    nodes = n_own.shape[0]
    ext[:HALO, :half] = low[...]
    ext[:HALO, half:] = rims_got[:HALO]
    ext[HALO : HALO + nodes, :half] = n_own[...]
    ext[HALO : HALO + nodes, half:] = n_got[...]
    ext[HALO + nodes :, :half] = high[...]
    ext[HALO + nodes :, half:] = rims_got[HALO:]
    node_x = ext[HALO : HALO + nodes]
    chunk = 192
    for start in range(0, x_own.shape[0], chunk):
        rows = pl.ds(start, chunk)
        x = jnp.concatenate([x_own[rows], x_got[rows]], 1)
        sender = dot(one_hot(idx_c[rows, 0:1], ext.shape[0]), ext[...]).astype(BF16)
        receiver = dot(one_hot(idx_c[rows, 1:2], nodes), node_x).astype(BF16)
        edge_rows(x, sender, receiver, None, w_in, w_out, rows, half, slope, act, normed, inverse, out_own, out_sent, update)
    total = dot(one_hot_t(idx_r[1:2], nodes), update[...])
    partial[...] = total
    sent[...] = total.astype(BF16)


def long_kernel(info, x_own, x_got, n_own, n_got, same, other, idx_c, idx_r, w_in, w_out, after,
                slope, act, normed, inverse, out_own, out_sent, partial, sent, sender_rows, update):
    half = x_own.shape[1]
    rows = pl.ds(0, x_own.shape[0])
    count = same.shape[0]
    value = dot(one_hot(idx_c[:, 0:1], count), same[...])
    value = value + dot(one_hot(idx_c[:, 0:1] - count, count), other[...])
    sender_rows[...] = value.astype(BF16)
    x = jnp.concatenate([x_own[...], x_got[...]], 1)
    near = n_own.shape[0]
    node_x = jnp.concatenate([n_own[...], n_got[...]], 1)
    receiver = dot(one_hot(idx_c[:, 1:2], near), node_x).astype(BF16)
    edge_rows(x, sender_rows[...], receiver, idx_c[:, 2:3].astype(F32), w_in, w_out, rows, half, slope, act, normed, inverse, out_own, out_sent, update)
    total = dot(one_hot_t(idx_r[1:2], near), update[...])
    partial[...] = total
    sent[...] = total.astype(BF16)


def column_halves(info, half):
    lat, core = info[0], info[1]
    turn = (core + lat) % 2

    def at(which):
        return pl.ds(pl.multiple_of(which * half, half), half)

    return at(core), at(1 - core), at(turn), at(1 - turn), at(lat), at(1 - lat)


def edge_weight_grads(outs, xf, xl, node_x, extended, srow, cols, act_f, act_l, hidden, dpre, dy, near_sum, recv_sum, fine):
    half = xf.shape[1]
    head, tail = pl.ds(0, fine), pl.ds(fine, dpre.shape[0] - fine)
    for out, columns, columns_own in outs:
        grad = contract_rows(xf[...], dpre[head, columns]) + contract_rows(xl[...], dpre[tail, columns])
        out[:half] = grad.astype(BF16)
        grad = contract_rows(extended, near_sum[:, columns]) + contract_rows(srow[:, cols], dpre[tail, columns])
        out[half : 2 * half] = grad.astype(BF16)
        out[2 * half : 3 * half] = contract_rows(node_x, recv_sum[:, columns]).astype(BF16)
        grad = contract_rows(act_f[:, hidden], dy[head, columns_own]) + contract_rows(act_l[:, hidden], dy[tail, columns_own])
        out[3 * half : 4 * half] = grad.astype(BF16)


def far_sums(idx_r, dpre_long, weights, keep, send, count):
    grads = contract_cols(dpre_long, weights).astype(BF16)
    far = dot(one_hot_t(idx_r[0:1], 2 * count), grads).astype(BF16)
    keep[keep.shape[0] - count :] = far[:count]
    send[send.shape[0] - count :] = far[count:]


def back_kernel(info, partial, got, partial_l, got_l, n_own, n_got, ng_own, ng_got, low, high, rims_got, nin, nout,
                xf_own, xl_own, xf_got, xl_got, gf_own, gl_own, gf_got, gl_got,
                slope_f, slope_l, act_f, act_l, normed_f, normed_l, inverse_f, inverse_l, srow_l,
                idx_cf, idx_cl, idx_rf, idx_rl, w_in, w_out,
                node_out, node_self, keep_pair, send_pair, keep_own, send_own, dpre, near_sum, recv_sum,
                dy, ndpre, ndy, nact, agg_own, agg_grad, ext, ext_own):
    mine, theirs, mine_own, theirs_own, hidden_mine, hidden_theirs = column_halves(info, n_own.shape[1])
    half = n_own.shape[1]
    nodes = n_own.shape[0]
    fine, longs = xf_got.shape[0], xl_got.shape[0]
    far_count = keep_pair.shape[0] - 4 * half

    ext[:HALO] = rims_got[:HALO]
    ext[HALO : HALO + nodes] = n_got[...]
    ext[HALO + nodes :] = rims_got[HALO:]
    node_x = jnp.concatenate([n_own[...], n_got[...]], 1)
    received, received_l = got[...].astype(F32), got_l[...].astype(F32)
    total = partial[...] + jnp.concatenate([received[:, half:], received[:, :half]], 1)
    coarse = partial_l[...] + jnp.concatenate([received_l[:, half:], received_l[:, :half]], 1)
    near = coarse.shape[0]
    agg = jnp.concatenate([total[:near] + coarse, total[near:]], 0).astype(BF16)
    agg_own[...] = agg[:, :half]
    node_value, node_slope = swish_parts(dot(node_x, nin[0]) + dot(agg, nin[1]))
    nact[...] = node_value.astype(BF16)
    node_normed, node_inverse = layer_norm(dot(nact[...], nout[...]))
    node_out[...] = (n_own[...].astype(F32) + node_normed[:, :half]).astype(BF16)
    node_g = jnp.concatenate([ng_own[...], ng_got[...]], 1).astype(F32)
    ndy[...] = norm_backward(node_g, node_normed, node_inverse).astype(BF16)
    ndpre[...] = (contract_cols(ndy[...], nout[...]) * node_slope).astype(BF16)
    agg_grad[...] = contract_cols(ndpre[...], nin[1]).astype(BF16)
    node_self[...] = ng_own[...].astype(F32) + contract_cols(ndpre[...], nin[0, :half])

    chunk = 192
    for start in range(0, fine + longs, chunk):
        rows = pl.ds(start, chunk)
        if start < fine:
            part = pl.ds(start, chunk)
            idx_c = idx_cf
            g_own, g_got, normed, inverse, slope = gf_own, gf_got, normed_f, inverse_f, slope_f
        else:
            part = pl.ds(start - fine, chunk)
            idx_c = idx_cl
            g_own, g_got, normed, inverse, slope = gl_own, gl_got, normed_l, inverse_l, slope_l
        cotangent = jnp.concatenate([g_own[part], g_got[part]], 1).astype(F32)
        cotangent = cotangent + dot(one_hot(idx_c[part, 1:2], nodes), agg_grad[...])
        if start >= fine:
            cotangent = cotangent * idx_cl[part, 2:3].astype(F32)
        dy[rows] = norm_backward(cotangent, normed[part], inverse[part]).astype(BF16)
        dpre[rows] = (contract_cols(dy[rows], w_out[...]) * slope[part]).astype(BF16)

    tail = pl.ds(fine, longs)
    head = pl.ds(0, fine)
    near_sum[...] = dot(one_hot_t(idx_rf[0:1], ext.shape[0]), dpre[head]).astype(BF16)
    recv_sum[...] = (
        dot(one_hot_t(idx_rf[1:2], nodes), dpre[head]) + dot(one_hot_t(idx_rl[1:2], nodes), dpre[tail])
    ).astype(BF16)
    far_sums(idx_rl, dpre[tail], w_in[1, half:], keep_pair, send_pair, far_count)
    edge_weight_grads(
        ((send_pair, theirs, theirs_own), (keep_pair, mine, mine_own)),
        xf_got, xl_got, n_got[...], ext[...], srow_l, slice(half, 2 * half), act_f, act_l, hidden_theirs,
        dpre, dy, near_sum, recv_sum, fine,
    )
    ext_own[:HALO] = low[...]
    ext_own[HALO : HALO + nodes] = n_own[...]
    ext_own[HALO + nodes :] = high[...]
    for own, columns, columns_own in ((send_own, theirs, theirs_own), (keep_own, mine, mine_own)):
        own[4 * half : 5 * half] = contract_rows(n_own[...], ndpre[:, columns]).astype(BF16)
        own[5 * half : 6 * half] = contract_rows(agg_own[...], ndpre[:, columns]).astype(BF16)
        own[6 * half : 7 * half] = contract_rows(nact[:, hidden_mine], ndy[:, columns_own]).astype(BF16)
    far_sums(idx_rl, dpre[tail], w_in[1, :half], keep_own, send_own, far_count)
    edge_weight_grads(
        ((send_own, theirs, theirs_own), (keep_own, mine, mine_own)),
        xf_own, xl_own, n_own[...], ext_own[...], srow_l, slice(0, half), act_f, act_l, hidden_mine,
        dpre, dy, near_sum, recv_sum, fine,
    )


def inputs_kernel(info, dpre, gf_own, gl_own, g_got, near_sum, recv_sum, w_in,
                  grads_own, grads_sent, rim_own, rim_sent):
    half = g_got.shape[1]
    fine, longs = gf_own.shape[0], gl_own.shape[0]
    nodes = recv_sum.shape[0]
    for start, rows, own in ((0, fine, gf_own), (fine, longs, gl_own)):
        part = pl.ds(start, rows)
        change = contract_cols(dpre[part], w_in[0])
        grads_own[part] = (own[...].astype(F32) + change[:, :half]).astype(BF16)
        grads_sent[part] = (g_got[part].astype(F32) + change[:, half:]).astype(BF16)
    near = contract_cols(near_sum[...], w_in[1])
    received = contract_cols(recv_sum[...], w_in[2])
    for rows, value in (
        (slice(0, HALO), near[:HALO]),
        (slice(HALO, HALO + nodes), near[HALO : HALO + nodes] + received),
        (slice(HALO + nodes, 2 * HALO + nodes), near[HALO + nodes :]),
    ):
        rim_own[rows] = value[:, :half]
        rim_sent[rows] = value[:, half:].astype(BF16)


def body(
    node_latents,
    edge_latents,
    senders,
    receivers,
    long_count,
    edge_inner,
    edge_outer,
    node_inner,
    node_outer,
    node_cotangent,
    edge_cotangent,
):
    nodes, half = node_latents.shape
    full = 2 * half
    edges = edge_latents.shape[0]
    rows = edges // 2
    fine, longs = FINE // 2, (edges - FINE) // 2
    quarter = half // 2
    patches = lax.axis_size("patch")
    chips = patches // 2
    extent = nodes + 2 * HALO
    lat = lax.axis_index("lat")
    patch = lax.axis_index("patch")
    core = patch % 2
    first_node = patch * nodes
    info = jnp.stack([lat, core]).astype(I32)

    x_hbm, g_hbm = pinned(edge_latents), pinned(edge_cotangent)
    n_hbm, ng_hbm = pinned(node_latents), pinned(node_cotangent)
    wi_hbm, wo_hbm = pinned(edge_inner), pinned(edge_outer)
    ni_hbm, no_hbm = pinned(node_inner), pinned(node_outer)

    def rows_of(value):
        return (
            lax.dynamic_slice_in_dim(value, lat * fine, fine, 0),
            lax.dynamic_slice_in_dim(value, FINE + lat * longs, longs, 0),
        )

    near_ids, far_ids = rows_of(senders.reshape(edges))
    recv_f, recv_l = rows_of(receivers.reshape(edges))
    near = (near_ids - first_node + HALO) % (nodes * patches)
    far_patch, far_row = far_ids // nodes, far_ids % nodes
    is_same = far_patch % 2 == core
    far_slot = jnp.where(is_same, 0, chips * COARSE) + far_patch // 2 * COARSE + far_row
    live = (jnp.arange(longs, dtype=I32) + lat * longs < long_count[0]).astype(I32)
    idx_rf = jnp.stack([near, recv_f - first_node])
    idx_rl = jnp.stack([far_slot, recv_l - first_node, live])
    idx_cf, idx_cl = idx_rf.T, idx_rl.T

    fine_other = block((fine, half), lambda i, s: (1 - s[0], 0))
    long_other = block((longs, half), lambda i, s: (FINE // longs + 1 - s[0], 0))
    quarter_rows = block((quarter, full), lambda i, s: (s[1], 0))
    sent_x, sent_g, sent_we, rim_low, rim_high = call(
        pack_kernel,
        info,
        (x_hbm, x_hbm, g_hbm, g_hbm, n_hbm, ng_hbm, wi_hbm, wo_hbm),
        [
            fine_other, long_other, fine_other, long_other, whole((nodes, half)), whole((nodes, half)),
            block((3, quarter, full), lambda i, s: (0, s[1], 0)), quarter_rows,
        ],
        [((rows + nodes, half), BF16), ((rows + nodes, half), BF16), ((4, quarter, full), BF16), ((HALO, half), BF16), ((HALO, half), BF16)],
        moved=3_000_000,
        name="pack",
    )
    we_got = other_neighbour(sent_we)
    x_got = pinned(swap_lat(sent_x))
    low, high = shifted(rim_high, 1), shifted(rim_low, -1)
    far_rows = chips * COARSE
    (sent_coarse,) = call(
        coarse_kernel,
        info,
        (n_hbm, swap_lat(node_latents[:16]), rim_low),
        [whole((16, half)), whole((16, half)), pl.BlockSpec(memory_space=pl.ANY)],
        [((chips, COARSE, full), BF16)],
        [pltpu.VMEM((chips, COARSE, full), BF16), pltpu.SemaphoreType.DMA],
        moved=600_000,
        name="coarse_rows",
        in_hbm=(0,),
    )
    same = chips_all_to_all(sent_coarse)
    rims_got = swap_lat(gated(info, jnp.concatenate([low, high], 0), (x_got,)))
    we_got = gated(info, we_got, (rims_got,))
    we_again = swap_core(we_got)

    got_spec = [whole((4, quarter, full))] * 2
    w_in, w_out, sent_wn = call(
        edge_weights_kernel,
        info,
        (wi_hbm, wo_hbm, pinned(we_got), pinned(we_again), ni_hbm, no_hbm, x_got, idx_cf, idx_cl),
        [whole((3, half, full)), whole((half, full))] + got_spec + [
            block((2, quarter, full), lambda i, s: (0, s[1], 0)), quarter_rows,
            pl.BlockSpec(memory_space=pl.ANY), whole((fine, 2)), whole((longs, 3)),
        ],
        [((3, full, full), BF16), ((full, full), BF16), ((3, quarter, full), BF16)],
        moved=7_000_000,
        name="edge_weights",
    )
    wn_got = other_neighbour(sent_wn)
    g_got = swap_lat(sent_g)
    def fine_own():
        return block((fine, half), lambda i, s: (s[0], 0))

    def long_own():
        return block((longs, half), lambda i, s: (FINE // longs + s[0], 0))

    def fine_got():
        return whole((fine, half))

    def long_got():
        return block((longs, half), lambda i, s: (fine // longs, 0))

    node_spec = whole((nodes, half))
    got_nodes = block((nodes, half), lambda i, s: (rows // nodes, 0))
    rim = whole((HALO, half))
    win_spec, wout_spec = whole((3, full, full)), whole((full, full))

    def forward_outs(count, reach):
        return [
            ((count, full), F32),
            ((count, full), BF16),
            ((count, full), F32),
            ((count, 1), F32),
            ((count, half), BF16),
            ((count, half), BF16),
            ((reach, full), F32),
            ((reach, full), BF16),
        ]

    slope_f, act_f, normed_f, inverse_f, fine_out, fine_sent, partial_f, partial_f_sent = call(
        fine_kernel,
        info,
        (x_hbm, x_got, n_hbm, x_got, low, high, rims_got, idx_cf, idx_rf, w_in, w_out),
        [
            fine_own(), fine_got(), node_spec, got_nodes, rim, rim, whole((2 * HALO, half)),
            whole((fine, 2)), whole((2, fine)), win_spec, wout_spec,
        ],
        forward_outs(fine, nodes),
        [pltpu.VMEM((extent, full), BF16), pltpu.VMEM((fine, full), BF16)],
        flops=2 * fine * full * (4 * full + extent + 2 * nodes),
        moved=8_000_000,
        name="edges_forward_fine",
    )
    other = swap_core(same).reshape(far_rows, full)
    same = same.reshape(far_rows, full)
    slope_l, act_l, normed_l, inverse_l, long_out, long_sent, partial_l, partial_l_sent, srow_l = call(
        long_kernel,
        info,
        (x_hbm, x_got, n_hbm, x_got, same, other, idx_cl, idx_rl, w_in, w_out, g_got),
        [
            long_own(), long_got(), whole((16, half)), block((16, half), lambda i, s: (rows // 16, 0)),
            whole((far_rows, full)), whole((far_rows, full)),
            whole((longs, 3)), whole((3, longs)), win_spec, wout_spec,
            pl.BlockSpec(memory_space=pl.ANY),
        ],
        forward_outs(longs, 16) + [((longs, full), BF16)],
        [pltpu.VMEM((longs, full), BF16)],
        flops=2 * longs * full * (4 * full + 4 * patches * COARSE + 2 * nodes),
        moved=6_000_000,
        name="edges_forward_long",
    )
    partial_f_got = swap_lat(partial_f_sent)
    wn_got = gated(info, wn_got, (partial_l_sent, partial_f_got))
    wn_again = swap_core(wn_got)
    nin, nout = call(
        weights_kernel,
        info,
        (ni_hbm, no_hbm, wn_got, wn_again),
        [whole((2, half, full)), whole((half, full)), whole((3, quarter, full)), whole((3, quarter, full))],
        [((2, full, full), BF16), ((full, full), BF16)],
        moved=3_000_000,
        name="node_weights",
    )
    partial_l_got = swap_lat(partial_l_sent)

    edge_out_got = swap_lat(jnp.concatenate([fine_sent, long_sent], 0))
    rows_pair, rows_own = 4 * half + far_rows, 7 * half + far_rows

    node_output, node_self, keep_pair, send_pair, keep_own, send_own, dpre, near_sum, recv_sum = call(
        back_kernel,
        info,
        (partial_f, partial_f_got, partial_l, partial_l_got, n_hbm, x_got, ng_hbm, g_got, low, high, rims_got, nin, nout,
         x_hbm, x_hbm, x_got, x_got, g_hbm, g_hbm, g_got, g_got,
         slope_f, slope_l, act_f, act_l, normed_f, normed_l, inverse_f, inverse_l, srow_l,
         idx_cf, idx_cl, idx_rf, idx_rl, w_in, w_out),
        [
            whole((nodes, full)), whole((nodes, full)), whole((16, full)), whole((16, full)),
            node_spec, got_nodes, node_spec, got_nodes,
            rim, rim, whole((2 * HALO, half)), whole((2, full, full)), wout_spec,
            fine_own(), long_own(), fine_got(), long_got(), fine_own(), long_own(), fine_got(), long_got(),
            whole((fine, full)), whole((longs, full)), whole((fine, full)), whole((longs, full)),
            whole((fine, full)), whole((longs, full)), whole((fine, 1)), whole((longs, 1)),
            whole((longs, full)),
            whole((fine, 2)), whole((longs, 3)), whole((2, fine)), whole((3, longs)), win_spec, wout_spec,
        ],
        [
            ((nodes, half), BF16),
            ((nodes, half), F32),
            ((rows_pair, half), BF16),
            ((rows_pair, half), BF16),
            ((rows_own, half), BF16),
            ((rows_own, half), BF16),
            ((rows, full), BF16),
            ((extent, full), BF16),
            ((nodes, full), BF16),
        ],
        [
            pltpu.VMEM((rows, full), BF16),
            pltpu.VMEM((nodes, full), BF16),
            pltpu.VMEM((nodes, full), BF16),
            pltpu.VMEM((nodes, full), BF16),
            pltpu.VMEM((nodes, half), BF16),
            pltpu.VMEM((nodes, full), BF16),
            pltpu.VMEM((extent, half), BF16),
            pltpu.VMEM((extent, half), BF16),
        ],
        flops=8 * rows * full * full,
        moved=14_000_000,
        name="nodes_and_edges_backward",
        limit=28,
    )
    core_pair, core_own = swap_core(send_pair), swap_core(send_own)
    by_lat, by_other = call(
        lat_stage_kernel,
        info,
        (keep_pair, core_pair),
        [whole((rows_pair, half)), whole((rows_pair, half))],
        [((rows_pair // 2, half), BF16), ((rows_pair // 2, half), BF16)],
        moved=2_400_000,
        name="lat_stage",
    )
    blocks = half // LANES
    total_rows = 7 * half * blocks
    share = total_rows // chips
    slot = share + blocks * COARSE
    (gathered,) = call(
        combine_kernel,
        info,
        (keep_own, core_own, swap_lat(by_lat), other_neighbour(by_other)),
        [whole((rows_own, half)), whole((rows_own, half)), whole((rows_pair // 2, half)), whole((rows_pair // 2, half))],
        [((chips, slot, LANES), BF16)],
        [pltpu.VMEM((chips, slot, LANES), BF16), pltpu.SemaphoreType.DMA],
        moved=4_300_000,
        name="combine",
        in_hbm=(0,),
    )
    arrived = chips_all_to_all(gathered)

    grads_own, grads_sent, rim_own, rim_sent = call(
        inputs_kernel,
        info,
        (pinned(dpre), g_hbm, g_hbm, g_got, pinned(near_sum), pinned(recv_sum), w_in),
        [
            whole((rows, full)), fine_own(), long_own(), whole((rows, half)),
            whole((extent, full)), whole((nodes, full)), win_spec,
        ],
        [((rows, half), BF16), ((rows, half), BF16), ((extent, half), F32), ((extent, half), BF16)],
        flops=4 * rows * full * full,
        moved=5_000_000,
        name="input_gradients",
    )

    (edge_output,) = call(
        rows_kernel,
        info,
        (fine_out, long_out, edge_out_got),
        [whole((fine, half)), whole((longs, half)), whole((rows, half))],
        [((edges, half), BF16)],
        [pltpu.SemaphoreType.DMA((4,))],
        moved=1_600_000,
        name="edge_output_rows",
        in_hbm=(0,),
    )
    (edge_grads,) = call(
        rows_kernel,
        info,
        (grads_own, grads_own, swap_lat(grads_sent)),
        [whole((fine, half)), block((longs, half), lambda i, s: (fine // longs, 0)), whole((rows, half))],
        [((edges, half), BF16)],
        [pltpu.SemaphoreType.DMA((4,))],
        moved=1_600_000,
        name="edge_gradient_rows",
        in_hbm=(0,),
    )
    summed = rim_own + swap_lat(rim_sent).astype(F32)
    to_low = shifted(summed[:HALO].astype(BF16), -1).astype(F32)
    to_high = shifted(summed[HALO + nodes :].astype(BF16), 1).astype(F32)

    weight_share, coarse_total = call(
        functools.partial(share_kernel, scale=1.0 / patches),
        info,
        (arrived, pinned(edge_output), to_low, to_high),
        [pl.BlockSpec(memory_space=pl.ANY), pl.BlockSpec(memory_space=pltpu.HBM)]
        + [pl.BlockSpec(memory_space=pl.ANY)] * 2,
        [((chips, share, LANES), BF16), ((blocks * COARSE, LANES), F32)],
        [
            pltpu.VMEM((chips, slot, LANES), BF16),
            pltpu.VMEM((chips, share, LANES), BF16),
            pltpu.SemaphoreType.DMA,
        ],
        in_hbm=(0,),
        moved=2_200_000,
        name="share",
    )
    coarse_share = jnp.concatenate(
        [coarse_total[i * COARSE : (i + 1) * COARSE] for i in range(blocks)], 1
    )
    own_grads = node_self + summed[HALO : HALO + nodes]
    own_grads = own_grads.at[nodes - HALO :].add(to_low)
    own_grads = own_grads.at[:HALO].add(to_high)
    own_grads = own_grads.at[:COARSE].add(coarse_share)
    node_grads = own_grads.astype(BF16)
    mine = gated(info, chips_all_to_all(weight_share), (pinned(edge_grads), pinned(node_grads)), pltpu.HBM)
    mine = mine.reshape(blocks, total_rows // blocks, LANES)
    other = swap_core(mine)
    square = (half, full)
    weights = pl.pallas_call(
        results_kernel,
        grid_spec=pltpu.PrefetchScalarGridSpec(
            num_scalar_prefetch=1,
            grid=(1,),
            in_specs=[whole(mine.shape)] * 2,
            out_specs=[pl.BlockSpec(memory_space=pl.ANY)] * 4,
            scratch_shapes=[pltpu.VMEM((7,) + square, F32), pltpu.SemaphoreType.DMA((7,))],
        ),
        out_shape=[jax.ShapeDtypeStruct(shape, F32) for shape in ((3,) + square, square, (2,) + square, square)],
        compiler_params=pltpu.CompilerParams(vmem_limit_bytes=14 * MIB),
        cost_estimate=pl.CostEstimate(flops=0, bytes_accessed=6_000_000, transcendentals=0),
        name="results",
    )(info, mine, other)
    return (edge_output, node_output, edge_grads, node_grads, *weights)


def solution(mesh):
    placed = (
        P("patch", "lat"),
        P("patch", "lat"),
        P("patch", None),
        P("patch", None),
        P("patch"),
        P(None, "lat", None),
        P("lat", None),
        P(None, "lat", None),
        P("lat", None),
        P("patch", "lat"),
        P("patch", "lat"),
    )
    return jax.shard_map(
        body,
        mesh=mesh,
        in_specs=placed,
        out_specs=(
            P("patch", "lat"),
            P("patch", "lat"),
            P("patch", "lat"),
            P("patch", "lat"),
            P(None, "lat", None),
            P("lat", None),
            P(None, "lat", None),
            P("lat", None),
        ),
        check_vma=False,
    )
```
